32 devices in a mesh: ctx: 8 (over z, y), tp: 4 (over x, core).
Axes of the slice: x: 2, y: 2, z: 4, core: 2. Of those that a mesh axis runs over, the one named last changes fastest.
Arguments:
- inputs: bfloat16 [2, 4096, 1024], P(None, ('ctx', 'tp')), may hold values from -6 to 6
- cotangent: float32 [2, 4096, 1024], P(None, ('ctx', 'tp')), may hold values from -6 to 6
- lengths: int32 [2, 3], replicated, may hold values from 1 to 3968, as said below
- norm_gain: bfloat16 [2, 2, 1024], P(None, None, 'ctx'), may hold values from 0.5 to 1.5
- w_qkv: bfloat16 [2, 1024, 8, 512], P(None, 'ctx', 'tp'), may hold values from -0.1875 to 0.1875
- w_gate: bfloat16 [2, 1024, 8, 256], P(None, 'ctx', 'tp'), may hold values from -0.1875 to 0.1875
- w_rates: bfloat16 [2, 1024, 8, 2], P(None, 'ctx', 'tp'), may hold values from -0.1875 to 0.1875
- conv_weight: float32 [2, 4, 8, 512], P(None, None, 'tp'), may hold values from -2 to 2
- decay_log: float32 [2, 8], P(None, 'tp'), may hold values from -9 to -2
- decay_bias: float32 [2, 8], P(None, 'tp'), may hold values from -3 to 3
- out_gain: float32 [2, 256], replicated, may hold values from 0.5 to 1.5
- w_out: bfloat16 [2, 8, 256, 1024], P(None, 'tp', None, 'ctx'), may hold values from -0.125 to 0.125
- w_gu: bfloat16 [2, 2, 1024, 2816], P(None, None, 'ctx', 'tp'), may hold values from -0.1875 to 0.1875
- w_down: bfloat16 [2, 2816, 1024], P(None, 'tp', 'ctx'), may hold values from -0.109375 to 0.109375
Outputs:
- activations: float32 [2, 4096, 1024], P(None, ('ctx', 'tp'))
- input_grad: float32 [2, 4096, 1024], P(None, ('ctx', 'tp'))
- grad_norm_gain: float32 [2, 2, 1024], P(None, None, 'ctx')
- grad_w_qkv: float32 [2, 1024, 8, 512], P(None, 'ctx', 'tp')
- grad_w_gate: float32 [2, 1024, 8, 256], P(None, 'ctx', 'tp')
- grad_w_rates: float32 [2, 1024, 8, 2], P(None, 'ctx', 'tp')
- grad_conv: float32 [2, 4, 8, 512], P(None, None, 'tp')
- grad_decay_log: float32 [2, 8], P(None, 'tp')
- grad_decay_bias: float32 [2, 8], P(None, 'tp')
- grad_out_gain: float32 [2, 256], replicated
- grad_w_out: float32 [2, 8, 256, 1024], P(None, 'tp', None, 'ctx')
- grad_w_gu: float32 [2, 2, 1024, 2816], P(None, None, 'ctx', 'tp')
- grad_w_down: float32 [2, 2816, 1024], P(None, 'tp', 'ctx')
The draws below stay inside these ranges and needn't reach their ends.
Inputs may be any that keep to these rules, and one draw needn't show every extreme that they name: lengths[m] holds the real lengths of the 3 sequences packed in micro-batch m, in order; each takes its length rounded up to a multiple of 64 positions, these spans fill all 4096 positions of the micro-batch, and the positions past a sequence's length are padding.
All inputs are finite; a program needn't handle non-finite values.
Results may differ from the reference program's by a relative error of at most 0.035.
Values may be sent and summed in bfloat16 or wider, within the bound.
No kernel may reach another device: no remote copies, remote signals or barrier semaphores. Data moves between devices by JAX's collectives and lax.ppermute only.
A program may use at most 320 MiB of HBM per device.

```python
import jax
import jax.numpy as jnp
from jax import lax

D = 1024
H = 8
DK = 128
DV = 256
FF = 2816
CONV = 4
STRETCH = 64
LAYERS = 2
MICRO = 2
TOK_DEV = 512
QKV = 512
TOKENS = 4096


def draw_lengths(key, part):
    key = jax.random.fold_in(key, 7)
    per_piece = TOK_DEV // STRETCH
    total_blocks = TOKENS // STRETCH
    half_blocks = total_blocks // 2
    piece_count = TOKENS // TOK_DEV
    first_key, second_key, third_key, fourth_key = jax.random.split(key, 4)
    micro_ids = jnp.arange(MICRO, dtype=jnp.int32)
    head_blocks = jax.random.randint(first_key, (MICRO,), 1, half_blocks)
    tail_blocks = jax.random.randint(second_key, (MICRO,), 1, half_blocks)
    boundary_piece = jax.random.randint(fourth_key, (MICRO,), 1, piece_count)
    head_blocks = jnp.where(micro_ids == MICRO - 1, boundary_piece * per_piece, head_blocks)
    head_blocks = jnp.where(micro_ids == 0, 1, head_blocks)
    tail_blocks = jnp.where((micro_ids == 0) | (micro_ids == MICRO - 1), 1, tail_blocks)
    middle_blocks = total_blocks - head_blocks - tail_blocks
    blocks = jnp.stack([head_blocks, middle_blocks, tail_blocks], axis=1)
    padding = jax.random.randint(third_key, (MICRO, 3), 0, STRETCH)
    column_ids = jnp.arange(3, dtype=jnp.int32)
    padding = jnp.where((micro_ids[:, None] == 0) & (column_ids[None, :] == 1), 0, padding)
    padding = jnp.where((micro_ids[:, None] == MICRO - 1) & (column_ids[None, :] == 2), STRETCH - 1, padding)
    return (blocks * STRETCH - padding).astype(jnp.int32)


def shard_levels(own_key, extent, cuts, least, top_value):
    loudness = 1.0
    for axis_at, blocks in cuts:
        draws = jax.random.uniform(jax.random.fold_in(jax.random.fold_in(own_key, 6), axis_at), (blocks,), jnp.float32, least / len(cuts), top_value / len(cuts))
        loudness = loudness * jnp.repeat(jnp.exp(draws), extent[axis_at] // blocks).reshape((-1,) + (1,) * (len(extent) - 1 - axis_at))
    return loudness


def scatter_about(rng, extent, scale, bound, pieces=(), held_as=jnp.bfloat16):
    values = jax.random.normal(rng, extent, jnp.float32) * scale
    if len(pieces) > 0:
        values = shard_levels(rng, extent, pieces, -0.22, 0.18) * values
    return jnp.clip(values, min=-bound, max=bound).astype(held_as)


def setup_inputs(seed: int = 0) -> dict:
    key_of = jax.random.split(jax.random.key(seed), 15)
    inputs = scatter_about(key_of[0], (MICRO, TOKENS, D), 1.0, 6.0, ((1, 32),))
    cotangent = scatter_about(key_of[1], (MICRO, TOKENS, D), 1.0, 6.0, ((1, 32),), jnp.float32)
    lengths = draw_lengths(jax.random.fold_in(key_of[14], 71), 0)
    norm_gain = jnp.clip(1.0 + 0.1 * jax.random.normal(key_of[3], (LAYERS, 2, D), jnp.float32), 0.5, 1.5).astype(jnp.bfloat16)
    w_qkv = scatter_about(key_of[4], (LAYERS, D, H, QKV), D ** -0.5, 0.1875, ((1, 8), (2, 4)))
    w_gate = scatter_about(key_of[5], (LAYERS, D, H, DV), D ** -0.5, 0.1875, ((1, 8), (2, 4)))
    w_rates = scatter_about(key_of[6], (LAYERS, D, H, 2), D ** -0.5, 0.1875, ((1, 8), (2, 4)))
    conv_weight = scatter_about(key_of[7], (LAYERS, CONV, H, QKV), 0.5, 2.0, ((2, 4),), jnp.float32)
    decay_log = jnp.clip(-9.0 + 7.0 * jax.random.uniform(key_of[8], (LAYERS, H), jnp.float32) ** shard_levels(key_of[8], (LAYERS, H), ((1, 4),), -0.2, 0.2), -9.0, -2.0)
    decay_bias = scatter_about(key_of[9], (LAYERS, H), 1.0, 3.0, ((1, 4),), jnp.float32)
    out_gain = jnp.clip(1.0 + 0.1 * jax.random.normal(key_of[10], (LAYERS, DV), jnp.float32), 0.5, 1.5)
    w_out = scatter_about(key_of[11], (LAYERS, H, DV, D), (H * DV) ** -0.5, 0.125, ((1, 4), (3, 8)))
    w_gu = scatter_about(key_of[12], (LAYERS, 2, D, FF), D ** -0.5, 0.1875, ((2, 8), (3, 4)))
    w_down = scatter_about(key_of[13], (LAYERS, FF, D), FF ** -0.5, 0.109375, ((1, 4), (2, 8)))
    return {"inputs": inputs, "cotangent": cotangent, "lengths": lengths, "norm_gain": norm_gain, "w_qkv": w_qkv, "w_gate": w_gate, "w_rates": w_rates, "conv_weight": conv_weight, "decay_log": decay_log, "decay_bias": decay_bias, "out_gain": out_gain, "w_out": w_out, "w_gu": w_gu, "w_down": w_down}


epsilon = 1e-05
precise = lax.Precision.HIGHEST

@jax.custom_vjp
def low(v):
    return lax.optimization_barrier(v.astype(jnp.bfloat16)).astype(jnp.float32)

@jax.custom_vjp
def low_back(v):
    return v

def low_keep(v):
    return (low(v), None)

def low_pass(kept, grad):
    return (grad,)

def back_keep(v):
    return (v, None)

def back_low(kept, grad):
    return (low(grad),)
low.defvjp(low_keep, low_pass)
low_back.defvjp(back_keep, back_low)

def product(left, right):
    return jnp.dot(left, right, precision=precise, preferred_element_type=jnp.float32)

def rms_norm(values, gain_row):
    return values * lax.rsqrt(lax.optimization_barrier(jnp.mean(values * values, axis=-1, keepdims=True)) + epsilon) * gain_row

def unit_rows(values):
    return values * lax.rsqrt(lax.optimization_barrier(jnp.sum(values * values, axis=-1, keepdims=True)) + 1e-06)

def gated_norm(outputs, gate_rows, gain_row):
    return rms_norm(outputs, gain_row) * jax.nn.silu(gate_rows)

def token_layout(seq_lengths, positions):
    padded = (seq_lengths + STRETCH - 1) // STRETCH * STRETCH
    seq_ends = jnp.cumsum(padded).astype(jnp.int32)
    starts = (seq_ends - padded).astype(jnp.int32)
    inside = (positions[:, None] >= starts[None, :]) & (positions[:, None] < seq_ends[None, :])
    start_of = lax.optimization_barrier(jnp.sum(jnp.where(inside, starts[None, :], 0), axis=1)).astype(jnp.int32)
    length_of = lax.optimization_barrier(jnp.sum(jnp.where(inside, seq_lengths[None, :], 0), axis=1)).astype(jnp.int32)
    offset = (positions - start_of).astype(jnp.int32)
    return (offset, offset < length_of)

def short_conv(mixed_rows, weights, offset):
    row_count = mixed_rows.shape[0]
    padded = jnp.concatenate([jnp.zeros((CONV - 1, mixed_rows.shape[1]), jnp.float32), mixed_rows], axis=0)
    summed = jnp.zeros_like(mixed_rows)
    for tap_at in range(CONV):
        reach_back = CONV - 1 - tap_at
        summed = summed + jnp.where((offset >= reach_back)[:, None], padded[tap_at:tap_at + row_count], 0.0) * weights[tap_at]
    return summed

def prepare(conv_out, rates, decay_log_row, decay_bias_row):
    active = jax.nn.silu(conv_out)
    queries = unit_rows(active[..., :DK])
    keys_in = unit_rows(active[..., DK:2 * DK])
    values = active[..., 2 * DK:]
    betas = jax.nn.sigmoid(rates[..., 1])
    decays = -jnp.exp(decay_log_row) * jax.nn.softplus(rates[..., 0] + decay_bias_row)
    return (queries, keys_in, values, betas, decays)

def token_step(memory, inputs_now):
    query_now, key_now, value_now, beta_now, decay_now, keep_now = inputs_now
    memory = memory * keep_now
    retain = jnp.exp(decay_now)[:, None, None]
    recalled = jnp.einsum('hvk,hk->hv', memory, key_now, precision=precise)
    update = beta_now[:, None] * (value_now - retain[:, :, 0] * recalled)
    memory = retain * memory + update[:, :, None] * key_now[:, None, :]
    return (memory, jnp.einsum('hvk,hk->hv', memory, query_now, precision=precise))

def block_scan(memory, block):
    return lax.scan(token_step, memory, block)

def delta_rule(queries, keys_in, values, betas, decays, keep):
    row_count = queries.shape[0]
    blocks = tuple((source.reshape((row_count // STRETCH, STRETCH) + source.shape[1:]) for source in (queries, keys_in, values, betas, decays, keep)))
    memory = jnp.zeros((H, DV, DK), jnp.float32)
    memory, outputs = lax.scan(jax.checkpoint(block_scan), memory, blocks)
    return outputs.reshape(row_count, H, DV)

def layer(hidden_in, offset, valid, keep, gain_pair, w_qkv, w_gate, w_rates, conv_weight, decay_log, decay_bias, out_gain, w_out, w_gu, w_down):
    row_count = hidden_in.shape[0]
    normed = low(rms_norm(hidden_in, gain_pair[0]))
    mixed_rows = low_back(product(normed, w_qkv.reshape(D, H * QKV)))
    gate_pre = low_back(product(normed, w_gate.reshape(D, H * DV)))
    rate_pre = low_back(product(normed, w_rates.reshape(D, H * 2)))
    conv_out = short_conv(mixed_rows, conv_weight.reshape(CONV, H * QKV), offset)
    queries, keys_in, values, betas, decays = prepare(conv_out.reshape(row_count, H, QKV), rate_pre.reshape(row_count, H, 2), decay_log, decay_bias)
    outputs = delta_rule(queries, keys_in, values, betas, decays, keep)
    gated_out = low(gated_norm(outputs, gate_pre.reshape(row_count, H, DV), out_gain).reshape(row_count, H * DV))
    mixer_out = low_back(product(gated_out, w_out.reshape(H * DV, D)))
    middle = hidden_in + valid[:, None] * mixer_out
    normed_two = low(rms_norm(middle, gain_pair[1]))
    gate_ff = low_back(product(normed_two, w_gu[0]))
    up_ff = low_back(product(normed_two, w_gu[1]))
    hidden_ff = low(jax.nn.silu(gate_ff) * up_ff)
    ff_out = low_back(product(hidden_ff, w_down))
    return middle + valid[:, None] * ff_out

def reference(inputs, cotangent, lengths, norm_gain, w_qkv, w_gate, w_rates, conv_weight, decay_log, decay_bias, out_gain, w_out, w_gu, w_down):
    positions = jnp.arange(TOKENS, dtype=jnp.int32)
    weight_set = tuple((source.astype(jnp.float32) for source in (norm_gain, w_qkv, w_gate, w_rates, conv_weight, decay_log, decay_bias, out_gain, w_out, w_gu, w_down)))

    def forward(activations, *weight_all):
        results = []
        for micro_at in range(MICRO):
            offset, valid = token_layout(lengths[micro_at], positions)
            keep = (offset > 0).astype(jnp.float32)
            hidden_now = activations[micro_at]
            for layer_at in range(LAYERS):
                hidden_now = layer(hidden_now, offset, valid.astype(jnp.float32), keep, *[member[layer_at] for member in weight_all])
            results.append(hidden_now)
        return jnp.stack(results)
    outputs, pull = jax.vjp(forward, inputs.astype(jnp.float32), *weight_set)
    grads = pull(cotangent.astype(jnp.float32))
    return (outputs, grads[0], grads[1], grads[2], grads[3], grads[4], grads[5], grads[6], grads[7], grads[8], grads[9], grads[10], grads[11])
```

```python
from functools import partial

import jax
import jax.numpy as jnp
from jax import lax
from jax.experimental import pallas as pl
from jax.experimental.pallas import tpu as pltpu
from jax.sharding import PartitionSpec as P

D = 1024
DK = 128
DV = 256
QKV = 512
AUG = DV + DK
CONV = 4
STRETCH = 64
PACK = 256
PER_PACK = PACK // STRETCH
LANES = 128
HALO = 8

epsilon = 1e-05
unit_eps = 1e-06
f32 = jnp.float32
bf16 = jnp.bfloat16
VMEM_BYTES = 56 * 1024 * 1024


def swap(value, axis, bit):
    count = lax.axis_size(axis)
    return lax.ppermute(value, axis, [(i, i ^ bit) for i in range(count)])


def bits_of(axis):
    count = lax.axis_size(axis)
    bits = []
    bit = count // 2
    while bit >= 1:
        bits.append(bit)
        bit //= 2
    return bits


def turned(place, axis):
    offset = 0
    for step, bit in enumerate(bits_of(axis)):
        if place >> step & 1:
            offset |= bit
    return offset


def gather_blocks(value, axis):
    blocks = value[None]
    for bit in bits_of(axis):
        blocks = jnp.concatenate([blocks, swap(blocks, axis, bit)], axis=0)
    return blocks


def in_order(blocks, axis):
    count = lax.axis_size(axis)
    me = lax.axis_index(axis)
    place_of = [turned(offset, axis) for offset in range(count)]
    place_of = jnp.asarray(place_of, jnp.int32)
    return jnp.stack(
        [
            lax.dynamic_index_in_dim(blocks, place_of[me ^ device], 0, False)
            for device in range(count)
        ]
    )


def to_relative(blocks, axis):
    me = lax.axis_index(axis)
    return jnp.stack(
        [
            lax.dynamic_index_in_dim(blocks, me ^ turned(place, axis), 0, False)
            for place in range(blocks.shape[0])
        ]
    )


def gather_rows(rows):
    return gather_blocks(rows, "tp")


def scatter_rows(product_of, count):
    half = count // 2
    kept = None
    for bit in reversed(bits_of("tp")):
        if kept is None:
            sent = product_of(half, count).astype(bf16)
            received = swap(sent, "tp", bit)
            kept = product_of(0, half) + received.astype(f32)
        else:
            received = swap(kept[half:].astype(bf16), "tp", bit)
            kept = kept[:half] + received.astype(f32)
        half //= 2
    return kept[0]


def sum_over(value, axis):
    for bit in bits_of(axis):
        value = value + swap(value, axis, bit)
    return value


def passed_along(value, axis, steps):
    count = lax.axis_size(axis)
    initial, last = (max(0, -steps), min(count, count - steps))
    return lax.ppermute(value, axis, [(source, source + steps) for source in range(initial, last)])


def dot(left, right, contract):
    return lax.dot_general(
        left.astype(bf16),
        right.astype(bf16),
        (contract, ((), ())),
        preferred_element_type=f32,
    )


def nn(left, right):
    return dot(left, right, ((1,), (0,)))


def nt(left, right):
    return dot(left, right, ((1,), (1,)))


def tn(left, right):
    return dot(left, right, ((0,), (0,)))


def halves(value):
    high = value.astype(bf16)
    return high, (value - high.astype(f32)).astype(bf16)


def nn_fine(left, right):
    left_hi, left_lo = left
    right_hi, right_lo = right
    return nn(left_hi, right_hi) + (nn(left_hi, right_lo) + nn(left_lo, right_hi))


def sigmoid(value):
    return 1.0 / (1.0 + jnp.exp(-value))


def index_grids():
    row_at = lax.broadcasted_iota(jnp.int32, (PACK, PACK), 0)
    col_at = lax.broadcasted_iota(jnp.int32, (PACK, PACK), 1)
    return row_at, col_at


def unit_lower_inverse(lower, row_at, col_at):
    eye = (row_at == col_at).astype(f32)
    small = jnp.where(row_at // 8 == col_at // 8, lower, 0.0)
    small_h = halves(small)
    power2 = nn_fine(small_h, small_h)
    power2_h = halves(power2)
    inverse = eye - small
    inverse = inverse + nn_fine(halves(inverse), power2_h)
    power4 = nn_fine(power2_h, power2_h)
    inverse = inverse + nn_fine(halves(inverse), halves(power4))
    size = 8
    while size < STRETCH:
        corner = jnp.where(
            (row_at // (2 * size) == col_at // (2 * size)) & (row_at // size != col_at // size),
            lower,
            0.0,
        )
        inverse_h = halves(inverse)
        inverse = inverse - nn_fine(inverse_h, halves(nn_fine(halves(corner), inverse_h)))
        size *= 2
    return inverse


def load_pieces(order_ref, x_ref, halo_ref, xs, head):
    tp, _, rows, _ = x_ref.shape
    lanes = pl.ds(head * QKV, QKV)
    xs[0:HALO, :] = halo_ref[0, :, lanes]
    for place in range(tp):
        at = pl.multiple_of(order_ref[1 + place] * rows + HALO, 8)
        xs[pl.ds(at, rows), :] = x_ref[place, 0, :, lanes]


def conv_of(xs, weights, cols, first, count):
    total = None
    for reach in range(CONV):
        rows = xs[HALO + first - reach : HALO + first - reach + count, :]
        if reach > 0:
            rows = rows * cols[first : first + count, 4 + reach : 5 + reach]
        term = rows * weights[CONV - 1 - reach : CONV - reach, :]
        total = term if total is None else total + term
    return total


def front(conv_out):
    gate = sigmoid(conv_out)
    active = conv_out * gate
    raw_q, raw_k, values = active[:, :DK], active[:, DK : 2 * DK], active[:, 2 * DK :]
    scale_q = lax.rsqrt(jnp.sum(raw_q * raw_q, axis=1, keepdims=True) + unit_eps)
    scale_k = lax.rsqrt(jnp.sum(raw_k * raw_k, axis=1, keepdims=True) + unit_eps)
    return gate, raw_q * scale_q, raw_k * scale_k, values, scale_q, scale_k


def pack_terms(queries, keys, cols, cum_row, row_at, col_at):
    inside = (row_at // STRETCH == col_at // STRETCH) & (row_at >= col_at)
    spread = cols[:, 0:1] - cum_row
    weight = jnp.where(inside, jnp.exp(jnp.where(inside, spread, 0.0)), 0.0)
    keys_low = keys.astype(bf16)
    key_dots = nt(keys_low, keys_low)
    scores = nt(queries, keys_low) * weight
    pair = jnp.where(row_at > col_at, key_dots * weight, 0.0)
    return weight, pair, scores


def local_kernel(
    order_ref,
    x_ref,
    halo_ref,
    conv_ref,
    cols_ref,
    rows_ref,
    steps_ref,
    out_ref,
    reach_ref,
    starts_ref,
    inverse_ref,
    transit_ref,
    map_ref,
    xs,
    o_scr,
    r_scr,
):
    tp, _, rows, _ = x_ref.shape
    heads = conv_ref.shape[0]
    piece = tp * rows
    packs = piece // PACK
    blocks = piece // STRETCH
    row_at, col_at = index_grids()
    units = [(head, pack) for head in range(heads) for pack in range(packs)]
    held = {}
    for head in range(heads):
        load_pieces(order_ref, x_ref, halo_ref, xs.at[head], head)
    for head, pack in units:
        first = pack * PACK
        cols_all = cols_ref.at[0, head]
        conv_out = conv_of(xs.at[head], conv_ref.at[head], cols_all, first, PACK)
        _, queries, keys, values, _, _ = front(conv_out)
        cols = cols_all[first : first + PACK, :]
        weight, pair, scores = pack_terms(
            queries, keys, cols, rows_ref[0, head, 0:1, first : first + PACK], row_at, col_at
        )
        lower = pair * cols[:, 1:2]
        held[head, pack] = (queries, keys, values, cols, lower, scores)
    inverses = {
        unit: unit_lower_inverse(held[unit][4], row_at, col_at).astype(bf16) for unit in units
    }
    solved = {}
    moves = {}
    for unit in units:
        head, pack = unit
        queries, keys, values, cols, _, scores = held[unit]
        inverse_ref[0, head, pack] = inverses[unit]
        solved_w = nn(inverses[unit], keys * cols[:, 4:5])
        solved_u = nn(inverses[unit], values * cols[:, 1:2])
        tails = (keys * cols[:, 3:4]).astype(bf16)
        solved_w = solved_w.astype(bf16)
        solved_u_low = solved_u.astype(bf16)
        for sub in range(PER_PACK):
            part = slice(sub * STRETCH, (sub + 1) * STRETCH)
            block = pack * PER_PACK + sub
            transit = tn(tails[part], solved_w[part]).astype(bf16)
            transit_ref[0, head, block] = transit
            moves[head, block] = (transit, tn(tails[part], solved_u_low[part]))
        solved[unit] = (solved_w, solved_u)
    eye = (row_at[:DK, :DK] == col_at[:DK, :DK]).astype(f32)
    biases = [jnp.zeros((DK, DV), f32) for _ in range(heads)]
    maps = [eye for _ in range(heads)]
    for block in range(blocks):
        for head in range(heads):
            retain = steps_ref[0, head, block : block + 1, :]
            keep = steps_ref[0, head, blocks + block : blocks + block + 1, :]
            bias = biases[head] * jnp.concatenate([keep, keep], axis=1)
            whole = maps[head] * keep
            low = jnp.concatenate([bias, whole], axis=1).astype(bf16)
            starts_ref[0, head, block] = low
            transit, fresh = moves[head, block]
            moved = nn(transit, low)
            biases[head] = (
                bias * jnp.concatenate([retain, retain], axis=1) - moved[:, :DV] + fresh
            )
            maps[head] = whole * retain - moved[:, DV:]
    for head in range(heads):
        map_ref[0, head, :, :DV] = biases[head].astype(bf16)
        map_ref[0, head, :, DV:] = maps[head].astype(bf16)
    for unit in units:
        head, pack = unit
        queries, keys, values, cols, _, scores = held[unit]
        solved_w, solved_u = solved[unit]
        reading = (queries * cols[:, 2:3]).astype(bf16)
        carried, recalled = [], []
        for sub in range(PER_PACK):
            part = slice(sub * STRETCH, (sub + 1) * STRETCH)
            start = starts_ref[0, head, pack * PER_PACK + sub]
            both = nn(jnp.concatenate([reading[part], solved_w[part]], axis=0), start)
            carried.append(both[:STRETCH])
            recalled.append(both[STRETCH:])
        carried = jnp.concatenate(carried, axis=0)
        recalled = jnp.concatenate(recalled, axis=0)
        low_scores = scores.astype(bf16)
        first = pack * PACK
        o_scr[head, first : first + PACK, :] = carried[:, :DV] + nn(
            low_scores, solved_u - recalled[:, :DV]
        )
        r_scr[head, first : first + PACK, :] = carried[:, DV:] - nn(low_scores, recalled[:, DV:])
    for place in range(tp):
        at = pl.multiple_of(order_ref[1 + place] * rows, 8)
        for head in range(heads):
            out_ref[place, 0, :, head * DV : (head + 1) * DV] = o_scr[head, pl.ds(at, rows), :]
            reach_ref[place, 0, :, head * DK : (head + 1) * DK] = r_scr[
                head, pl.ds(at, rows), :
            ].astype(bf16)


def finish_kernel(order_ref, maps_ref, out_ref, reach_ref, gate_ref, gain_ref, gated_ref, entry_ref):
    tp = out_ref.shape[0]

    def one(step, entry):
        whole = maps_ref[step, 0, 0]
        return whole[:, :DV].astype(f32) + nn(whole[:, DV:], entry)

    entry = lax.fori_loop(0, order_ref[0], one, jnp.zeros((DK, DV), f32))
    entry_ref[0, 0] = entry
    entry_low = entry.astype(bf16)
    for place in range(tp):
        outputs = out_ref[place, 0] + nn(reach_ref[place, 0], entry_low)
        scale = lax.rsqrt(jnp.mean(outputs * outputs, axis=1, keepdims=True) + epsilon)
        gate = gate_ref[place, 0]
        gated = outputs * scale * gain_ref[0:1, :] * (gate * sigmoid(gate))
        gated_ref[place, 0] = gated.astype(bf16)


def unfinish_kernel(
    entry_ref, out_ref, reach_ref, gate_ref, gain_ref, grad_ref, ograd_ref, zgrad_ref, ggrad_ref, base_ref
):
    tp = out_ref.shape[0]
    entry_low = entry_ref[0, 0].astype(bf16)
    gain = gain_ref[0:1, :]
    base = jnp.zeros((DK, DV), f32)
    gain_grad = jnp.zeros((1, DV), f32)
    for place in range(tp):
        reach = reach_ref[place, 0]
        outputs = out_ref[place, 0] + nn(reach, entry_low)
        scale = lax.rsqrt(jnp.mean(outputs * outputs, axis=1, keepdims=True) + epsilon)
        unit = outputs * scale
        gate = gate_ref[place, 0]
        open_at = sigmoid(gate)
        grad = grad_ref[place, 0]
        normed_grad = grad * (gate * open_at)
        gate_grad = grad * (unit * gain) * (open_at * (1.0 + gate * (1.0 - open_at)))
        zgrad_ref[place, 0] = gate_grad.astype(bf16)
        gain_grad = gain_grad + jnp.sum(normed_grad * unit, axis=0, keepdims=True)
        inner = normed_grad * gain
        out_grad = scale * (inner - unit * jnp.mean(inner * unit, axis=1, keepdims=True))
        out_grad = out_grad.astype(bf16)
        ograd_ref[place, 0] = out_grad
        base = base + tn(reach, out_grad)
    ggrad_ref[0, 0] = jnp.broadcast_to(gain_grad, (8, DV))
    base_ref[0, 0] = base.astype(bf16)


def adjoint_kernel(
    order_ref,
    x_ref,
    halo_ref,
    conv_ref,
    cols_ref,
    rows_ref,
    steps_ref,
    starts_ref,
    inverse_ref,
    transit_ref,
    entry_ref,
    maps_ref,
    bases_ref,
    ograd_ref,
    xgrad_ref,
    hgrad_ref,
    cgrad_ref,
    dcols_ref,
    drows_ref,
    dlast_ref,
    xs,
    gs,
    ds,
):
    tp, _, rows, _ = x_ref.shape
    piece = tp * rows
    packs = piece // PACK
    blocks = piece // STRETCH
    ctx = maps_ref.shape[0]
    row_at, col_at = index_grids()
    load_pieces(order_ref, x_ref, halo_ref, xs, 0)
    for place in range(tp):
        at = pl.multiple_of(order_ref[1 + place] * rows, 16)
        gs[pl.ds(at, rows), :] = ograd_ref[place, 0]

    def one(step, grad):
        source = ctx - 1 - step
        return bases_ref[source, 0, 0].astype(f32) + tn(maps_ref[source, 0, 0], grad)

    after = lax.fori_loop(0, ctx - 1 - order_ref[0], one, jnp.zeros((DK, DV), f32))
    entry_low = entry_ref[0, 0].astype(bf16)
    held = {}
    starts = {}
    turns = {}
    for pack in range(packs):
        first = pack * PACK
        cols_all = cols_ref.at[0, 0]
        conv_out = conv_of(xs, conv_ref.at[0], cols_all, first, PACK)
        _, queries, keys, values, _, _ = front(conv_out)
        cols = cols_all[first : first + PACK, :]
        weight, pair, scores = pack_terms(
            queries, keys, cols, rows_ref[0, 0, 0:1, first : first + PACK], row_at, col_at
        )
        inverse = inverse_ref[0, 0, pack]
        solved_w = nn(inverse, keys * cols[:, 4:5]).astype(bf16)
        solved_u = nn(inverse, values * cols[:, 1:2])
        out_grad = gs[first : first + PACK, :]
        through = tn(scores, out_grad)
        through_low = through.astype(bf16)
        reading = (queries * cols[:, 2:3]).astype(bf16)
        fresh = []
        for sub in range(PER_PACK):
            part = slice(sub * STRETCH, (sub + 1) * STRETCH)
            block = pack * PER_PACK + sub
            start = starts_ref[0, 0, block]
            start = start[:, :DV].astype(f32) + nn(start[:, DV:], entry_low)
            starts[block] = start
            fresh.append(solved_u[part] - nn(solved_w[part], start))
            turns[block] = tn(reading[part], out_grad[part]) - tn(solved_w[part], through_low[part])
        held[pack] = (
            queries,
            keys,
            values,
            cols,
            weight,
            pair,
            scores,
            inverse,
            solved_w,
            solved_u,
            out_grad,
            through,
            jnp.concatenate(fresh, axis=0),
        )
    grads = {}
    grad = after
    for block in reversed(range(blocks)):
        grads[block] = grad
        retain = steps_ref[0, 0, block : block + 1, :]
        keep = steps_ref[0, 0, blocks + block : blocks + block + 1, :]
        grad = grad * jnp.concatenate([retain, retain], axis=1)
        grad = grad - tn(transit_ref[0, 0, block], grads[block]) + turns[block]
        grad = grad * jnp.concatenate([keep, keep], axis=1)
    ds[0:HALO, :] = jnp.zeros((HALO, QKV), f32)
    ds[HALO + piece : 2 * HALO + piece, :] = jnp.zeros((HALO, QKV), f32)
    for pack in range(packs):
        first = pack * PACK
        (
            queries,
            keys,
            values,
            cols,
            weight,
            pair,
            scores,
            inverse,
            solved_w,
            solved_u,
            out_grad,
            through,
            fresh,
        ) = held[pack]
        beta, grown, tail, beta_grown = cols[:, 1:2], cols[:, 2:3], cols[:, 3:4], cols[:, 4:5]
        tails = keys * tail
        tails_low = tails.astype(bf16)
        fresh_low = fresh.astype(bf16)
        fresh_grad, read_grad, solved_w_grad, tails_grad, last_grad = [], [], [], [], []
        for sub in range(PER_PACK):
            part = slice(sub * STRETCH, (sub + 1) * STRETCH)
            block = pack * PER_PACK + sub
            grad_now = grads[block]
            grad_low = grad_now.astype(bf16)
            now = through[part] + nn(tails_low[part], grad_low)
            fresh_grad.append(now)
            both = nt(jnp.concatenate([out_grad[part], now.astype(bf16)], axis=0), starts[block])
            read_grad.append(both[:STRETCH])
            solved_w_grad.append(-both[STRETCH:])
            tails_grad.append(nt(fresh_low[part], grad_low))
            retain = steps_ref[0, 0, block : block + 1, :]
            meet = starts[block] * grad_now
            last_grad.append(
                retain * jnp.sum(meet[:, :DK] + meet[:, DK:], axis=0, keepdims=True)
            )
        fresh_grad = jnp.concatenate(fresh_grad, axis=0)
        read_grad = jnp.concatenate(read_grad, axis=0)
        solved_w_grad = jnp.concatenate(solved_w_grad, axis=0)
        tails_grad = jnp.concatenate(tails_grad, axis=0)
        score_grad = nt(out_grad, fresh_low)
        dots_grad = (score_grad * weight).astype(bf16)
        right_grad = tn(inverse, jnp.concatenate([fresh_grad, solved_w_grad], axis=1))
        right_u, right_w = right_grad[:, :DV], right_grad[:, DV:]
        lower_grad = -(nt(right_u, solved_u) + nt(right_w, solved_w))
        lower_grad = jnp.where(row_at > col_at, lower_grad, 0.0)
        pair_grad = lower_grad * pair
        key_dots_grad = (lower_grad * weight * beta).astype(bf16)
        spread_grad = pair_grad * beta + score_grad * scores
        keys_low = keys.astype(bf16)
        queries_low = queries.astype(bf16)
        keys_right = jnp.sum(keys * right_w, axis=1, keepdims=True)
        tails_meet = tails * tails_grad
        keys_grad = (
            beta_grown * right_w
            + nn(key_dots_grad, keys_low)
            + tn(key_dots_grad, keys_low)
            + tn(dots_grad, queries_low)
            + tail * tails_grad
        )
        queries_grad = grown * read_grad + nn(dots_grad, keys_low)
        values_grad = beta * right_u
        beta_grad = (
            jnp.sum(values * right_u, axis=1, keepdims=True)
            + grown * keys_right
            + jnp.sum(pair_grad, axis=1, keepdims=True)
        )
        cum_grad = (
            jnp.sum(spread_grad, axis=1, keepdims=True)
            + beta_grown * keys_right
            + grown * jnp.sum(queries * read_grad, axis=1, keepdims=True)
            - jnp.sum(tails_meet, axis=1, keepdims=True)
        )
        lane_at = lax.broadcasted_iota(jnp.int32, (PACK, 8), 1)
        dcols_ref[0, 0, first : first + PACK, :] = jnp.where(
            lane_at == 0, beta_grad, jnp.where(lane_at == 1, cum_grad, 0.0)
        )
        drows_ref[0, 0, :, first : first + PACK] = jnp.broadcast_to(
            -jnp.sum(spread_grad, axis=0, keepdims=True), (8, PACK)
        )
        for sub in range(PER_PACK):
            block = pack * PER_PACK + sub
            part = slice(sub * STRETCH, (sub + 1) * STRETCH)
            dlast_ref[0, 0, block : block + 1, :] = last_grad[sub] + jnp.sum(
                tails_meet[part], axis=0, keepdims=True
            )
        conv_out = conv_of(xs, conv_ref.at[0], cols_ref.at[0, 0], first, PACK)
        gate, _, _, _, scale_q, scale_k = front(conv_out)
        raw_q_grad = scale_q * (
            queries_grad - queries * jnp.sum(queries * queries_grad, axis=1, keepdims=True)
        )
        raw_k_grad = scale_k * (
            keys_grad - keys * jnp.sum(keys * keys_grad, axis=1, keepdims=True)
        )
        active_grad = jnp.concatenate([raw_q_grad, raw_k_grad, values_grad], axis=1)
        ds[HALO + first : HALO + first + PACK, :] = active_grad * (
            gate * (1.0 + conv_out * (1.0 - gate))
        )
    taps = []
    for reach in range(CONV):
        grad_rows = ds[HALO : HALO + piece, :]
        if reach > 0:
            grad_rows = grad_rows * cols_ref[0, 0, :, 4 + reach : 5 + reach]
        taps.append(
            jnp.sum(grad_rows * xs[HALO - reach : HALO - reach + piece, :], axis=0, keepdims=True)
        )
    cgrad_ref[0, 0] = jnp.concatenate(taps[::-1] + [jnp.zeros((8 - CONV, QKV), f32)], axis=0)
    total = ds[0 : HALO + piece, :] * conv_ref[0, CONV - 1 : CONV, :]
    for reach in range(1, CONV):
        masked = ds[HALO : HALO + piece, :] * cols_ref[0, 0, :, 4 + reach : 5 + reach]
        xs[HALO : HALO + piece, :] = masked
        xs[0:HALO, :] = jnp.zeros((HALO, QKV), f32)
        xs[HALO + piece : 2 * HALO + piece, :] = jnp.zeros((HALO, QKV), f32)
        total = total + xs[reach : reach + HALO + piece, :] * conv_ref[
            0, CONV - 1 - reach : CONV - reach, :
        ]
    hgrad_ref[0, 0] = total[:HALO, :]
    ds[0:piece, :] = total[HALO:, :]
    for place in range(tp):
        at = pl.multiple_of(order_ref[1 + place] * rows, 8)
        xgrad_ref[place, 0] = ds[pl.ds(at, rows), :].astype(bf16)


def shape_of(shape, dtype):
    return jax.ShapeDtypeStruct(shape, dtype)


def local_call(order, pre, halo, conv_w, cols, rows_in, steps, heads):
    tp, micro, rows, _ = pre.shape
    piece = tp * rows
    packs, blocks = piece // PACK, piece // STRETCH
    grid = pltpu.PrefetchScalarGridSpec(
        num_scalar_prefetch=1,
        grid=(micro,),
        in_specs=[
            pl.BlockSpec((tp, 1, rows, heads * QKV), lambda m, s: (0, m, 0, 0)),
            pl.BlockSpec((1, HALO, heads * QKV), lambda m, s: (m, 0, 0)),
            pl.BlockSpec((heads, 8, QKV), lambda m, s: (0, 0, 0)),
            pl.BlockSpec((1, heads, piece, 8), lambda m, s: (m, 0, 0, 0)),
            pl.BlockSpec((1, heads, 8, piece), lambda m, s: (m, 0, 0, 0)),
            pl.BlockSpec((1, heads, 2 * blocks, LANES), lambda m, s: (m, 0, 0, 0)),
        ],
        out_specs=[
            pl.BlockSpec((tp, 1, rows, heads * DV), lambda m, s: (0, m, 0, 0)),
            pl.BlockSpec((tp, 1, rows, heads * DK), lambda m, s: (0, m, 0, 0)),
            pl.BlockSpec((1, heads, blocks, DK, AUG), lambda m, s: (m, 0, 0, 0, 0)),
            pl.BlockSpec((1, heads, packs, PACK, PACK), lambda m, s: (m, 0, 0, 0, 0)),
            pl.BlockSpec((1, heads, blocks, DK, DK), lambda m, s: (m, 0, 0, 0, 0)),
            pl.BlockSpec((1, heads, DK, AUG), lambda m, s: (m, 0, 0, 0)),
        ],
        scratch_shapes=[
            pltpu.VMEM((heads, HALO + piece, QKV), f32),
            pltpu.VMEM((heads, piece, DV), f32),
            pltpu.VMEM((heads, piece, DK), f32),
        ],
    )
    return pl.pallas_call(
        local_kernel,
        grid_spec=grid,
        out_shape=[
            shape_of((tp, micro, rows, heads * DV), f32),
            shape_of((tp, micro, rows, heads * DK), bf16),
            shape_of((micro, heads, blocks, DK, AUG), bf16),
            shape_of((micro, heads, packs, PACK, PACK), bf16),
            shape_of((micro, heads, blocks, DK, DK), bf16),
            shape_of((micro, heads, DK, AUG), bf16),
        ],
        compiler_params=pltpu.CompilerParams(vmem_limit_bytes=VMEM_BYTES),
        name="delta_local",
    )(order, pre, halo, conv_w, cols, rows_in, steps)


def finish_call(order, maps, out_local, reach, pre, gain, heads):
    ctx = maps.shape[0]
    tp, micro, rows, _ = out_local.shape
    gate_at = heads * QKV // DV
    grid = pltpu.PrefetchScalarGridSpec(
        num_scalar_prefetch=1,
        grid=(micro, heads),
        in_specs=[
            pl.BlockSpec((ctx, 1, 1, DK, AUG), lambda m, a, s: (0, m, a, 0, 0)),
            pl.BlockSpec((tp, 1, rows, DV), lambda m, a, s: (0, m, 0, a)),
            pl.BlockSpec((tp, 1, rows, DK), lambda m, a, s: (0, m, 0, a)),
            pl.BlockSpec((tp, 1, rows, DV), lambda m, a, s: (0, m, 0, gate_at + a)),
            pl.BlockSpec((8, DV), lambda m, a, s: (0, 0)),
        ],
        out_specs=[
            pl.BlockSpec((tp, 1, rows, DV), lambda m, a, s: (0, m, 0, a)),
            pl.BlockSpec((1, 1, DK, DV), lambda m, a, s: (m, a, 0, 0)),
        ],
    )
    return pl.pallas_call(
        finish_kernel,
        grid_spec=grid,
        out_shape=[
            shape_of((tp, micro, rows, heads * DV), bf16),
            shape_of((micro, heads, DK, DV), f32),
        ],
        compiler_params=pltpu.CompilerParams(vmem_limit_bytes=VMEM_BYTES),
        name="delta_finish",
    )(order, maps, out_local, reach, pre, gain)


def unfinish_call(entry, out_local, reach, pre, gain, grad, heads):
    tp, micro, rows, _ = out_local.shape
    gate_at = heads * QKV // DV
    return pl.pallas_call(
        unfinish_kernel,
        grid=(micro, heads),
        in_specs=[
            pl.BlockSpec((1, 1, DK, DV), lambda m, a: (m, a, 0, 0)),
            pl.BlockSpec((tp, 1, rows, DV), lambda m, a: (0, m, 0, a)),
            pl.BlockSpec((tp, 1, rows, DK), lambda m, a: (0, m, 0, a)),
            pl.BlockSpec((tp, 1, rows, DV), lambda m, a: (0, m, 0, gate_at + a)),
            pl.BlockSpec((8, DV), lambda m, a: (0, 0)),
            pl.BlockSpec((tp, 1, rows, DV), lambda m, a: (0, m, 0, a)),
        ],
        out_specs=[
            pl.BlockSpec((tp, 1, rows, DV), lambda m, a: (0, m, 0, a)),
            pl.BlockSpec((tp, 1, rows, DV), lambda m, a: (0, m, 0, a)),
            pl.BlockSpec((1, 1, 8, DV), lambda m, a: (m, a, 0, 0)),
            pl.BlockSpec((1, 1, DK, DV), lambda m, a: (m, a, 0, 0)),
        ],
        out_shape=[
            shape_of((tp, micro, rows, heads * DV), bf16),
            shape_of((tp, micro, rows, heads * DV), bf16),
            shape_of((micro, heads, 8, DV), f32),
            shape_of((micro, heads, DK, DV), bf16),
        ],
        compiler_params=pltpu.CompilerParams(vmem_limit_bytes=VMEM_BYTES),
        name="delta_unfinish",
    )(entry, out_local, reach, pre, gain, grad)


def adjoint_call(
    order, pre, halo, conv_w, cols, rows_in, steps, starts, inverse, transit, entry, maps, bases, ograd, heads
):
    tp, micro, rows, _ = pre.shape
    ctx = maps.shape[0]
    piece = tp * rows
    packs, blocks = piece // PACK, piece // STRETCH
    grid = pltpu.PrefetchScalarGridSpec(
        num_scalar_prefetch=1,
        grid=(micro, heads),
        in_specs=[
            pl.BlockSpec((tp, 1, rows, QKV), lambda m, a, s: (0, m, 0, a)),
            pl.BlockSpec((1, HALO, QKV), lambda m, a, s: (m, 0, a)),
            pl.BlockSpec((1, 8, QKV), lambda m, a, s: (a, 0, 0)),
            pl.BlockSpec((1, 1, piece, 8), lambda m, a, s: (m, a, 0, 0)),
            pl.BlockSpec((1, 1, 8, piece), lambda m, a, s: (m, a, 0, 0)),
            pl.BlockSpec((1, 1, 2 * blocks, LANES), lambda m, a, s: (m, a, 0, 0)),
            pl.BlockSpec((1, 1, blocks, DK, AUG), lambda m, a, s: (m, a, 0, 0, 0)),
            pl.BlockSpec((1, 1, packs, PACK, PACK), lambda m, a, s: (m, a, 0, 0, 0)),
            pl.BlockSpec((1, 1, blocks, DK, DK), lambda m, a, s: (m, a, 0, 0, 0)),
            pl.BlockSpec((1, 1, DK, DV), lambda m, a, s: (m, a, 0, 0)),
            pl.BlockSpec((ctx, 1, 1, DK, DK), lambda m, a, s: (0, m, a, 0, DV // DK)),
            pl.BlockSpec((ctx, 1, 1, DK, DV), lambda m, a, s: (0, m, a, 0, 0)),
            pl.BlockSpec((tp, 1, rows, DV), lambda m, a, s: (0, m, 0, a)),
        ],
        out_specs=[
            pl.BlockSpec((tp, 1, rows, QKV), lambda m, a, s: (0, m, 0, a)),
            pl.BlockSpec((1, 1, HALO, QKV), lambda m, a, s: (m, a, 0, 0)),
            pl.BlockSpec((1, 1, 8, QKV), lambda m, a, s: (m, a, 0, 0)),
            pl.BlockSpec((1, 1, piece, 8), lambda m, a, s: (m, a, 0, 0)),
            pl.BlockSpec((1, 1, 8, piece), lambda m, a, s: (m, a, 0, 0)),
            pl.BlockSpec((1, 1, blocks, LANES), lambda m, a, s: (m, a, 0, 0)),
        ],
        scratch_shapes=[
            pltpu.VMEM((2 * HALO + piece, QKV), f32),
            pltpu.VMEM((piece, DV), bf16),
            pltpu.VMEM((2 * HALO + piece, QKV), f32),
        ],
    )
    return pl.pallas_call(
        adjoint_kernel,
        grid_spec=grid,
        out_shape=[
            shape_of((tp, micro, rows, heads * QKV), bf16),
            shape_of((micro, heads, HALO, QKV), f32),
            shape_of((micro, heads, 8, QKV), f32),
            shape_of((micro, heads, piece, 8), f32),
            shape_of((micro, heads, 8, piece), f32),
            shape_of((micro, heads, blocks, LANES), f32),
        ],
        compiler_params=pltpu.CompilerParams(vmem_limit_bytes=VMEM_BYTES),
        name="delta_adjoint",
    )(order, pre, halo, conv_w, cols, rows_in, steps, starts, inverse, transit, entry, maps, bases, ograd)


def rms_norm(values, gain_row):
    return (
        values * lax.rsqrt(jnp.mean(values * values, axis=-1, keepdims=True) + epsilon) * gain_row
    )


def rms_back(values, gain_row, grad):
    scale = lax.rsqrt(jnp.mean(values * values, axis=-1, keepdims=True) + epsilon)
    unit = values * scale
    gain_grad = jnp.sum(grad * unit, axis=0)
    inner = grad * gain_row
    return scale * (inner - unit * jnp.mean(inner * unit, axis=-1, keepdims=True)), gain_grad


def matmul(left, right):
    return jnp.dot(left, right, preferred_element_type=f32)


def matmul_nt(left, right):
    return lax.dot_general(left, right, (((1,), (1,)), ((), ())), preferred_element_type=f32)


def matmul_tn(left, right):
    return lax.dot_general(left, right, (((0,), (0,)), ((), ())), preferred_element_type=f32)


def flat(rows):
    return rows.reshape(-1, rows.shape[-1])


def token_layout(seq_lengths, positions):
    padded = (seq_lengths + STRETCH - 1) // STRETCH * STRETCH
    seq_ends = jnp.cumsum(padded)
    starts = seq_ends - padded
    inside = (positions[:, None] >= starts[None, :]) & (positions[:, None] < seq_ends[None, :])
    start_of = jnp.sum(jnp.where(inside, starts[None, :], 0), axis=1)
    length_of = jnp.sum(jnp.where(inside, seq_lengths[None, :], 0), axis=1)
    offset = positions - start_of
    return (offset, offset < length_of)


def rate_terms(rate_rel, decay_log, decay_bias, layout):
    offset, valid = layout[:2]
    heads = decay_log.shape[0]
    rates = in_order(rate_rel, "tp")
    tp, micro, rows, _ = rates.shape
    piece = tp * rows
    blocks = piece // STRETCH
    rates = rates.reshape(tp, micro, rows, heads, 2)
    rates = jnp.transpose(rates, (4, 1, 3, 0, 2)).reshape(2, micro, heads, piece)
    shifted = rates[0] + decay_bias[None, :, None]
    decays = -jnp.exp(decay_log)[None, :, None] * jax.nn.softplus(shifted)
    betas = jax.nn.sigmoid(rates[1])
    stretched = decays.reshape(micro, heads, blocks, STRETCH)
    order_at = jnp.arange(STRETCH)
    upto = (order_at[:, None] <= order_at[None, :]).astype(f32)
    cumulative = jnp.einsum(
        "mhbs,st->mhbt", stretched, upto, precision=lax.Precision.HIGHEST
    )
    last = cumulative[..., -1:]
    tails = jnp.exp(last - cumulative).reshape(micro, heads, piece)
    cumulative = cumulative.reshape(micro, heads, piece)
    grown = jnp.exp(cumulative)
    masks = [
        jnp.broadcast_to((offset >= reach).astype(f32)[:, None, :], cumulative.shape)
        for reach in range(1, CONV)
    ]
    cols = jnp.stack([cumulative, betas, grown, tails, betas * grown] + masks, axis=-1)
    rows_out = jnp.broadcast_to(cumulative[:, :, None, :], (micro, heads, 8, piece))
    retain = jnp.broadcast_to(jnp.exp(last), (micro, heads, blocks, LANES))
    keep = (offset[:, ::STRETCH] > 0).astype(f32)
    keep = jnp.broadcast_to(keep[:, None, :, None], (micro, heads, blocks, LANES))
    steps = jnp.concatenate([retain, keep], axis=2)
    return cols, rows_out, steps, (shifted, decays, betas, upto)


def rate_back(dcols, drows, dlast, kept, decay_log):
    shifted, decays, betas, upto = kept
    micro, heads, piece = shifted.shape
    blocks = piece // STRETCH
    cum_grad = (dcols[..., 1] + drows[:, :, 0, :]).reshape(micro, heads, blocks, STRETCH)
    last = jnp.sum(dlast, axis=-1)
    decay_grad = jnp.einsum("mhbt,st->mhbs", cum_grad, upto, precision=lax.Precision.HIGHEST)
    decay_grad = (decay_grad + last[..., None]).reshape(micro, heads, piece)
    log_grad = jnp.sum(decay_grad * decays, axis=(0, 2))
    shifted_grad = decay_grad * -jnp.exp(decay_log)[None, :, None] * jax.nn.sigmoid(shifted)
    bias_grad = jnp.sum(shifted_grad, axis=(0, 2))
    beta_grad = dcols[..., 0] * betas * (1.0 - betas)
    rate_grad = jnp.stack([shifted_grad, beta_grad], axis=-1)
    tp = lax.axis_size("tp")
    rate_grad = rate_grad.reshape(micro, heads, tp, piece // tp, 2)
    rate_grad = jnp.transpose(rate_grad, (2, 0, 3, 1, 4)).reshape(tp, micro, piece // tp, heads * 2)
    return to_relative(rate_grad, "tp").astype(bf16), log_grad, bias_grad


def last_place():
    tp = lax.axis_size("tp")
    place_of = jnp.asarray([turned(offset, "tp") for offset in range(tp)], jnp.int32)
    return place_of[lax.axis_index("tp") ^ (tp - 1)]


def layer_forward(hidden_in, weights, small, layout):
    w_in, w_ff, gains = weights
    conv_w, decay_log, decay_bias, gain_row, widths = small
    order, valid = layout[2], layout[3]
    heads, ff = widths
    tp = lax.axis_size("tp")
    micro, rows, _ = hidden_in.shape
    hidden = flat(hidden_in)
    normed = rms_norm(hidden, gains[0]).astype(bf16)
    normed_all = gather_rows(normed)
    pre = matmul(flat(normed_all), w_in).reshape(tp, micro, rows, -1)
    tail = lax.dynamic_index_in_dim(pre, last_place(), 0, False)[:, rows - HALO :, : heads * QKV]
    halo = passed_along(tail, "ctx", 1)
    rate_rel = pre[..., heads * (QKV + DV) : heads * (QKV + DV + 2)]
    cols, rows_in, steps, rate_kept = rate_terms(rate_rel, decay_log, decay_bias, layout)
    out_local, reach, starts, inverse, transit, piece_map = local_call(
        order, pre, halo, conv_w, cols, rows_in, steps, heads
    )
    maps = lax.all_gather(piece_map, "ctx")
    gated, entry = finish_call(order, maps, out_local, reach, pre, gain_row, heads)
    gated = gated.reshape(tp, micro * rows, heads * DV)
    w_out = w_ff[:, 2 * ff : 2 * ff + heads * DV]

    def mixer_part(low, high):
        return matmul_nt(flat(gated[low:high]), w_out).reshape(high - low, micro * rows, D)

    middle = hidden + valid * scatter_rows(mixer_part, tp)
    normed_two = rms_norm(middle, gains[1]).astype(bf16)
    normed_two_all = flat(gather_rows(normed_two))
    gate_ff = matmul(normed_two_all, w_ff[:, :ff])
    up_ff = matmul(normed_two_all, w_ff[:, ff : 2 * ff])
    hidden_ff = (jax.nn.silu(gate_ff) * up_ff).astype(bf16).reshape(tp, micro * rows, ff)
    w_down = w_ff[:, 2 * ff + heads * DV : 3 * ff + heads * DV]

    def ff_part(low, high):
        return matmul_nt(flat(hidden_ff[low:high]), w_down).reshape(high - low, micro * rows, D)

    leaving = middle + valid * scatter_rows(ff_part, tp)
    saved = (
        hidden,
        normed_all,
        pre,
        halo,
        cols,
        rows_in,
        steps,
        rate_kept,
        out_local,
        reach,
        starts,
        inverse,
        transit,
        maps,
        entry,
        gated,
        middle,
        normed_two_all,
        gate_ff,
        up_ff,
        hidden_ff,
    )
    return leaving.reshape(hidden_in.shape), saved


def layer_backward(grad_out, saved, weights, small, layout):
    (
        hidden,
        normed_all,
        pre,
        halo,
        cols,
        rows_in,
        steps,
        rate_kept,
        out_local,
        reach,
        starts,
        inverse,
        transit,
        maps,
        entry,
        gated,
        middle,
        normed_two_all,
        gate_ff,
        up_ff,
        hidden_ff,
    ) = saved
    w_in, w_ff, gains = weights
    conv_w, decay_log, decay_bias, gain_row, widths = small
    order, valid = layout[2], layout[3]
    heads, ff = widths
    tp = lax.axis_size("tp")
    micro, rows, _ = grad_out.shape
    grad = flat(grad_out)
    ff_grad = flat(gather_rows((valid * grad).astype(bf16)))
    w_down = w_ff[:, 2 * ff + heads * DV : 3 * ff + heads * DV]
    hidden_grad = matmul(ff_grad, w_down)
    open_at = jax.nn.sigmoid(gate_ff)
    gate_grad = (hidden_grad * up_ff * open_at * (1.0 + gate_ff * (1.0 - open_at))).astype(bf16)
    up_grad = (hidden_grad * gate_ff * open_at).astype(bf16)
    grad_down = matmul_tn(ff_grad, flat(hidden_ff))
    grad_gate = matmul_tn(normed_two_all, gate_grad)
    grad_up = matmul_tn(normed_two_all, up_grad)
    blocks_gate = gate_grad.reshape(tp, micro * rows, ff)
    blocks_up = up_grad.reshape(tp, micro * rows, ff)

    def two_part(low, high):
        part = matmul_nt(flat(blocks_gate[low:high]), w_ff[:, :ff]) + matmul_nt(
            flat(blocks_up[low:high]), w_ff[:, ff : 2 * ff]
        )
        return part.reshape(high - low, micro * rows, D)

    middle_part, gain_two = rms_back(middle, gains[1], scatter_rows(two_part, tp))
    middle_grad = grad + middle_part
    mixer_grad = flat(gather_rows((valid * middle_grad).astype(bf16)))
    w_out = w_ff[:, 2 * ff : 2 * ff + heads * DV]
    gated_grad = matmul(mixer_grad, w_out).reshape(tp, micro, rows, heads * DV)
    out_grad, gate_low, gain_grad, base = unfinish_call(
        entry, out_local, reach, pre, gain_row, gated_grad, heads
    )
    bases = lax.all_gather(base, "ctx")
    grad_out_w = matmul_tn(mixer_grad, flat(gated))
    low_ff = jnp.concatenate(
        [part.astype(bf16) for part in (grad_gate, grad_up, grad_out_w, grad_down)], axis=1
    )
    owned_ff = lax.psum_scatter(low_ff, "ctx", scatter_dimension=0, tiled=True)
    x_grad, halo_grad, conv_grad, dcols, drows, dlast = adjoint_call(
        order, pre, halo, conv_w, cols, rows_in, steps, starts, inverse, transit, entry, maps, bases, out_grad, heads
    )
    rate_low, log_grad, bias_grad = rate_back(dcols, drows, dlast, rate_kept, decay_log)
    back_rows = passed_along(halo_grad, "ctx", -1)
    back_rows = jnp.transpose(back_rows, (0, 2, 1, 3)).reshape(1, micro, HALO, heads * QKV)
    at = last_place()
    zero = jnp.zeros((), jnp.int32)
    corner = (at, zero, zero + rows - HALO, zero)
    tail = lax.dynamic_slice(x_grad, corner, (1, micro, HALO, heads * QKV))
    tail = (tail.astype(f32) + back_rows).astype(bf16)
    x_grad = lax.dynamic_update_slice(x_grad, tail, corner)
    spare = jnp.zeros((tp, micro, rows, w_in.shape[1] - heads * (QKV + DV + 2)), bf16)
    pre_grad = jnp.concatenate([x_grad, gate_low, rate_low, spare], axis=-1)
    pre_grad = pre_grad.reshape(tp, micro * rows, -1)

    def one_part(low, high):
        return matmul_nt(flat(pre_grad[low:high]), w_in).reshape(high - low, micro * rows, D)

    hidden_part, gain_one = rms_back(hidden, gains[0], scatter_rows(one_part, tp))
    leaving = middle_grad + hidden_part
    low_in = matmul_tn(flat(normed_all), flat(pre_grad)).astype(bf16)
    owned_in = lax.psum_scatter(low_in, "ctx", scatter_dimension=0, tiled=True)
    conv_grad = jnp.sum(conv_grad, axis=0)[:, :CONV]
    gain_grad = jnp.sum(gain_grad[:, :, 0], axis=(0, 1))
    small_grads = (conv_grad, log_grad, bias_grad, gain_grad, gain_one, gain_two)
    return leaving.reshape(grad_out.shape), owned_in, owned_ff, small_grads


def body(
    inputs,
    cotangent,
    lengths,
    norm_gain,
    w_qkv,
    w_gate,
    w_rates,
    conv_weight,
    decay_log,
    decay_bias,
    out_gain,
    w_out,
    w_gu,
    w_down,
):
    tp = lax.axis_size("tp")
    ctx = lax.axis_size("ctx")
    micro, shard_rows, _ = inputs.shape
    piece_rows = shard_rows * tp
    layers = w_qkv.shape[0]
    own = w_qkv.shape[1]
    heads = w_qkv.shape[2]
    ff = w_gu.shape[3]
    ctx_at = lax.axis_index("ctx")
    tp_at = lax.axis_index("tp")
    piece_pos = ctx_at * piece_rows + jnp.arange(piece_rows, dtype=jnp.int32)
    shard_pos = (ctx_at * tp + tp_at) * shard_rows + jnp.arange(shard_rows, dtype=jnp.int32)
    offset = jnp.stack([token_layout(lengths[m], piece_pos)[0] for m in range(micro)])
    valid = jnp.stack([token_layout(lengths[m], shard_pos)[1] for m in range(micro)])
    valid = valid.astype(f32).reshape(-1, 1)
    order = jnp.stack([ctx_at] + [tp_at ^ turned(place, "tp") for place in range(tp)])
    layout = (offset, None, order.astype(jnp.int32), valid)

    gains = in_order(gather_blocks(norm_gain, "ctx"), "ctx")
    gains = jnp.transpose(gains, (1, 2, 0, 3)).reshape(layers, 2, D).astype(f32)
    in_width = heads * (QKV + DV + 2)
    in_spare = -in_width % LANES
    weights = []
    for layer_at in range(layers):
        shard_in = jnp.concatenate(
            [
                w_qkv[layer_at].reshape(own, -1),
                w_gate[layer_at].reshape(own, -1),
                w_rates[layer_at].reshape(own, -1),
                jnp.zeros((own, in_spare), bf16),
            ],
            axis=1,
        )
        shard_ff = jnp.concatenate(
            [
                w_gu[layer_at, 0],
                w_gu[layer_at, 1],
                w_out[layer_at].reshape(-1, own).T,
                w_down[layer_at].T,
            ],
            axis=1,
        )
        weights.append(
            (
                lax.all_gather(shard_in, "ctx", axis=0, tiled=True),
                lax.all_gather(shard_ff, "ctx", axis=0, tiled=True),
                gains[layer_at],
            )
        )
    smalls = []
    for layer_at in range(layers):
        conv_w = jnp.transpose(conv_weight[layer_at], (1, 0, 2))
        conv_w = jnp.concatenate([conv_w, jnp.zeros((heads, 8 - CONV, QKV), f32)], axis=1)
        gain_row = jnp.broadcast_to(out_gain[layer_at][None], (8, DV))
        smalls.append(
            (conv_w, decay_log[layer_at], decay_bias[layer_at], gain_row, (heads, ff))
        )

    hidden_now = inputs.astype(f32)
    saved_all = []
    for layer_at in range(layers):
        hidden_now, saved = layer_forward(hidden_now, weights[layer_at], smalls[layer_at], layout)
        saved_all.append(saved)
    grad_now = cotangent
    big = [None] * layers
    small = [None] * layers
    for layer_at in reversed(range(layers)):
        grad_now, owned_in, owned_ff, small_grads = layer_backward(
            grad_now, saved_all[layer_at], weights[layer_at], smalls[layer_at], layout
        )
        big[layer_at] = (owned_in.astype(f32), owned_ff.astype(f32))
        small[layer_at] = small_grads

    head_parts = [jnp.stack([small[at][member] for at in range(layers)]) for member in range(3)]
    wide_parts = [jnp.stack([small[at][member] for at in range(layers)]) for member in range(3, 6)]
    sizes = [part.size for part in head_parts + wide_parts]
    head_size = sum(sizes[:3])
    packed = jnp.concatenate([part.reshape(-1) for part in head_parts + wide_parts])
    spare = -packed.size % (8 * LANES)
    packed = jnp.concatenate([packed, jnp.zeros((spare,), f32)]).reshape(-1, LANES)
    packed = sum_over(packed, "ctx").reshape(-1)
    wide = packed[head_size : sum(sizes)]
    wide_size = wide.size
    spare = -wide_size % (8 * LANES)
    wide = jnp.concatenate([wide, jnp.zeros((spare,), f32)]).reshape(-1, LANES)
    wide = sum_over(wide, "tp").reshape(-1)
    parts = []
    start = 0
    for part, size in zip(head_parts, sizes[:3]):
        parts.append(packed[start : start + size].reshape(part.shape))
        start += size
    start = 0
    for part, size in zip(wide_parts, sizes[3:]):
        parts.append(wide[start : start + size].reshape(part.shape))
        start += size
    conv_grad, log_grad, bias_grad, ogain_grad, gain_one, gain_two = parts
    conv_grad = jnp.transpose(conv_grad, (0, 2, 1, 3))
    norm_grad = jnp.stack([gain_one, gain_two], axis=1)
    norm_grad = lax.dynamic_slice_in_dim(norm_grad, ctx_at * own, own, 2)

    in_all = jnp.stack([big[at][0] for at in range(layers)])
    ff_all = jnp.stack([big[at][1] for at in range(layers)])
    qkv_end, gate_end = heads * QKV, heads * (QKV + DV)
    grad_qkv = in_all[..., :qkv_end].reshape(w_qkv.shape)
    grad_gate_w = in_all[..., qkv_end:gate_end].reshape(w_gate.shape)
    grad_rates = in_all[..., gate_end:in_width].reshape(w_rates.shape)
    grad_gu = jnp.stack([ff_all[..., :ff], ff_all[..., ff : 2 * ff]], axis=1)
    out_end = 2 * ff + heads * DV
    grad_out_w = jnp.swapaxes(ff_all[..., 2 * ff : out_end], 1, 2).reshape(w_out.shape)
    grad_down = jnp.swapaxes(ff_all[..., out_end:], 1, 2)
    return (
        hidden_now,
        grad_now,
        norm_grad,
        grad_qkv,
        grad_gate_w,
        grad_rates,
        conv_grad,
        log_grad,
        bias_grad,
        ogain_grad,
        grad_out_w,
        grad_gu,
        grad_down,
    )


def solution(mesh):
    placed = (
        P(None, ("ctx", "tp"), None),
        P(None, ("ctx", "tp"), None),
        P(),
        P(None, None, "ctx"),
        P(None, "ctx", "tp", None),
        P(None, "ctx", "tp", None),
        P(None, "ctx", "tp", None),
        P(None, None, "tp", None),
        P(None, "tp"),
        P(None, "tp"),
        P(),
        P(None, "tp", None, "ctx"),
        P(None, None, "ctx", "tp"),
        P(None, "tp", "ctx"),
    )
    return jax.shard_map(
        body,
        mesh=mesh,
        in_specs=placed,
        out_specs=(
            P(None, ("ctx", "tp"), None),
            P(None, ("ctx", "tp"), None),
            P(None, None, "ctx"),
            P(None, "ctx", "tp", None),
            P(None, "ctx", "tp", None),
            P(None, "ctx", "tp", None),
            P(None, None, "tp", None),
            P(None, "tp"),
            P(None, "tp"),
            P(),
            P(None, "tp", None, "ctx"),
            P(None, None, "ctx", "tp"),
            P(None, "tp", "ctx"),
        ),
        check_vma=False,
    )
```

```python
from functools import partial

import jax
import jax.numpy as jnp
from jax import lax
from jax.experimental import pallas as pl
from jax.experimental.pallas import tpu as pltpu
from jax.sharding import PartitionSpec as P

D = 1024
DK = 128
DV = 256
QKV = 512
AUG = DV + DK
CONV = 4
STRETCH = 64
PACK = 256
PER_PACK = PACK // STRETCH
LANES = 128
HALO = 8

epsilon = 1e-05
unit_eps = 1e-06
f32 = jnp.float32
bf16 = jnp.bfloat16
VMEM_BYTES = 56 * 1024 * 1024


def swap(value, axis, bit):
    count = lax.axis_size(axis)
    return lax.ppermute(value, axis, [(i, i ^ bit) for i in range(count)])


def bits_of(axis):
    count = lax.axis_size(axis)
    bits = []
    bit = count // 2
    while bit >= 1:
        bits.append(bit)
        bit //= 2
    return bits


def turned(place, axis):
    offset = 0
    for step, bit in enumerate(bits_of(axis)):
        if place >> step & 1:
            offset |= bit
    return offset


def gather_blocks(value, axis):
    blocks = value[None]
    for bit in bits_of(axis):
        blocks = jnp.concatenate([blocks, swap(blocks, axis, bit)], axis=0)
    return blocks


def in_order(blocks, axis):
    count = lax.axis_size(axis)
    me = lax.axis_index(axis)
    place_of = [turned(offset, axis) for offset in range(count)]
    place_of = jnp.asarray(place_of, jnp.int32)
    return jnp.stack(
        [
            lax.dynamic_index_in_dim(blocks, place_of[me ^ device], 0, False)
            for device in range(count)
        ]
    )


def to_relative(blocks, axis):
    me = lax.axis_index(axis)
    return jnp.stack(
        [
            lax.dynamic_index_in_dim(blocks, me ^ turned(place, axis), 0, False)
            for place in range(blocks.shape[0])
        ]
    )


def gather_rows(rows):
    return gather_blocks(rows, "tp")


def scatter_rows(product_of, count):
    half = count // 2
    kept = None
    for bit in reversed(bits_of("tp")):
        if kept is None:
            sent = product_of(half, count).astype(bf16)
            received = swap(sent, "tp", bit)
            kept = product_of(0, half) + received.astype(f32)
        else:
            received = swap(kept[half:].astype(bf16), "tp", bit)
            kept = kept[:half] + received.astype(f32)
        half //= 2
    return kept[0]


def sum_over(value, axis):
    for bit in bits_of(axis):
        value = value + swap(value, axis, bit)
    return value


def ring_of(count):
    if count % 4 != 0 or count < 8:
        return list(range(count))
    wide = count // 4
    ring = [row * wide for row in range(4)]
    for row in reversed(range(4)):
        columns = range(1, wide) if row % 2 == 1 else reversed(range(1, wide))
        ring += [row * wide + column for column in columns]
    return ring


def ring_gather(value, **options):
    ring = ring_of(lax.axis_size("ctx"))
    return lax.all_gather(value, "ctx", axis_index_groups=[ring], **options)


def ring_scatter(value):
    ring = ring_of(lax.axis_size("ctx"))
    return lax.psum_scatter(
        value, "ctx", scatter_dimension=0, tiled=True, axis_index_groups=[ring]
    )


def ring_places():
    ring = ring_of(lax.axis_size("ctx"))
    return [ring.index(device) for device in range(len(ring))]


def blocks_moved(value, source_of):
    parts = jnp.split(value, len(source_of), axis=-1)
    return jnp.concatenate([parts[source] for source in source_of], axis=-1)


def after(value, *others):
    return lax.optimization_barrier((value,) + others)[0]


def passed_along(value, axis, steps):
    count = lax.axis_size(axis)
    initial, last = (max(0, -steps), min(count, count - steps))
    return lax.ppermute(value, axis, [(source, source + steps) for source in range(initial, last)])


def dot(left, right, contract):
    return lax.dot_general(
        left.astype(bf16),
        right.astype(bf16),
        (contract, ((), ())),
        preferred_element_type=f32,
    )


def nn(left, right):
    return dot(left, right, ((1,), (0,)))


def nt(left, right):
    return dot(left, right, ((1,), (1,)))


def tn(left, right):
    return dot(left, right, ((0,), (0,)))


def halves(value):
    high = value.astype(bf16)
    return high, (value - high.astype(f32)).astype(bf16)


def nn_fine(left, right):
    left_hi, left_lo = left
    right_hi, right_lo = right
    return nn(left_hi, right_hi) + (nn(left_hi, right_lo) + nn(left_lo, right_hi))


def sigmoid(value):
    return 1.0 / (1.0 + jnp.exp(-value))


def index_grids():
    row_at = lax.broadcasted_iota(jnp.int32, (PACK, PACK), 0)
    col_at = lax.broadcasted_iota(jnp.int32, (PACK, PACK), 1)
    return row_at, col_at


def unit_lower_inverse(lower, row_at, col_at):
    eye = (row_at == col_at).astype(f32)
    small = jnp.where(row_at // 8 == col_at // 8, lower, 0.0)
    small_h = halves(small)
    power2 = nn_fine(small_h, small_h)
    power2_h = halves(power2)
    inverse = eye - small
    inverse = inverse + nn_fine(halves(inverse), power2_h)
    power4 = nn_fine(power2_h, power2_h)
    inverse = inverse + nn_fine(halves(inverse), halves(power4))
    size = 8
    while size < STRETCH:
        corner = jnp.where(
            (row_at // (2 * size) == col_at // (2 * size)) & (row_at // size != col_at // size),
            lower,
            0.0,
        )
        inverse_h = halves(inverse)
        inverse = inverse - nn_fine(inverse_h, halves(nn_fine(halves(corner), inverse_h)))
        size *= 2
    return inverse


def load_rates(order_ref, rate_ref, rs):
    tp, _, rows, _ = rate_ref.shape
    for place in range(tp):
        at = pl.multiple_of(order_ref[1 + place] * rows, 8)
        rs[pl.ds(at, rows), :] = rate_ref[place, 0]


def rate_parts(raw, decay_ref):
    shifted = raw + decay_ref[1:2, :]
    soft = jnp.maximum(shifted, 0.0) + jnp.log1p(jnp.exp(-jnp.abs(shifted)))
    return shifted, decay_ref[0:1, :] * soft, sigmoid(raw)


def exact_sums(pattern, values):
    high, low = halves(values)
    return nn(pattern, high) + nn(pattern, low)


def decay_terms(decays, row_at, col_at):
    same = row_at // STRETCH == col_at // STRETCH
    upto = (same & (row_at >= col_at)).astype(f32).astype(bf16)
    whole = same.astype(f32).astype(bf16)
    running = exact_sums(upto, decays)
    total = exact_sums(whole, decays)
    high, low = halves(decays[:, :8])
    running_rows = dot(high, upto, ((0,), (1,))) + dot(low, upto, ((0,), (1,)))
    return running, running_rows, total


def load_pieces(order_ref, x_ref, halo_ref, xs, head):
    tp, _, rows, _ = x_ref.shape
    lanes = pl.ds(head * QKV, QKV)
    xs[0:HALO, :] = halo_ref[0, :, lanes]
    for place in range(tp):
        at = pl.multiple_of(order_ref[1 + place] * rows + HALO, 8)
        xs[pl.ds(at, rows), :] = x_ref[place, 0, :, lanes]


def conv_of(xs, weights, cols, first, count):
    total = None
    for reach in range(CONV):
        rows = xs[HALO + first - reach : HALO + first - reach + count, :]
        if reach > 0:
            rows = rows * cols[first : first + count, reach - 1 : reach]
        term = rows * weights[CONV - 1 - reach : CONV - reach, :]
        total = term if total is None else total + term
    return total


def front(conv_out):
    gate = sigmoid(conv_out)
    active = conv_out * gate
    raw_q, raw_k, values = active[:, :DK], active[:, DK : 2 * DK], active[:, 2 * DK :]
    scale_q = lax.rsqrt(jnp.sum(raw_q * raw_q, axis=1, keepdims=True) + unit_eps)
    scale_k = lax.rsqrt(jnp.sum(raw_k * raw_k, axis=1, keepdims=True) + unit_eps)
    return gate, raw_q * scale_q, raw_k * scale_k, values, scale_q, scale_k


def pack_terms(queries, keys, running, running_row, row_at, col_at):
    inside = (row_at // STRETCH == col_at // STRETCH) & (row_at >= col_at)
    spread = running - running_row
    weight = jnp.where(inside, jnp.exp(jnp.where(inside, spread, 0.0)), 0.0)
    keys_low = keys.astype(bf16)
    key_dots = nt(keys_low, keys_low)
    scores = nt(queries, keys_low) * weight
    pair = jnp.where(row_at > col_at, key_dots * weight, 0.0)
    return weight, pair, scores


def local_kernel(
    order_ref,
    x_ref,
    rate_ref,
    halo_ref,
    conv_ref,
    decay_ref,
    cols_ref,
    out_ref,
    reach_ref,
    starts_ref,
    inverse_ref,
    transit_ref,
    map_ref,
    xs,
    rs,
    o_scr,
    r_scr,
):
    tp, _, rows, _ = x_ref.shape
    heads = conv_ref.shape[0]
    piece = tp * rows
    packs = piece // PACK
    blocks = piece // STRETCH
    row_at, col_at = index_grids()
    units = [(head, pack) for head in range(heads) for pack in range(packs)]
    held = {}
    shared = {}
    load_rates(order_ref, rate_ref, rs)
    for head in range(heads):
        load_pieces(order_ref, x_ref, halo_ref, xs.at[head], head)
    for pack in range(packs):
        _, decays, betas = rate_parts(rs[pack * PACK : (pack + 1) * PACK, :], decay_ref)
        running, running_rows, total = decay_terms(decays, row_at, col_at)
        shared[pack] = (
            running,
            running_rows,
            betas,
            jnp.exp(running),
            jnp.exp(total - running),
            jnp.exp(total),
        )
    for head, pack in units:
        first = pack * PACK
        conv_out = conv_of(xs.at[head], conv_ref.at[head], cols_ref.at[0], first, PACK)
        _, queries, keys, values, _, _ = front(conv_out)
        lane = 2 * head
        running, running_rows, betas, grown, tail, _ = shared[pack]
        beta = betas[:, lane + 1 : lane + 2]
        grown = grown[:, lane : lane + 1]
        weight, pair, scores = pack_terms(
            queries,
            keys,
            running[:, lane : lane + 1],
            running_rows[lane : lane + 1, :],
            row_at,
            col_at,
        )
        cols = (beta, grown, tail[:, lane : lane + 1], beta * grown)
        held[head, pack] = (queries, keys, values, cols, pair * beta, scores)
    inverses = {
        unit: unit_lower_inverse(held[unit][4], row_at, col_at).astype(bf16) for unit in units
    }
    solved = {}
    moves = {}
    for unit in units:
        head, pack = unit
        queries, keys, values, cols, _, scores = held[unit]
        inverse_ref[0, head, pack] = inverses[unit]
        solved_w = nn(inverses[unit], keys * cols[3])
        solved_u = nn(inverses[unit], values * cols[0])
        tails = (keys * cols[2]).astype(bf16)
        solved_w = solved_w.astype(bf16)
        solved_u_low = solved_u.astype(bf16)
        for sub in range(PER_PACK):
            part = slice(sub * STRETCH, (sub + 1) * STRETCH)
            block = pack * PER_PACK + sub
            transit = tn(tails[part], solved_w[part]).astype(bf16)
            transit_ref[0, head, block] = transit
            moves[head, block] = (transit, tn(tails[part], solved_u_low[part]))
        solved[unit] = (solved_w, solved_u)
    eye = (row_at[:DK, :DK] == col_at[:DK, :DK]).astype(f32)
    biases = [jnp.zeros((DK, DV), f32) for _ in range(heads)]
    maps = [eye for _ in range(heads)]
    for block in range(blocks):
        for head in range(heads):
            at = block % PER_PACK * STRETCH
            retain = shared[block // PER_PACK][5][at : at + 1, 2 * head : 2 * head + 1]
            keep = cols_ref[0, block * STRETCH : block * STRETCH + 1, 3:4]
            bias = biases[head] * keep
            whole = maps[head] * keep
            low = jnp.concatenate([bias, whole], axis=1).astype(bf16)
            starts_ref[0, head, block] = low
            transit, fresh = moves[head, block]
            moved = nn(transit, low)
            biases[head] = bias * retain - moved[:, :DV] + fresh
            maps[head] = whole * retain - moved[:, DV:]
    for head in range(heads):
        map_ref[0, head, :, :DV] = biases[head].astype(bf16)
        map_ref[0, head, :, DV:] = maps[head].astype(bf16)
    for unit in units:
        head, pack = unit
        queries, keys, values, cols, _, scores = held[unit]
        solved_w, solved_u = solved[unit]
        reading = (queries * cols[1]).astype(bf16)
        carried, recalled = [], []
        for sub in range(PER_PACK):
            part = slice(sub * STRETCH, (sub + 1) * STRETCH)
            start = starts_ref[0, head, pack * PER_PACK + sub]
            both = nn(jnp.concatenate([reading[part], solved_w[part]], axis=0), start)
            carried.append(both[:STRETCH])
            recalled.append(both[STRETCH:])
        carried = jnp.concatenate(carried, axis=0)
        recalled = jnp.concatenate(recalled, axis=0)
        low_scores = scores.astype(bf16)
        first = pack * PACK
        o_scr[head, first : first + PACK, :] = carried[:, :DV] + nn(
            low_scores, solved_u - recalled[:, :DV]
        )
        r_scr[head, first : first + PACK, :] = carried[:, DV:] - nn(low_scores, recalled[:, DV:])
    for place in range(tp):
        at = pl.multiple_of(order_ref[1 + place] * rows, 8)
        for head in range(heads):
            out_ref[place, 0, :, head * DV : (head + 1) * DV] = o_scr[head, pl.ds(at, rows), :]
            reach_ref[place, 0, :, head * DK : (head + 1) * DK] = r_scr[
                head, pl.ds(at, rows), :
            ].astype(bf16)


def finish_kernel(order_ref, maps_ref, out_ref, reach_ref, gate_ref, gain_ref, gated_ref, entry_ref):
    tp = out_ref.shape[0]

    def one(step, entry):
        whole = maps_ref[order_ref[1 + tp + step], 0, 0]
        return whole[:, :DV].astype(f32) + nn(whole[:, DV:], entry)

    entry = lax.fori_loop(0, order_ref[0], one, jnp.zeros((DK, DV), f32))
    entry_ref[0, 0] = entry
    entry_low = entry.astype(bf16)
    for place in range(tp):
        outputs = out_ref[place, 0] + nn(reach_ref[place, 0], entry_low)
        scale = lax.rsqrt(jnp.mean(outputs * outputs, axis=1, keepdims=True) + epsilon)
        gate = gate_ref[place, 0]
        gated = outputs * scale * gain_ref[0:1, :] * (gate * sigmoid(gate))
        gated_ref[place, 0] = gated.astype(bf16)


def unfinish_kernel(
    entry_ref, out_ref, reach_ref, gate_ref, gain_ref, grad_ref, ograd_ref, zgrad_ref, ggrad_ref, base_ref
):
    tp = out_ref.shape[0]
    entry_low = entry_ref[0, 0].astype(bf16)
    gain = gain_ref[0:1, :]
    base = jnp.zeros((DK, DV), f32)
    gain_grad = jnp.zeros((1, DV), f32)
    for place in range(tp):
        reach = reach_ref[place, 0]
        outputs = out_ref[place, 0] + nn(reach, entry_low)
        scale = lax.rsqrt(jnp.mean(outputs * outputs, axis=1, keepdims=True) + epsilon)
        unit = outputs * scale
        gate = gate_ref[place, 0]
        open_at = sigmoid(gate)
        grad = grad_ref[place, 0]
        normed_grad = grad * (gate * open_at)
        gate_grad = grad * (unit * gain) * (open_at * (1.0 + gate * (1.0 - open_at)))
        zgrad_ref[place, 0] = gate_grad.astype(bf16)
        gain_grad = gain_grad + jnp.sum(normed_grad * unit, axis=0, keepdims=True)
        inner = normed_grad * gain
        out_grad = scale * (inner - unit * jnp.mean(inner * unit, axis=1, keepdims=True))
        out_grad = out_grad.astype(bf16)
        ograd_ref[place, 0] = out_grad
        base = base + tn(reach, out_grad)
    ggrad_ref[0, 0] = jnp.broadcast_to(gain_grad, (8, DV))
    base_ref[0, 0] = base.astype(bf16)


def adjoint_kernel(
    order_ref,
    x_ref,
    rate_ref,
    halo_ref,
    conv_ref,
    decay_ref,
    cols_ref,
    starts_ref,
    inverse_ref,
    transit_ref,
    entry_ref,
    maps_ref,
    bases_ref,
    ograd_ref,
    xgrad_ref,
    hgrad_ref,
    cgrad_ref,
    rgrad_ref,
    dgrad_ref,
    xs,
    rs,
    gs,
    ds,
    rgs,
):
    tp, _, rows, _ = x_ref.shape
    piece = tp * rows
    packs = piece // PACK
    blocks = piece // STRETCH
    ctx = maps_ref.shape[0]
    row_at, col_at = index_grids()
    head_at = pl.program_id(1)
    load_pieces(order_ref, x_ref, halo_ref, xs, 0)
    load_rates(order_ref, rate_ref, rs)
    lanes = lax.broadcasted_iota(jnp.int32, (PACK, LANES), 1)
    decay_lane = (lanes == 2 * head_at).astype(f32)
    beta_lane = (lanes == 2 * head_at + 1).astype(f32)

    @pl.when(head_at == 0)
    def _():
        rgs[...] = jnp.zeros_like(rgs)

    for place in range(tp):
        at = pl.multiple_of(order_ref[1 + place] * rows, 16)
        gs[pl.ds(at, rows), :] = ograd_ref[place, 0]

    def one(step, grad):
        source = order_ref[1 + tp + ctx - 1 - step]
        return bases_ref[source, 0, 0].astype(f32) + tn(maps_ref[source, 0, 0], grad)

    after = lax.fori_loop(0, ctx - 1 - order_ref[0], one, jnp.zeros((DK, DV), f32))
    entry_low = entry_ref[0, 0].astype(bf16)
    held = {}
    starts = {}
    turns = {}
    retains = {}
    decay_sum = jnp.zeros((1, 1), f32)
    rate_sum = jnp.zeros((1, LANES), f32)
    for pack in range(packs):
        first = pack * PACK
        conv_out = conv_of(xs, conv_ref.at[0], cols_ref.at[0], first, PACK)
        _, queries, keys, values, _, _ = front(conv_out)
        shifted, decays, betas = rate_parts(rs[first : first + PACK, :], decay_ref)
        decay = jnp.sum(decays * decay_lane, axis=1, keepdims=True)
        beta = jnp.sum(betas * beta_lane, axis=1, keepdims=True)
        running, running_rows, total = decay_terms(
            jnp.broadcast_to(decay, (PACK, LANES)), row_at, col_at
        )
        retains[pack] = jnp.exp(total)
        grown = jnp.exp(running)[:, 0:1]
        cols = (beta, grown, jnp.exp(total - running)[:, 0:1], beta * grown)
        weight, pair, scores = pack_terms(
            queries, keys, running[:, 0:1], running_rows[0:1, :], row_at, col_at
        )
        inverse = inverse_ref[0, 0, pack]
        solved_w = nn(inverse, keys * cols[3]).astype(bf16)
        solved_u = nn(inverse, values * cols[0])
        out_grad = gs[first : first + PACK, :]
        through = tn(scores, out_grad)
        through_low = through.astype(bf16)
        reading = (queries * cols[1]).astype(bf16)
        fresh = []
        for sub in range(PER_PACK):
            part = slice(sub * STRETCH, (sub + 1) * STRETCH)
            block = pack * PER_PACK + sub
            start = starts_ref[0, 0, block]
            start = start[:, :DV].astype(f32) + nn(start[:, DV:], entry_low)
            starts[block] = start
            fresh.append(solved_u[part] - nn(solved_w[part], start))
            turns[block] = tn(reading[part], out_grad[part]) - tn(solved_w[part], through_low[part])
        held[pack] = (
            queries,
            keys,
            values,
            cols,
            weight,
            pair,
            scores,
            inverse,
            solved_w,
            solved_u,
            out_grad,
            through,
            jnp.concatenate(fresh, axis=0),
            shifted,
            decay,
            betas,
        )
    grads = {}
    grad = after
    for block in reversed(range(blocks)):
        grads[block] = grad
        at = block % PER_PACK * STRETCH
        grad = grad * retains[block // PER_PACK][at : at + 1, 0:1]
        grad = grad - tn(transit_ref[0, 0, block], grads[block]) + turns[block]
        grad = grad * cols_ref[0, block * STRETCH : block * STRETCH + 1, 3:4]
    ds[0:HALO, :] = jnp.zeros((HALO, QKV), f32)
    ds[HALO + piece : 2 * HALO + piece, :] = jnp.zeros((HALO, QKV), f32)
    for pack in range(packs):
        first = pack * PACK
        (
            queries,
            keys,
            values,
            cols,
            weight,
            pair,
            scores,
            inverse,
            solved_w,
            solved_u,
            out_grad,
            through,
            fresh,
            shifted,
            decay,
            betas,
        ) = held[pack]
        beta, grown, tail, beta_grown = cols
        tails = keys * tail
        tails_low = tails.astype(bf16)
        fresh_low = fresh.astype(bf16)
        fresh_grad, read_grad, solved_w_grad, tails_grad, last_grad = [], [], [], [], []
        for sub in range(PER_PACK):
            part = slice(sub * STRETCH, (sub + 1) * STRETCH)
            block = pack * PER_PACK + sub
            grad_now = grads[block]
            grad_low = grad_now.astype(bf16)
            now = through[part] + nn(tails_low[part], grad_low)
            fresh_grad.append(now)
            both = nt(jnp.concatenate([out_grad[part], now.astype(bf16)], axis=0), starts[block])
            read_grad.append(both[:STRETCH])
            solved_w_grad.append(-both[STRETCH:])
            tails_grad.append(nt(fresh_low[part], grad_low))
            retain = retains[pack][sub * STRETCH : sub * STRETCH + 1, 0:1]
            meet = starts[block] * grad_now
            last_grad.append(
                retain * jnp.sum(meet[:, :DK] + meet[:, DK:], axis=0, keepdims=True)
            )
        fresh_grad = jnp.concatenate(fresh_grad, axis=0)
        read_grad = jnp.concatenate(read_grad, axis=0)
        solved_w_grad = jnp.concatenate(solved_w_grad, axis=0)
        tails_grad = jnp.concatenate(tails_grad, axis=0)
        score_grad = nt(out_grad, fresh_low)
        dots_grad = (score_grad * weight).astype(bf16)
        right_grad = tn(inverse, jnp.concatenate([fresh_grad, solved_w_grad], axis=1))
        right_u, right_w = right_grad[:, :DV], right_grad[:, DV:]
        lower_grad = -(nt(right_u, solved_u) + nt(right_w, solved_w))
        lower_grad = jnp.where(row_at > col_at, lower_grad, 0.0)
        pair_grad = lower_grad * pair
        key_dots_grad = (lower_grad * weight * beta).astype(bf16)
        spread_grad = pair_grad * beta + score_grad * scores
        keys_low = keys.astype(bf16)
        queries_low = queries.astype(bf16)
        keys_right = jnp.sum(keys * right_w, axis=1, keepdims=True)
        tails_meet = tails * tails_grad
        keys_grad = (
            beta_grown * right_w
            + nn(key_dots_grad, keys_low)
            + tn(key_dots_grad, keys_low)
            + tn(dots_grad, queries_low)
            + tail * tails_grad
        )
        queries_grad = grown * read_grad + nn(dots_grad, keys_low)
        values_grad = beta * right_u
        beta_grad = (
            jnp.sum(values * right_u, axis=1, keepdims=True)
            + grown * keys_right
            + jnp.sum(pair_grad, axis=1, keepdims=True)
        )
        cum_grad = (
            jnp.sum(spread_grad, axis=1, keepdims=True)
            + beta_grown * keys_right
            + grown * jnp.sum(queries * read_grad, axis=1, keepdims=True)
            - jnp.sum(tails_meet, axis=1, keepdims=True)
        )
        cum_row_grad = -jnp.sum(spread_grad, axis=0, keepdims=True)
        later = (row_at // STRETCH == col_at // STRETCH) & (row_at <= col_at)
        from_rows = jnp.sum(jnp.where(later, cum_row_grad, 0.0), axis=1, keepdims=True)
        later_low = later.astype(f32).astype(bf16)
        from_cols = exact_sums(later_low, jnp.broadcast_to(cum_grad, (PACK, LANES)))[:, 0:1]
        ends = []
        for sub in range(PER_PACK):
            part = slice(sub * STRETCH, (sub + 1) * STRETCH)
            end = last_grad[sub] + jnp.sum(tails_meet[part], axis=0, keepdims=True)
            ends.append(
                jnp.broadcast_to(jnp.sum(end, axis=1, keepdims=True), (STRETCH, 1))
            )
        decay_grad = from_rows + from_cols + jnp.concatenate(ends, axis=0)
        decay_sum = decay_sum + jnp.sum(decay_grad * decay, axis=0, keepdims=True)
        rate_grad = decay_grad * (decay_ref[0:1, :] * decay_lane) * sigmoid(shifted)
        rate_grad = rate_grad + beta_grad * (betas * (1.0 - betas)) * beta_lane
        rate_sum = rate_sum + jnp.sum(rate_grad, axis=0, keepdims=True)
        rgs[first : first + PACK, :] += rate_grad
        conv_out = conv_of(xs, conv_ref.at[0], cols_ref.at[0], first, PACK)
        gate, _, _, _, scale_q, scale_k = front(conv_out)
        raw_q_grad = scale_q * (
            queries_grad - queries * jnp.sum(queries * queries_grad, axis=1, keepdims=True)
        )
        raw_k_grad = scale_k * (
            keys_grad - keys * jnp.sum(keys * keys_grad, axis=1, keepdims=True)
        )
        active_grad = jnp.concatenate([raw_q_grad, raw_k_grad, values_grad], axis=1)
        ds[HALO + first : HALO + first + PACK, :] = active_grad * (
            gate * (1.0 + conv_out * (1.0 - gate))
        )
    taps = []
    for reach in range(CONV):
        grad_rows = ds[HALO : HALO + piece, :]
        if reach > 0:
            grad_rows = grad_rows * cols_ref[0, :, reach - 1 : reach]
        taps.append(
            jnp.sum(grad_rows * xs[HALO - reach : HALO - reach + piece, :], axis=0, keepdims=True)
        )
    cgrad_ref[0, 0] = jnp.concatenate(taps[::-1] + [jnp.zeros((8 - CONV, QKV), f32)], axis=0)
    total = ds[0 : HALO + piece, :] * conv_ref[0, CONV - 1 : CONV, :]
    for reach in range(1, CONV):
        masked = ds[HALO : HALO + piece, :] * cols_ref[0, :, reach - 1 : reach]
        xs[HALO : HALO + piece, :] = masked
        xs[0:HALO, :] = jnp.zeros((HALO, QKV), f32)
        xs[HALO + piece : 2 * HALO + piece, :] = jnp.zeros((HALO, QKV), f32)
        total = total + xs[reach : reach + HALO + piece, :] * conv_ref[
            0, CONV - 1 - reach : CONV - reach, :
        ]
    hgrad_ref[0, 0] = total[:HALO, :]
    ds[0:piece, :] = total[HALO:, :]
    for place in range(tp):
        at = pl.multiple_of(order_ref[1 + place] * rows, 8)
        xgrad_ref[place, 0] = ds[pl.ds(at, rows), :].astype(bf16)
        rgrad_ref[place, 0] = rgs[pl.ds(at, rows), :].astype(bf16)
    dgrad_ref[0, 0] = jnp.concatenate(
        [jnp.broadcast_to(decay_sum, (4, LANES)), jnp.broadcast_to(rate_sum, (4, LANES))], axis=0
    )


def shape_of(shape, dtype):
    return jax.ShapeDtypeStruct(shape, dtype)


def local_call(order, pre, halo, conv_w, decay_rows, cols, heads):
    tp, micro, rows, _ = pre.shape
    piece = tp * rows
    packs, blocks = piece // PACK, piece // STRETCH
    rate_at = heads * (QKV + DV) // LANES
    grid = pltpu.PrefetchScalarGridSpec(
        num_scalar_prefetch=1,
        grid=(micro,),
        in_specs=[
            pl.BlockSpec((tp, 1, rows, heads * QKV), lambda m, s: (0, m, 0, 0)),
            pl.BlockSpec((tp, 1, rows, LANES), lambda m, s: (0, m, 0, rate_at)),
            pl.BlockSpec((1, HALO, heads * QKV), lambda m, s: (m, 0, 0)),
            pl.BlockSpec((heads, 8, QKV), lambda m, s: (0, 0, 0)),
            pl.BlockSpec((8, LANES), lambda m, s: (0, 0)),
            pl.BlockSpec((1, piece, 8), lambda m, s: (m, 0, 0)),
        ],
        out_specs=[
            pl.BlockSpec((tp, 1, rows, heads * DV), lambda m, s: (0, m, 0, 0)),
            pl.BlockSpec((tp, 1, rows, heads * DK), lambda m, s: (0, m, 0, 0)),
            pl.BlockSpec((1, heads, blocks, DK, AUG), lambda m, s: (m, 0, 0, 0, 0)),
            pl.BlockSpec((1, heads, packs, PACK, PACK), lambda m, s: (m, 0, 0, 0, 0)),
            pl.BlockSpec((1, heads, blocks, DK, DK), lambda m, s: (m, 0, 0, 0, 0)),
            pl.BlockSpec((1, heads, DK, AUG), lambda m, s: (m, 0, 0, 0)),
        ],
        scratch_shapes=[
            pltpu.VMEM((heads, HALO + piece, QKV), f32),
            pltpu.VMEM((piece, LANES), f32),
            pltpu.VMEM((heads, piece, DV), f32),
            pltpu.VMEM((heads, piece, DK), f32),
        ],
    )
    return pl.pallas_call(
        local_kernel,
        grid_spec=grid,
        out_shape=[
            shape_of((tp, micro, rows, heads * DV), f32),
            shape_of((tp, micro, rows, heads * DK), bf16),
            shape_of((micro, heads, blocks, DK, AUG), bf16),
            shape_of((micro, heads, packs, PACK, PACK), bf16),
            shape_of((micro, heads, blocks, DK, DK), bf16),
            shape_of((micro, heads, DK, AUG), bf16),
        ],
        compiler_params=pltpu.CompilerParams(vmem_limit_bytes=VMEM_BYTES),
        name="delta_local",
    )(order, pre, pre, halo, conv_w, decay_rows, cols)


def finish_call(order, maps, out_local, reach, pre, gain, heads):
    ctx = maps.shape[0]
    tp, micro, rows, _ = out_local.shape
    gate_at = heads * QKV // DV
    grid = pltpu.PrefetchScalarGridSpec(
        num_scalar_prefetch=1,
        grid=(micro, heads),
        in_specs=[
            pl.BlockSpec((ctx, 1, 1, DK, AUG), lambda m, a, s: (0, m, a, 0, 0)),
            pl.BlockSpec((tp, 1, rows, DV), lambda m, a, s: (0, m, 0, a)),
            pl.BlockSpec((tp, 1, rows, DK), lambda m, a, s: (0, m, 0, a)),
            pl.BlockSpec((tp, 1, rows, DV), lambda m, a, s: (0, m, 0, gate_at + a)),
            pl.BlockSpec((8, DV), lambda m, a, s: (0, 0)),
        ],
        out_specs=[
            pl.BlockSpec((tp, 1, rows, DV), lambda m, a, s: (0, m, 0, a)),
            pl.BlockSpec((1, 1, DK, DV), lambda m, a, s: (m, a, 0, 0)),
        ],
    )
    return pl.pallas_call(
        finish_kernel,
        grid_spec=grid,
        out_shape=[
            shape_of((tp, micro, rows, heads * DV), bf16),
            shape_of((micro, heads, DK, DV), f32),
        ],
        compiler_params=pltpu.CompilerParams(vmem_limit_bytes=VMEM_BYTES),
        name="delta_finish",
    )(order, maps, out_local, reach, pre, gain)


def unfinish_call(entry, out_local, reach, pre, gain, grad, heads):
    tp, micro, rows, _ = out_local.shape
    gate_at = heads * QKV // DV
    return pl.pallas_call(
        unfinish_kernel,
        grid=(micro, heads),
        in_specs=[
            pl.BlockSpec((1, 1, DK, DV), lambda m, a: (m, a, 0, 0)),
            pl.BlockSpec((tp, 1, rows, DV), lambda m, a: (0, m, 0, a)),
            pl.BlockSpec((tp, 1, rows, DK), lambda m, a: (0, m, 0, a)),
            pl.BlockSpec((tp, 1, rows, DV), lambda m, a: (0, m, 0, gate_at + a)),
            pl.BlockSpec((8, DV), lambda m, a: (0, 0)),
            pl.BlockSpec((tp, 1, rows, DV), lambda m, a: (0, m, 0, a)),
        ],
        out_specs=[
            pl.BlockSpec((tp, 1, rows, DV), lambda m, a: (0, m, 0, a)),
            pl.BlockSpec((tp, 1, rows, DV), lambda m, a: (0, m, 0, a)),
            pl.BlockSpec((1, 1, 8, DV), lambda m, a: (m, a, 0, 0)),
            pl.BlockSpec((1, 1, DK, DV), lambda m, a: (m, a, 0, 0)),
        ],
        out_shape=[
            shape_of((tp, micro, rows, heads * DV), bf16),
            shape_of((tp, micro, rows, heads * DV), bf16),
            shape_of((micro, heads, 8, DV), f32),
            shape_of((micro, heads, DK, DV), bf16),
        ],
        compiler_params=pltpu.CompilerParams(vmem_limit_bytes=VMEM_BYTES),
        name="delta_unfinish",
    )(entry, out_local, reach, pre, gain, grad)


def adjoint_call(
    order, pre, halo, conv_w, decay_rows, cols, starts, inverse, transit, entry, maps, bases, ograd, heads
):
    tp, micro, rows, _ = pre.shape
    ctx = maps.shape[0]
    piece = tp * rows
    packs, blocks = piece // PACK, piece // STRETCH
    rate_at = heads * (QKV + DV) // LANES
    grid = pltpu.PrefetchScalarGridSpec(
        num_scalar_prefetch=1,
        grid=(micro, heads),
        in_specs=[
            pl.BlockSpec((tp, 1, rows, QKV), lambda m, a, s: (0, m, 0, a)),
            pl.BlockSpec((tp, 1, rows, LANES), lambda m, a, s: (0, m, 0, rate_at)),
            pl.BlockSpec((1, HALO, QKV), lambda m, a, s: (m, 0, a)),
            pl.BlockSpec((1, 8, QKV), lambda m, a, s: (a, 0, 0)),
            pl.BlockSpec((8, LANES), lambda m, a, s: (0, 0)),
            pl.BlockSpec((1, piece, 8), lambda m, a, s: (m, 0, 0)),
            pl.BlockSpec((1, 1, blocks, DK, AUG), lambda m, a, s: (m, a, 0, 0, 0)),
            pl.BlockSpec((1, 1, packs, PACK, PACK), lambda m, a, s: (m, a, 0, 0, 0)),
            pl.BlockSpec((1, 1, blocks, DK, DK), lambda m, a, s: (m, a, 0, 0, 0)),
            pl.BlockSpec((1, 1, DK, DV), lambda m, a, s: (m, a, 0, 0)),
            pl.BlockSpec((ctx, 1, 1, DK, DK), lambda m, a, s: (0, m, a, 0, DV // DK)),
            pl.BlockSpec((ctx, 1, 1, DK, DV), lambda m, a, s: (0, m, a, 0, 0)),
            pl.BlockSpec((tp, 1, rows, DV), lambda m, a, s: (0, m, 0, a)),
        ],
        out_specs=[
            pl.BlockSpec((tp, 1, rows, QKV), lambda m, a, s: (0, m, 0, a)),
            pl.BlockSpec((1, 1, HALO, QKV), lambda m, a, s: (m, a, 0, 0)),
            pl.BlockSpec((1, 1, 8, QKV), lambda m, a, s: (m, a, 0, 0)),
            pl.BlockSpec((tp, 1, rows, LANES), lambda m, a, s: (0, m, 0, 0)),
            pl.BlockSpec((1, 1, 8, LANES), lambda m, a, s: (m, a, 0, 0)),
        ],
        scratch_shapes=[
            pltpu.VMEM((2 * HALO + piece, QKV), f32),
            pltpu.VMEM((piece, LANES), f32),
            pltpu.VMEM((piece, DV), bf16),
            pltpu.VMEM((2 * HALO + piece, QKV), f32),
            pltpu.VMEM((piece, LANES), f32),
        ],
    )
    return pl.pallas_call(
        adjoint_kernel,
        grid_spec=grid,
        out_shape=[
            shape_of((tp, micro, rows, heads * QKV), bf16),
            shape_of((micro, heads, HALO, QKV), f32),
            shape_of((micro, heads, 8, QKV), f32),
            shape_of((tp, micro, rows, LANES), bf16),
            shape_of((micro, heads, 8, LANES), f32),
        ],
        compiler_params=pltpu.CompilerParams(vmem_limit_bytes=VMEM_BYTES),
        name="delta_adjoint",
    )(order, pre, pre, halo, conv_w, decay_rows, cols, starts, inverse, transit, entry, maps, bases, ograd)


def weights_kernel(uses, *refs):
    out_ref = refs[-1]
    start = 0
    for place, use in enumerate(uses):
        still_ref = refs[max(uses) + 1 + place]
        width = still_ref.shape[1]
        out_ref[:, start : start + width] = tn(refs[use][...], still_ref[...]).astype(bf16)
        start += width


def weights_call(moving, uses, still):
    rows = moving[0].shape[0]
    total = sum(part.shape[1] for part in still)
    block = 2 * LANES
    return pl.pallas_call(
        partial(weights_kernel, uses),
        grid=(D // block,),
        in_specs=[pl.BlockSpec((rows, block), lambda i: (0, i)) for _ in moving]
        + [pl.BlockSpec((rows, part.shape[1]), lambda i: (0, 0)) for part in still],
        out_specs=pl.BlockSpec((block, total), lambda i: (i, 0)),
        out_shape=shape_of((D, total), bf16),
        compiler_params=pltpu.CompilerParams(vmem_limit_bytes=VMEM_BYTES),
        cost_estimate=pl.CostEstimate(
            flops=2 * rows * D * total,
            bytes_accessed=2 * (rows * (len(moving) * D + total) + D * total),
            transcendentals=0,
        ),
        name="weight_grads",
    )(*moving, *still)


def rms_norm(values, gain_row):
    return (
        values * lax.rsqrt(jnp.mean(values * values, axis=-1, keepdims=True) + epsilon) * gain_row
    )


def rms_back(values, gain_row, grad):
    scale = lax.rsqrt(jnp.mean(values * values, axis=-1, keepdims=True) + epsilon)
    unit = values * scale
    gain_grad = jnp.sum(grad * unit, axis=0)
    inner = grad * gain_row
    return scale * (inner - unit * jnp.mean(inner * unit, axis=-1, keepdims=True)), gain_grad


def matmul(left, right):
    return jnp.dot(left, right, preferred_element_type=f32)


def matmul_nt(left, right):
    return lax.dot_general(left, right, (((1,), (1,)), ((), ())), preferred_element_type=f32)


def matmul_tn(left, right):
    return lax.dot_general(left, right, (((0,), (0,)), ((), ())), preferred_element_type=f32)


def flat(rows):
    return rows.reshape(-1, rows.shape[-1])


def token_layout(seq_lengths, positions):
    padded = (seq_lengths + STRETCH - 1) // STRETCH * STRETCH
    seq_ends = jnp.cumsum(padded)
    starts = seq_ends - padded
    inside = (positions[:, None] >= starts[None, :]) & (positions[:, None] < seq_ends[None, :])
    start_of = jnp.sum(jnp.where(inside, starts[None, :], 0), axis=1)
    length_of = jnp.sum(jnp.where(inside, seq_lengths[None, :], 0), axis=1)
    offset = positions - start_of
    return (offset, offset < length_of)


def last_place():
    tp = lax.axis_size("tp")
    place_of = jnp.asarray([turned(offset, "tp") for offset in range(tp)], jnp.int32)
    return place_of[lax.axis_index("tp") ^ (tp - 1)]


def layer_forward(hidden_in, w_in, gains, small, layout, layer_at, hooks):
    on_normed, on_maps, on_hidden = hooks
    conv_w, decay_rows, gain_row, widths = small
    order, valid = layout[1], layout[2]
    heads, ff = widths
    tp = lax.axis_size("tp")
    micro, rows, _ = hidden_in.shape
    hidden = flat(hidden_in)
    normed = rms_norm(hidden, gains[0]).astype(bf16)
    normed_all = gather_rows(normed)
    w_ff = on_normed(layer_at, normed_all)
    pre = matmul(flat(normed_all), w_in).reshape(tp, micro, rows, -1)
    tail = lax.dynamic_index_in_dim(pre, last_place(), 0, False)[:, rows - HALO :, : heads * QKV]
    halo = passed_along(tail, "ctx", 1)
    out_local, reach, starts, inverse, transit, piece_map = local_call(
        order, pre, halo, conv_w, decay_rows, layout[0], heads
    )
    maps = ring_gather(after(piece_map, w_ff))
    on_maps(layer_at, maps)
    gated, entry = finish_call(order, maps, out_local, reach, pre, gain_row, heads)
    gated = gated.reshape(tp, micro * rows, heads * DV)
    w_out = w_ff[:, 2 * ff : 2 * ff + heads * DV]

    def mixer_part(low, high):
        return matmul_nt(flat(gated[low:high]), w_out).reshape(high - low, micro * rows, D)

    middle = hidden + valid * scatter_rows(mixer_part, tp)
    normed_two = rms_norm(middle, gains[1]).astype(bf16)
    normed_two_all = flat(gather_rows(normed_two))
    gate_ff = matmul(normed_two_all, w_ff[:, :ff])
    up_ff = matmul(normed_two_all, w_ff[:, ff : 2 * ff])
    hidden_ff = (jax.nn.silu(gate_ff) * up_ff).astype(bf16).reshape(tp, micro * rows, ff)
    on_hidden(layer_at, hidden_ff)
    w_down = w_ff[:, 2 * ff + heads * DV : 3 * ff + heads * DV]

    def ff_part(low, high):
        return matmul_nt(flat(hidden_ff[low:high]), w_down).reshape(high - low, micro * rows, D)

    leaving = middle + valid * scatter_rows(ff_part, tp)
    saved = (
        hidden,
        normed_all,
        pre,
        halo,
        out_local,
        reach,
        starts,
        inverse,
        transit,
        maps,
        entry,
        gated,
        middle,
        normed_two_all,
        gate_ff,
        up_ff,
        hidden_ff,
    )
    return leaving.reshape(hidden_in.shape), saved


def layer_backward(grad_out, saved, weights, small, layout, before):
    (
        hidden,
        normed_all,
        pre,
        halo,
        out_local,
        reach,
        starts,
        inverse,
        transit,
        maps,
        entry,
        gated,
        middle,
        normed_two_all,
        gate_ff,
        up_ff,
        hidden_ff,
    ) = saved
    w_in, w_ff, gains = weights
    conv_w, decay_rows, gain_row, widths = small
    order, valid = layout[1], layout[2]
    heads, ff = widths
    tp = lax.axis_size("tp")
    micro, rows, _ = grad_out.shape
    grad = flat(grad_out)
    ff_grad = flat(gather_rows((valid * grad).astype(bf16)))
    w_down = w_ff[:, 2 * ff + heads * DV : 3 * ff + heads * DV]
    hidden_grad = matmul(ff_grad, w_down)
    open_at = jax.nn.sigmoid(gate_ff)
    gate_grad = (hidden_grad * up_ff * open_at * (1.0 + gate_ff * (1.0 - open_at))).astype(bf16)
    up_grad = (hidden_grad * gate_ff * open_at).astype(bf16)
    blocks_gate = gate_grad.reshape(tp, micro * rows, ff)
    blocks_up = up_grad.reshape(tp, micro * rows, ff)

    def two_part(low, high):
        part = matmul_nt(flat(blocks_gate[low:high]), w_ff[:, :ff]) + matmul_nt(
            flat(blocks_up[low:high]), w_ff[:, ff : 2 * ff]
        )
        return part.reshape(high - low, micro * rows, D)

    middle_part, gain_two = rms_back(middle, gains[1], scatter_rows(two_part, tp))
    middle_grad = grad + middle_part
    mixer_grad = flat(gather_rows((valid * middle_grad).astype(bf16)))
    w_out = w_ff[:, 2 * ff : 2 * ff + heads * DV]
    gated_grad = matmul(mixer_grad, w_out).reshape(tp, micro, rows, heads * DV)
    out_grad, gate_low, gain_grad, base = unfinish_call(
        entry, out_local, reach, pre, gain_row, gated_grad, heads
    )
    bases = ring_gather(after(base, *before))
    low_ff = weights_call(
        (normed_two_all, mixer_grad, ff_grad),
        (0, 0, 1, 2),
        (gate_grad, up_grad, flat(gated), flat(hidden_ff)),
    )
    low_ff = after(low_ff, bases)
    owned_ff = ring_scatter(low_ff)
    x_grad, halo_grad, conv_grad, rate_low, decay_grad = adjoint_call(
        order, pre, halo, conv_w, decay_rows, layout[0], starts, inverse, transit, entry, maps, bases, out_grad, heads
    )
    log_grad = jnp.sum(decay_grad[:, :, 0, 0], axis=0)
    bias_grad = jnp.stack([jnp.sum(decay_grad[:, at, 4, 2 * at]) for at in range(heads)])
    back_rows = passed_along(halo_grad, "ctx", -1)
    back_rows = jnp.transpose(back_rows, (0, 2, 1, 3)).reshape(1, micro, HALO, heads * QKV)
    at = last_place()
    zero = jnp.zeros((), jnp.int32)
    corner = (at, zero, zero + rows - HALO, zero)
    tail = lax.dynamic_slice(x_grad, corner, (1, micro, HALO, heads * QKV))
    tail = (tail.astype(f32) + back_rows).astype(bf16)
    x_grad = lax.dynamic_update_slice(x_grad, tail, corner)
    parts = [part.reshape(tp, micro * rows, -1) for part in (x_grad, gate_low, rate_low)]

    def one_part(low, high):
        total, start = None, 0
        for part in parts:
            width = part.shape[-1]
            term = matmul_nt(flat(part[low:high]), w_in[:, start : start + width])
            total = term if total is None else total + term
            start += width
        return total.reshape(high - low, micro * rows, D)

    hidden_part, gain_one = rms_back(hidden, gains[0], scatter_rows(one_part, tp))
    leaving = middle_grad + hidden_part
    low_in = weights_call((flat(normed_all),), (0, 0, 0), [flat(part) for part in parts])
    owned_in = ring_scatter(after(low_in, owned_ff))
    conv_grad = jnp.sum(conv_grad, axis=0)[:, :CONV]
    gain_grad = jnp.sum(gain_grad[:, :, 0], axis=(0, 1))
    small_grads = (conv_grad, log_grad, bias_grad, gain_grad, gain_one, gain_two)
    return leaving.reshape(grad_out.shape), owned_in, owned_ff, small_grads


def body(
    inputs,
    cotangent,
    lengths,
    norm_gain,
    w_qkv,
    w_gate,
    w_rates,
    conv_weight,
    decay_log,
    decay_bias,
    out_gain,
    w_out,
    w_gu,
    w_down,
):
    tp = lax.axis_size("tp")
    ctx = lax.axis_size("ctx")
    micro, shard_rows, _ = inputs.shape
    piece_rows = shard_rows * tp
    layers = w_qkv.shape[0]
    own = w_qkv.shape[1]
    heads = w_qkv.shape[2]
    ff = w_gu.shape[3]
    ctx_at = lax.axis_index("ctx")
    tp_at = lax.axis_index("tp")
    piece_pos = ctx_at * piece_rows + jnp.arange(piece_rows, dtype=jnp.int32)
    shard_pos = (ctx_at * tp + tp_at) * shard_rows + jnp.arange(shard_rows, dtype=jnp.int32)
    offset = jnp.stack([token_layout(lengths[m], piece_pos)[0] for m in range(micro)])
    valid = jnp.stack([token_layout(lengths[m], shard_pos)[1] for m in range(micro)])
    valid = valid.astype(f32).reshape(-1, 1)
    ring, places = ring_of(ctx), ring_places()
    order = [ctx_at] + [tp_at ^ turned(place, "tp") for place in range(tp)]
    order = jnp.stack([part.astype(jnp.int32) for part in order] + [jnp.int32(p) for p in places])
    marks = [(offset >= reach).astype(f32) for reach in (1, 2, 3, 1)]
    cols = jnp.stack(marks + [jnp.zeros_like(marks[0])] * 4, axis=-1)
    layout = (cols, order, valid)

    gains = in_order(gather_blocks(norm_gain, "ctx"), "ctx")
    gains = jnp.stack([gains[device] for device in ring])
    gains = jnp.transpose(gains, (1, 2, 0, 3)).reshape(layers, 2, D).astype(f32)
    in_width = heads * (QKV + DV + 2)
    in_spare = -in_width % LANES
    shards = []
    for layer_at in range(layers):
        shard_in = jnp.concatenate(
            [
                w_qkv[layer_at].reshape(own, -1),
                w_gate[layer_at].reshape(own, -1),
                w_rates[layer_at].reshape(own, -1),
                jnp.zeros((own, in_spare), bf16),
            ],
            axis=1,
        )
        shard_ff = jnp.concatenate(
            [
                w_gu[layer_at, 0],
                w_gu[layer_at, 1],
                w_out[layer_at].reshape(-1, own).T,
                w_down[layer_at].T,
            ],
            axis=1,
        )
        shards.append((shard_in, shard_ff))

    def gathered(shard, *before):
        return ring_gather(after(shard, *before), axis=0, tiled=True)

    weights_in = [gathered(shards[0][0])] + [None] * (layers - 1)
    weights_ff = [None] * layers

    def on_normed(layer_at, token):
        if layer_at == 0:
            weights_ff[0] = gathered(shards[0][1], weights_in[0], token)
        return weights_ff[layer_at]

    def on_maps(layer_at, token):
        if layer_at + 1 < layers:
            weights_in[layer_at + 1] = gathered(shards[layer_at + 1][0], token)

    def on_hidden(layer_at, token):
        if layer_at + 1 < layers:
            following = layer_at + 1
            weights_ff[following] = gathered(shards[following][1], weights_in[following], token)

    hooks = (on_normed, on_maps, on_hidden)
    smalls = []
    for layer_at in range(layers):
        conv_w = jnp.transpose(conv_weight[layer_at], (1, 0, 2))
        conv_w = jnp.concatenate([conv_w, jnp.zeros((heads, 8 - CONV, QKV), f32)], axis=1)
        gain_row = jnp.broadcast_to(out_gain[layer_at][None], (8, DV))
        scale, bias = -jnp.exp(decay_log[layer_at]), decay_bias[layer_at]
        pair = jnp.stack([jnp.stack([part, jnp.zeros_like(part)], axis=1) for part in (scale, bias)])
        decay_rows = jnp.pad(pair.reshape(2, -1), ((0, 6), (0, LANES - 2 * heads)))
        smalls.append(
            (conv_w, decay_rows, gain_row, (heads, ff))
        )

    hidden_now = blocks_moved(inputs.astype(f32), ring)
    saved_all = []
    for layer_at in range(layers):
        hidden_now, saved = layer_forward(
            hidden_now, weights_in[layer_at], gains[layer_at], smalls[layer_at], layout, layer_at, hooks
        )
        saved_all.append(saved)
    weights = list(zip(weights_in, weights_ff, gains))
    grad_now = blocks_moved(cotangent, ring)
    before = ()
    big = [None] * layers
    small = [None] * layers
    for layer_at in reversed(range(layers)):
        grad_now, owned_in, owned_ff, small_grads = layer_backward(
            grad_now, saved_all[layer_at], weights[layer_at], smalls[layer_at], layout, before
        )
        before = (owned_in,)
        big[layer_at] = (owned_in.astype(f32), owned_ff.astype(f32))
        small[layer_at] = small_grads

    head_parts = [jnp.stack([small[at][member] for at in range(layers)]) for member in range(3)]
    wide_parts = [jnp.stack([small[at][member] for at in range(layers)]) for member in range(3, 6)]
    sizes = [part.size for part in head_parts + wide_parts]
    head_size = sum(sizes[:3])
    packed = jnp.concatenate([part.reshape(-1) for part in head_parts + wide_parts])
    spare = -packed.size % (8 * LANES)
    packed = jnp.concatenate([packed, jnp.zeros((spare,), f32)]).reshape(-1, LANES)
    packed = sum_over(packed, "ctx").reshape(-1)
    wide = packed[head_size : sum(sizes)]
    wide_size = wide.size
    spare = -wide_size % (8 * LANES)
    wide = jnp.concatenate([wide, jnp.zeros((spare,), f32)]).reshape(-1, LANES)
    wide = sum_over(wide, "tp").reshape(-1)
    parts = []
    start = 0
    for part, size in zip(head_parts, sizes[:3]):
        parts.append(packed[start : start + size].reshape(part.shape))
        start += size
    start = 0
    for part, size in zip(wide_parts, sizes[3:]):
        parts.append(wide[start : start + size].reshape(part.shape))
        start += size
    conv_grad, log_grad, bias_grad, ogain_grad, gain_one, gain_two = parts
    conv_grad = jnp.transpose(conv_grad, (0, 2, 1, 3))
    norm_grad = jnp.stack([gain_one, gain_two], axis=1)
    own_place = jnp.asarray(places, jnp.int32)[ctx_at]
    norm_grad = lax.dynamic_slice_in_dim(norm_grad, own_place * own, own, 2)

    in_all = jnp.stack([big[at][0] for at in range(layers)])
    ff_all = jnp.stack([big[at][1] for at in range(layers)])
    qkv_end, gate_end = heads * QKV, heads * (QKV + DV)
    grad_qkv = in_all[..., :qkv_end].reshape(w_qkv.shape)
    grad_gate_w = in_all[..., qkv_end:gate_end].reshape(w_gate.shape)
    grad_rates = in_all[..., gate_end:in_width].reshape(w_rates.shape)
    grad_gu = jnp.stack([ff_all[..., :ff], ff_all[..., ff : 2 * ff]], axis=1)
    out_end = 2 * ff + heads * DV
    grad_out_w = jnp.swapaxes(ff_all[..., 2 * ff : out_end], 1, 2).reshape(w_out.shape)
    grad_down = jnp.swapaxes(ff_all[..., out_end:], 1, 2)
    return (
        blocks_moved(hidden_now, places),
        blocks_moved(grad_now, places),
        norm_grad,
        grad_qkv,
        grad_gate_w,
        grad_rates,
        conv_grad,
        log_grad,
        bias_grad,
        ogain_grad,
        grad_out_w,
        grad_gu,
        grad_down,
    )


def solution(mesh):
    placed = (
        P(None, ("ctx", "tp"), None),
        P(None, ("ctx", "tp"), None),
        P(),
        P(None, None, "ctx"),
        P(None, "ctx", "tp", None),
        P(None, "ctx", "tp", None),
        P(None, "ctx", "tp", None),
        P(None, None, "tp", None),
        P(None, "tp"),
        P(None, "tp"),
        P(),
        P(None, "tp", None, "ctx"),
        P(None, None, "ctx", "tp"),
        P(None, "tp", "ctx"),
    )
    return jax.shard_map(
        body,
        mesh=mesh,
        in_specs=placed,
        out_specs=(
            P(None, ("ctx", "tp"), None),
            P(None, ("ctx", "tp"), None),
            P(None, None, "ctx"),
            P(None, "ctx", "tp", None),
            P(None, "ctx", "tp", None),
            P(None, "ctx", "tp", None),
            P(None, None, "tp", None),
            P(None, "tp"),
            P(None, "tp"),
            P(),
            P(None, "tp", None, "ctx"),
            P(None, None, "ctx", "tp"),
            P(None, "tp", "ctx"),
        ),
        check_vma=False,
    )
```

```python
from functools import partial

import jax
import jax.numpy as jnp
from jax import lax
from jax.experimental import pallas as pl
from jax.experimental.pallas import tpu as pltpu
from jax.sharding import PartitionSpec as P

D = 1024
DK = 128
DV = 256
QKV = 512
AUG = DV + DK
CONV = 4
STRETCH = 64
PACK = 256
PER_PACK = PACK // STRETCH
LANES = 128
HALO = 8

epsilon = 1e-05
unit_eps = 1e-06
f32 = jnp.float32
bf16 = jnp.bfloat16
VMEM_BYTES = 56 * 1024 * 1024


def swap(value, axis, bit):
    count = lax.axis_size(axis)
    return lax.ppermute(value, axis, [(i, i ^ bit) for i in range(count)])


def bits_of(axis):
    count = lax.axis_size(axis)
    bits = []
    bit = count // 2
    while bit >= 1:
        bits.append(bit)
        bit //= 2
    return bits


def turned(place, axis):
    offset = 0
    for step, bit in enumerate(bits_of(axis)):
        if place >> step & 1:
            offset |= bit
    return offset


def gather_blocks(value, axis):
    blocks = value[None]
    for bit in bits_of(axis):
        blocks = jnp.concatenate([blocks, swap(blocks, axis, bit)], axis=0)
    return blocks


def in_order(blocks, axis):
    count = lax.axis_size(axis)
    me = lax.axis_index(axis)
    place_of = [turned(offset, axis) for offset in range(count)]
    place_of = jnp.asarray(place_of, jnp.int32)
    return jnp.stack(
        [
            lax.dynamic_index_in_dim(blocks, place_of[me ^ device], 0, False)
            for device in range(count)
        ]
    )


def to_relative(blocks, axis):
    me = lax.axis_index(axis)
    return jnp.stack(
        [
            lax.dynamic_index_in_dim(blocks, me ^ turned(place, axis), 0, False)
            for place in range(blocks.shape[0])
        ]
    )


def gather_rows(rows):
    return gather_blocks(rows, "tp")


def scatter_rows(product_of, count):
    half = count // 2
    kept = None
    for bit in reversed(bits_of("tp")):
        if kept is None:
            sent = product_of(half, count).astype(bf16)
            received = swap(sent, "tp", bit)
            kept = product_of(0, half) + received.astype(f32)
        else:
            received = swap(kept[half:].astype(bf16), "tp", bit)
            kept = kept[:half] + received.astype(f32)
        half //= 2
    return kept[0]


def sum_over(value, axis):
    for bit in bits_of(axis):
        value = value + swap(value, axis, bit)
    return value


def ring_of(count):
    if count % 4 != 0 or count < 8:
        return list(range(count))
    wide = count // 4
    ring = [row * wide for row in range(4)]
    for row in reversed(range(4)):
        columns = range(1, wide) if row % 2 == 1 else reversed(range(1, wide))
        ring += [row * wide + column for column in columns]
    return ring


def ring_gather(value, **options):
    ring = ring_of(lax.axis_size("ctx"))
    return lax.all_gather(value, "ctx", axis_index_groups=[ring], **options)


def ring_scatter(value):
    ring = ring_of(lax.axis_size("ctx"))
    return lax.psum_scatter(
        value, "ctx", scatter_dimension=0, tiled=True, axis_index_groups=[ring]
    )


def ring_places():
    ring = ring_of(lax.axis_size("ctx"))
    return [ring.index(device) for device in range(len(ring))]


def blocks_moved(value, source_of):
    parts = jnp.split(value, len(source_of), axis=-1)
    return jnp.concatenate([parts[source] for source in source_of], axis=-1)


def after(value, *others):
    return lax.optimization_barrier((value,) + others)[0]


def passed_along(value, axis, steps):
    count = lax.axis_size(axis)
    initial, last = (max(0, -steps), min(count, count - steps))
    return lax.ppermute(value, axis, [(source, source + steps) for source in range(initial, last)])


def dot(left, right, contract):
    return lax.dot_general(
        left.astype(bf16),
        right.astype(bf16),
        (contract, ((), ())),
        preferred_element_type=f32,
    )


def nn(left, right):
    return dot(left, right, ((1,), (0,)))


def nt(left, right):
    return dot(left, right, ((1,), (1,)))


def tn(left, right):
    return dot(left, right, ((0,), (0,)))


def split_right(product, left, right):
    high, low = halves(right)
    return product(left, high) + product(left, low)


def split_left(product, left, right):
    high, low = halves(left)
    return product(high, right) + product(low, right)


def halves(value):
    high = value.astype(bf16)
    return high, (value - high.astype(f32)).astype(bf16)


def nn_fine(left, right):
    left_hi, left_lo = left
    right_hi, right_lo = right
    return nn(left_hi, right_hi) + (nn(left_hi, right_lo) + nn(left_lo, right_hi))


def sigmoid(value):
    return 1.0 / (1.0 + jnp.exp(-value))


def index_grids():
    row_at = lax.broadcasted_iota(jnp.int32, (PACK, PACK), 0)
    col_at = lax.broadcasted_iota(jnp.int32, (PACK, PACK), 1)
    return row_at, col_at


def unit_lower_inverse(lower, row_at, col_at):
    eye = (row_at == col_at).astype(f32)
    small = jnp.where(row_at // 8 == col_at // 8, lower, 0.0)
    small_h = halves(small)
    power2 = nn_fine(small_h, small_h)
    power2_h = halves(power2)
    inverse = eye - small
    inverse = inverse + nn_fine(halves(inverse), power2_h)
    power4 = nn_fine(power2_h, power2_h)
    inverse = inverse + nn_fine(halves(inverse), halves(power4))
    size = 8
    while size < STRETCH:
        corner = jnp.where(
            (row_at // (2 * size) == col_at // (2 * size)) & (row_at // size != col_at // size),
            lower,
            0.0,
        )
        inverse_h = halves(inverse)
        inverse = inverse - nn_fine(inverse_h, halves(nn_fine(halves(corner), inverse_h)))
        size *= 2
    return inverse


def load_rates(order_ref, rate_ref, rs):
    tp, _, rows, _ = rate_ref.shape
    for place in range(tp):
        at = pl.multiple_of(order_ref[1 + place] * rows, 8)
        rs[pl.ds(at, rows), :] = rate_ref[place, 0]


def rate_parts(raw, decay_ref):
    shifted = raw + decay_ref[1:2, :]
    soft = jnp.maximum(shifted, 0.0) + jnp.log1p(jnp.exp(-jnp.abs(shifted)))
    return shifted, decay_ref[0:1, :] * soft, sigmoid(raw)


def exact_sums(pattern, values):
    high, low = halves(values)
    return nn(pattern, high) + nn(pattern, low)


def decay_terms(decays, row_at, col_at):
    same = row_at // STRETCH == col_at // STRETCH
    upto = (same & (row_at >= col_at)).astype(f32).astype(bf16)
    whole = same.astype(f32).astype(bf16)
    running = exact_sums(upto, decays)
    total = exact_sums(whole, decays)
    high, low = halves(decays[:, :8])
    running_rows = dot(high, upto, ((0,), (1,))) + dot(low, upto, ((0,), (1,)))
    return running, running_rows, total


def load_pieces(order_ref, x_ref, halo_ref, xs, head):
    tp, _, rows, _ = x_ref.shape
    lanes = pl.ds(head * QKV, QKV)
    xs[0:HALO, :] = halo_ref[0, :, lanes]
    for place in range(tp):
        at = pl.multiple_of(order_ref[1 + place] * rows + HALO, 8)
        xs[pl.ds(at, rows), :] = x_ref[place, 0, :, lanes]


def conv_of(xs, weights, cols, first, count):
    total = None
    for reach in range(CONV):
        rows = xs[HALO + first - reach : HALO + first - reach + count, :]
        if reach > 0:
            rows = rows * cols[first : first + count, reach - 1 : reach]
        term = rows * weights[CONV - 1 - reach : CONV - reach, :]
        total = term if total is None else total + term
    return total


def front(conv_out):
    gate = sigmoid(conv_out)
    active = conv_out * gate
    raw_q, raw_k, values = active[:, :DK], active[:, DK : 2 * DK], active[:, 2 * DK :]
    scale_q = lax.rsqrt(jnp.sum(raw_q * raw_q, axis=1, keepdims=True) + unit_eps)
    scale_k = lax.rsqrt(jnp.sum(raw_k * raw_k, axis=1, keepdims=True) + unit_eps)
    return gate, raw_q * scale_q, raw_k * scale_k, values, scale_q, scale_k


def pack_terms(queries, keys, running, running_row, row_at, col_at):
    inside = (row_at // STRETCH == col_at // STRETCH) & (row_at >= col_at)
    spread = running - running_row
    weight = jnp.where(inside, jnp.exp(jnp.where(inside, spread, 0.0)), 0.0)
    keys_low = keys.astype(bf16)
    key_dots = nt(keys_low, keys_low)
    scores = nt(queries, keys_low) * weight
    pair = jnp.where(row_at > col_at, key_dots * weight, 0.0)
    return weight, pair, scores


def local_kernel(
    order_ref,
    x_ref,
    rate_ref,
    halo_ref,
    conv_ref,
    decay_ref,
    cols_ref,
    out_ref,
    reach_ref,
    starts_ref,
    inverse_ref,
    transit_ref,
    map_ref,
    xs,
    rs,
    o_scr,
    r_scr,
):
    tp, _, rows, _ = x_ref.shape
    heads = conv_ref.shape[0]
    piece = tp * rows
    packs = piece // PACK
    blocks = piece // STRETCH
    row_at, col_at = index_grids()
    units = [(head, pack) for head in range(heads) for pack in range(packs)]
    held = {}
    shared = {}
    load_rates(order_ref, rate_ref, rs)
    for head in range(heads):
        load_pieces(order_ref, x_ref, halo_ref, xs.at[head], head)
    for pack in range(packs):
        _, decays, betas = rate_parts(rs[pack * PACK : (pack + 1) * PACK, :], decay_ref)
        running, running_rows, total = decay_terms(decays, row_at, col_at)
        shared[pack] = (
            running,
            running_rows,
            betas,
            jnp.exp(running),
            jnp.exp(total - running),
            jnp.exp(total),
        )
    for head, pack in units:
        first = pack * PACK
        conv_out = conv_of(xs.at[head], conv_ref.at[head], cols_ref.at[0], first, PACK)
        _, queries, keys, values, _, _ = front(conv_out)
        lane = 2 * head
        running, running_rows, betas, grown, tail, _ = shared[pack]
        beta = betas[:, lane + 1 : lane + 2]
        grown = grown[:, lane : lane + 1]
        weight, pair, scores = pack_terms(
            queries,
            keys,
            running[:, lane : lane + 1],
            running_rows[lane : lane + 1, :],
            row_at,
            col_at,
        )
        cols = (beta, grown, tail[:, lane : lane + 1], beta * grown)
        held[head, pack] = (queries, keys, values, cols, pair * beta, scores)
    inverses = {
        unit: unit_lower_inverse(held[unit][4], row_at, col_at).astype(bf16) for unit in units
    }
    solved = {}
    moves = {}
    for unit in units:
        head, pack = unit
        queries, keys, values, cols, _, scores = held[unit]
        inverse_ref[0, head, pack] = inverses[unit]
        solved_w = nn(inverses[unit], keys * cols[3])
        solved_u = nn(inverses[unit], values * cols[0])
        tails = (keys * cols[2]).astype(bf16)
        solved_w = solved_w.astype(bf16)
        solved_u_low = solved_u.astype(bf16)
        for sub in range(PER_PACK):
            part = slice(sub * STRETCH, (sub + 1) * STRETCH)
            block = pack * PER_PACK + sub
            transit = tn(tails[part], solved_w[part]).astype(bf16)
            transit_ref[0, head, block] = transit
            moves[head, block] = (transit, tn(tails[part], solved_u_low[part]))
        solved[unit] = (solved_w, solved_u)
    eye = (row_at[:DK, :DK] == col_at[:DK, :DK]).astype(f32)
    biases = [jnp.zeros((DK, DV), f32) for _ in range(heads)]
    maps = [eye for _ in range(heads)]
    for block in range(blocks):
        for head in range(heads):
            at = block % PER_PACK * STRETCH
            retain = shared[block // PER_PACK][5][at : at + 1, 2 * head : 2 * head + 1]
            keep = cols_ref[0, block * STRETCH : block * STRETCH + 1, 3:4]
            bias = biases[head] * keep
            whole = maps[head] * keep
            low = jnp.concatenate([bias, whole], axis=1).astype(bf16)
            starts_ref[0, head, block] = low
            transit, fresh = moves[head, block]
            moved = nn(transit, low)
            biases[head] = bias * retain - moved[:, :DV] + fresh
            maps[head] = whole * retain - moved[:, DV:]
    for head in range(heads):
        map_ref[0, head, :, :DV] = biases[head].astype(bf16)
        map_ref[0, head, :, DV:] = maps[head].astype(bf16)
    for unit in units:
        head, pack = unit
        queries, keys, values, cols, _, scores = held[unit]
        solved_w, solved_u = solved[unit]
        reading = (queries * cols[1]).astype(bf16)
        carried, recalled = [], []
        for sub in range(PER_PACK):
            part = slice(sub * STRETCH, (sub + 1) * STRETCH)
            start = starts_ref[0, head, pack * PER_PACK + sub]
            both = nn(jnp.concatenate([reading[part], solved_w[part]], axis=0), start)
            carried.append(both[:STRETCH])
            recalled.append(both[STRETCH:])
        carried = jnp.concatenate(carried, axis=0)
        recalled = jnp.concatenate(recalled, axis=0)
        low_scores = scores.astype(bf16)
        first = pack * PACK
        o_scr[head, first : first + PACK, :] = carried[:, :DV] + nn(
            low_scores, solved_u - recalled[:, :DV]
        )
        r_scr[head, first : first + PACK, :] = carried[:, DV:] - nn(low_scores, recalled[:, DV:])
    for place in range(tp):
        at = pl.multiple_of(order_ref[1 + place] * rows, 8)
        for head in range(heads):
            out_ref[place, 0, :, head * DV : (head + 1) * DV] = o_scr[head, pl.ds(at, rows), :]
            reach_ref[place, 0, :, head * DK : (head + 1) * DK] = r_scr[
                head, pl.ds(at, rows), :
            ].astype(bf16)


def finish_kernel(order_ref, maps_ref, out_ref, reach_ref, gate_ref, gain_ref, gated_ref, entry_ref):
    tp = out_ref.shape[0]

    def one(step, entry):
        whole = maps_ref[order_ref[1 + tp + step], 0, 0]
        return whole[:, :DV].astype(f32) + nn(whole[:, DV:], entry)

    entry = lax.fori_loop(0, order_ref[0], one, jnp.zeros((DK, DV), f32))
    entry_ref[0, 0] = entry
    entry_low = entry.astype(bf16)
    for place in range(tp):
        outputs = out_ref[place, 0] + nn(reach_ref[place, 0], entry_low)
        scale = lax.rsqrt(jnp.mean(outputs * outputs, axis=1, keepdims=True) + epsilon)
        gate = gate_ref[place, 0]
        gated = outputs * scale * gain_ref[0:1, :] * (gate * sigmoid(gate))
        gated_ref[place, 0] = gated.astype(bf16)


def unfinish_kernel(
    entry_ref, out_ref, reach_ref, gate_ref, gain_ref, grad_ref, ograd_ref, zgrad_ref, ggrad_ref, base_ref
):
    tp = out_ref.shape[0]
    entry_low = entry_ref[0, 0].astype(bf16)
    gain = gain_ref[0:1, :]
    base = jnp.zeros((DK, DV), f32)
    gain_grad = jnp.zeros((1, DV), f32)
    for place in range(tp):
        reach = reach_ref[place, 0]
        outputs = out_ref[place, 0] + nn(reach, entry_low)
        scale = lax.rsqrt(jnp.mean(outputs * outputs, axis=1, keepdims=True) + epsilon)
        unit = outputs * scale
        gate = gate_ref[place, 0]
        open_at = sigmoid(gate)
        grad = grad_ref[place, 0]
        normed_grad = grad * (gate * open_at)
        gate_grad = grad * (unit * gain) * (open_at * (1.0 + gate * (1.0 - open_at)))
        zgrad_ref[place, 0] = gate_grad.astype(bf16)
        gain_grad = gain_grad + jnp.sum(normed_grad * unit, axis=0, keepdims=True)
        inner = normed_grad * gain
        out_grad = scale * (inner - unit * jnp.mean(inner * unit, axis=1, keepdims=True))
        ograd_ref[place, 0] = out_grad
        base = base + split_right(tn, reach, out_grad)
    ggrad_ref[0, 0] = jnp.broadcast_to(gain_grad, (8, DV))
    base_ref[0, 0] = base.astype(bf16)


def adjoint_kernel(
    order_ref,
    x_ref,
    rate_ref,
    halo_ref,
    conv_ref,
    decay_ref,
    cols_ref,
    starts_ref,
    inverse_ref,
    transit_ref,
    entry_ref,
    maps_ref,
    bases_ref,
    ograd_ref,
    xgrad_ref,
    hgrad_ref,
    cgrad_ref,
    rgrad_ref,
    dgrad_ref,
    xs,
    rs,
    gs,
    ds,
    rgs,
):
    tp, _, rows, _ = x_ref.shape
    piece = tp * rows
    packs = piece // PACK
    blocks = piece // STRETCH
    ctx = maps_ref.shape[0]
    row_at, col_at = index_grids()
    head_at = pl.program_id(1)
    load_pieces(order_ref, x_ref, halo_ref, xs, 0)
    load_rates(order_ref, rate_ref, rs)
    lanes = lax.broadcasted_iota(jnp.int32, (PACK, LANES), 1)
    decay_lane = (lanes == 2 * head_at).astype(f32)
    beta_lane = (lanes == 2 * head_at + 1).astype(f32)

    @pl.when(head_at == 0)
    def _():
        rgs[...] = jnp.zeros_like(rgs)

    for place in range(tp):
        at = pl.multiple_of(order_ref[1 + place] * rows, 16)
        gs[pl.ds(at, rows), :] = ograd_ref[place, 0]

    def one(step, grad):
        source = order_ref[1 + tp + ctx - 1 - step]
        return bases_ref[source, 0, 0].astype(f32) + tn(maps_ref[source, 0, 0], grad)

    after = lax.fori_loop(0, ctx - 1 - order_ref[0], one, jnp.zeros((DK, DV), f32))
    entry_low = entry_ref[0, 0].astype(bf16)
    held = {}
    starts = {}
    turns = {}
    retains = {}
    decay_sum = jnp.zeros((1, 1), f32)
    rate_sum = jnp.zeros((1, LANES), f32)
    for pack in range(packs):
        first = pack * PACK
        conv_out = conv_of(xs, conv_ref.at[0], cols_ref.at[0], first, PACK)
        _, queries, keys, values, _, _ = front(conv_out)
        shifted, decays, betas = rate_parts(rs[first : first + PACK, :], decay_ref)
        decay = jnp.sum(decays * decay_lane, axis=1, keepdims=True)
        beta = jnp.sum(betas * beta_lane, axis=1, keepdims=True)
        running, running_rows, total = decay_terms(
            jnp.broadcast_to(decay, (PACK, LANES)), row_at, col_at
        )
        retains[pack] = jnp.exp(total)
        grown = jnp.exp(running)[:, 0:1]
        cols = (beta, grown, jnp.exp(total - running)[:, 0:1], beta * grown)
        weight, pair, scores = pack_terms(
            queries, keys, running[:, 0:1], running_rows[0:1, :], row_at, col_at
        )
        inverse = inverse_ref[0, 0, pack]
        solved_w = nn(inverse, keys * cols[3]).astype(bf16)
        solved_u = nn(inverse, values * cols[0])
        out_grad = gs[first : first + PACK, :]
        through = split_right(tn, scores, out_grad)
        through_low = through.astype(bf16)
        reading = (queries * cols[1]).astype(bf16)
        fresh = []
        for sub in range(PER_PACK):
            part = slice(sub * STRETCH, (sub + 1) * STRETCH)
            block = pack * PER_PACK + sub
            start = starts_ref[0, 0, block]
            start = start[:, :DV].astype(f32) + nn(start[:, DV:], entry_low)
            starts[block] = start
            fresh.append(solved_u[part] - nn(solved_w[part], start))
            turns[block] = split_right(tn, reading[part], out_grad[part]) - tn(solved_w[part], through_low[part])
        held[pack] = (
            queries,
            keys,
            values,
            cols,
            weight,
            pair,
            scores,
            inverse,
            solved_w,
            solved_u,
            out_grad,
            through,
            jnp.concatenate(fresh, axis=0),
            shifted,
            decay,
            betas,
        )
    grads = {}
    grad = after
    for block in reversed(range(blocks)):
        grads[block] = grad
        at = block % PER_PACK * STRETCH
        grad = grad * retains[block // PER_PACK][at : at + 1, 0:1]
        grad = grad - tn(transit_ref[0, 0, block], grads[block]) + turns[block]
        grad = grad * cols_ref[0, block * STRETCH : block * STRETCH + 1, 3:4]
    ds[0:HALO, :] = jnp.zeros((HALO, QKV), f32)
    ds[HALO + piece : 2 * HALO + piece, :] = jnp.zeros((HALO, QKV), f32)
    for pack in range(packs):
        first = pack * PACK
        (
            queries,
            keys,
            values,
            cols,
            weight,
            pair,
            scores,
            inverse,
            solved_w,
            solved_u,
            out_grad,
            through,
            fresh,
            shifted,
            decay,
            betas,
        ) = held[pack]
        beta, grown, tail, beta_grown = cols
        tails = keys * tail
        tails_low = tails.astype(bf16)
        fresh_low = fresh.astype(bf16)
        fresh_grad, read_grad, solved_w_grad, tails_grad, last_grad = [], [], [], [], []
        for sub in range(PER_PACK):
            part = slice(sub * STRETCH, (sub + 1) * STRETCH)
            block = pack * PER_PACK + sub
            grad_now = grads[block]
            grad_low = grad_now.astype(bf16)
            now = through[part] + nn(tails_low[part], grad_low)
            fresh_grad.append(now)
            both = split_left(nt, jnp.concatenate([out_grad[part], now], axis=0), starts[block])
            read_grad.append(both[:STRETCH])
            solved_w_grad.append(-both[STRETCH:])
            tails_grad.append(nt(fresh_low[part], grad_low))
            retain = retains[pack][sub * STRETCH : sub * STRETCH + 1, 0:1]
            meet = starts[block] * grad_now
            last_grad.append(
                retain * jnp.sum(meet[:, :DK] + meet[:, DK:], axis=0, keepdims=True)
            )
        fresh_grad = jnp.concatenate(fresh_grad, axis=0)
        read_grad = jnp.concatenate(read_grad, axis=0)
        solved_w_grad = jnp.concatenate(solved_w_grad, axis=0)
        tails_grad = jnp.concatenate(tails_grad, axis=0)
        score_grad = split_left(nt, out_grad, fresh_low)
        dots_grad = (score_grad * weight).astype(bf16)
        right_grad = tn(inverse, jnp.concatenate([fresh_grad, solved_w_grad], axis=1))
        right_u, right_w = right_grad[:, :DV], right_grad[:, DV:]
        lower_grad = -(nt(right_u, solved_u) + nt(right_w, solved_w))
        lower_grad = jnp.where(row_at > col_at, lower_grad, 0.0)
        pair_grad = lower_grad * pair
        key_dots_grad = (lower_grad * weight * beta).astype(bf16)
        spread_grad = pair_grad * beta + score_grad * scores
        keys_low = keys.astype(bf16)
        queries_low = queries.astype(bf16)
        keys_right = jnp.sum(keys * right_w, axis=1, keepdims=True)
        tails_meet = tails * tails_grad
        keys_grad = (
            beta_grown * right_w
            + nn(key_dots_grad, keys_low)
            + tn(key_dots_grad, keys_low)
            + tn(dots_grad, queries_low)
            + tail * tails_grad
        )
        queries_grad = grown * read_grad + nn(dots_grad, keys_low)
        values_grad = beta * right_u
        beta_grad = (
            jnp.sum(values * right_u, axis=1, keepdims=True)
            + grown * keys_right
            + jnp.sum(pair_grad, axis=1, keepdims=True)
        )
        cum_grad = (
            jnp.sum(spread_grad, axis=1, keepdims=True)
            + beta_grown * keys_right
            + grown * jnp.sum(queries * read_grad, axis=1, keepdims=True)
            - jnp.sum(tails_meet, axis=1, keepdims=True)
        )
        cum_row_grad = -jnp.sum(spread_grad, axis=0, keepdims=True)
        later = (row_at // STRETCH == col_at // STRETCH) & (row_at <= col_at)
        from_rows = jnp.sum(jnp.where(later, cum_row_grad, 0.0), axis=1, keepdims=True)
        later_low = later.astype(f32).astype(bf16)
        from_cols = exact_sums(later_low, jnp.broadcast_to(cum_grad, (PACK, LANES)))[:, 0:1]
        ends = []
        for sub in range(PER_PACK):
            part = slice(sub * STRETCH, (sub + 1) * STRETCH)
            end = last_grad[sub] + jnp.sum(tails_meet[part], axis=0, keepdims=True)
            ends.append(
                jnp.broadcast_to(jnp.sum(end, axis=1, keepdims=True), (STRETCH, 1))
            )
        decay_grad = from_rows + from_cols + jnp.concatenate(ends, axis=0)
        decay_sum = decay_sum + jnp.sum(decay_grad * decay, axis=0, keepdims=True)
        rate_grad = decay_grad * (decay_ref[0:1, :] * decay_lane) * sigmoid(shifted)
        rate_grad = rate_grad + beta_grad * (betas * (1.0 - betas)) * beta_lane
        rate_sum = rate_sum + jnp.sum(rate_grad, axis=0, keepdims=True)
        rgs[first : first + PACK, :] += rate_grad
        conv_out = conv_of(xs, conv_ref.at[0], cols_ref.at[0], first, PACK)
        gate, _, _, _, scale_q, scale_k = front(conv_out)
        raw_q_grad = scale_q * (
            queries_grad - queries * jnp.sum(queries * queries_grad, axis=1, keepdims=True)
        )
        raw_k_grad = scale_k * (
            keys_grad - keys * jnp.sum(keys * keys_grad, axis=1, keepdims=True)
        )
        active_grad = jnp.concatenate([raw_q_grad, raw_k_grad, values_grad], axis=1)
        ds[HALO + first : HALO + first + PACK, :] = active_grad * (
            gate * (1.0 + conv_out * (1.0 - gate))
        )
    taps = []
    for reach in range(CONV):
        grad_rows = ds[HALO : HALO + piece, :]
        if reach > 0:
            grad_rows = grad_rows * cols_ref[0, :, reach - 1 : reach]
        taps.append(
            jnp.sum(grad_rows * xs[HALO - reach : HALO - reach + piece, :], axis=0, keepdims=True)
        )
    cgrad_ref[0, 0] = jnp.concatenate(taps[::-1] + [jnp.zeros((8 - CONV, QKV), f32)], axis=0)
    total = ds[0 : HALO + piece, :] * conv_ref[0, CONV - 1 : CONV, :]
    for reach in range(1, CONV):
        masked = ds[HALO : HALO + piece, :] * cols_ref[0, :, reach - 1 : reach]
        xs[HALO : HALO + piece, :] = masked
        xs[0:HALO, :] = jnp.zeros((HALO, QKV), f32)
        xs[HALO + piece : 2 * HALO + piece, :] = jnp.zeros((HALO, QKV), f32)
        total = total + xs[reach : reach + HALO + piece, :] * conv_ref[
            0, CONV - 1 - reach : CONV - reach, :
        ]
    hgrad_ref[0, 0] = total[:HALO, :]
    ds[0:piece, :] = total[HALO:, :]
    for place in range(tp):
        at = pl.multiple_of(order_ref[1 + place] * rows, 8)
        xgrad_ref[place, 0] = ds[pl.ds(at, rows), :].astype(bf16)
        rgrad_ref[place, 0] = rgs[pl.ds(at, rows), :].astype(bf16)
    dgrad_ref[0, 0] = jnp.concatenate(
        [jnp.broadcast_to(decay_sum, (4, LANES)), jnp.broadcast_to(rate_sum, (4, LANES))], axis=0
    )


def shape_of(shape, dtype):
    return jax.ShapeDtypeStruct(shape, dtype)


def local_call(order, pre, halo, conv_w, decay_rows, cols, heads):
    tp, micro, rows, _ = pre.shape
    piece = tp * rows
    packs, blocks = piece // PACK, piece // STRETCH
    rate_at = heads * (QKV + DV) // LANES
    grid = pltpu.PrefetchScalarGridSpec(
        num_scalar_prefetch=1,
        grid=(micro,),
        in_specs=[
            pl.BlockSpec((tp, 1, rows, heads * QKV), lambda m, s: (0, m, 0, 0)),
            pl.BlockSpec((tp, 1, rows, LANES), lambda m, s: (0, m, 0, rate_at)),
            pl.BlockSpec((1, HALO, heads * QKV), lambda m, s: (m, 0, 0)),
            pl.BlockSpec((heads, 8, QKV), lambda m, s: (0, 0, 0)),
            pl.BlockSpec((8, LANES), lambda m, s: (0, 0)),
            pl.BlockSpec((1, piece, 8), lambda m, s: (m, 0, 0)),
        ],
        out_specs=[
            pl.BlockSpec((tp, 1, rows, heads * DV), lambda m, s: (0, m, 0, 0)),
            pl.BlockSpec((tp, 1, rows, heads * DK), lambda m, s: (0, m, 0, 0)),
            pl.BlockSpec((1, heads, blocks, DK, AUG), lambda m, s: (m, 0, 0, 0, 0)),
            pl.BlockSpec((1, heads, packs, PACK, PACK), lambda m, s: (m, 0, 0, 0, 0)),
            pl.BlockSpec((1, heads, blocks, DK, DK), lambda m, s: (m, 0, 0, 0, 0)),
            pl.BlockSpec((1, heads, DK, AUG), lambda m, s: (m, 0, 0, 0)),
        ],
        scratch_shapes=[
            pltpu.VMEM((heads, HALO + piece, QKV), f32),
            pltpu.VMEM((piece, LANES), f32),
            pltpu.VMEM((heads, piece, DV), f32),
            pltpu.VMEM((heads, piece, DK), f32),
        ],
    )
    return pl.pallas_call(
        local_kernel,
        grid_spec=grid,
        out_shape=[
            shape_of((tp, micro, rows, heads * DV), f32),
            shape_of((tp, micro, rows, heads * DK), bf16),
            shape_of((micro, heads, blocks, DK, AUG), bf16),
            shape_of((micro, heads, packs, PACK, PACK), bf16),
            shape_of((micro, heads, blocks, DK, DK), bf16),
            shape_of((micro, heads, DK, AUG), bf16),
        ],
        compiler_params=pltpu.CompilerParams(vmem_limit_bytes=VMEM_BYTES),
        name="delta_local",
    )(order, pre, pre, halo, conv_w, decay_rows, cols)


def finish_call(order, maps, out_local, reach, pre, gain, heads):
    ctx = maps.shape[0]
    tp, micro, rows, _ = out_local.shape
    gate_at = heads * QKV // DV
    grid = pltpu.PrefetchScalarGridSpec(
        num_scalar_prefetch=1,
        grid=(micro, heads),
        in_specs=[
            pl.BlockSpec((ctx, 1, 1, DK, AUG), lambda m, a, s: (0, m, a, 0, 0)),
            pl.BlockSpec((tp, 1, rows, DV), lambda m, a, s: (0, m, 0, a)),
            pl.BlockSpec((tp, 1, rows, DK), lambda m, a, s: (0, m, 0, a)),
            pl.BlockSpec((tp, 1, rows, DV), lambda m, a, s: (0, m, 0, gate_at + a)),
            pl.BlockSpec((8, DV), lambda m, a, s: (0, 0)),
        ],
        out_specs=[
            pl.BlockSpec((tp, 1, rows, DV), lambda m, a, s: (0, m, 0, a)),
            pl.BlockSpec((1, 1, DK, DV), lambda m, a, s: (m, a, 0, 0)),
        ],
    )
    return pl.pallas_call(
        finish_kernel,
        grid_spec=grid,
        out_shape=[
            shape_of((tp, micro, rows, heads * DV), bf16),
            shape_of((micro, heads, DK, DV), f32),
        ],
        compiler_params=pltpu.CompilerParams(vmem_limit_bytes=VMEM_BYTES),
        name="delta_finish",
    )(order, maps, out_local, reach, pre, gain)


def unfinish_call(entry, out_local, reach, pre, gain, grad, heads):
    tp, micro, rows, _ = out_local.shape
    gate_at = heads * QKV // DV
    return pl.pallas_call(
        unfinish_kernel,
        grid=(micro, heads),
        in_specs=[
            pl.BlockSpec((1, 1, DK, DV), lambda m, a: (m, a, 0, 0)),
            pl.BlockSpec((tp, 1, rows, DV), lambda m, a: (0, m, 0, a)),
            pl.BlockSpec((tp, 1, rows, DK), lambda m, a: (0, m, 0, a)),
            pl.BlockSpec((tp, 1, rows, DV), lambda m, a: (0, m, 0, gate_at + a)),
            pl.BlockSpec((8, DV), lambda m, a: (0, 0)),
            pl.BlockSpec((tp, 1, rows, DV), lambda m, a: (0, m, 0, a)),
        ],
        out_specs=[
            pl.BlockSpec((tp, 1, rows, DV), lambda m, a: (0, m, 0, a)),
            pl.BlockSpec((tp, 1, rows, DV), lambda m, a: (0, m, 0, a)),
            pl.BlockSpec((1, 1, 8, DV), lambda m, a: (m, a, 0, 0)),
            pl.BlockSpec((1, 1, DK, DV), lambda m, a: (m, a, 0, 0)),
        ],
        out_shape=[
            shape_of((tp, micro, rows, heads * DV), f32),
            shape_of((tp, micro, rows, heads * DV), bf16),
            shape_of((micro, heads, 8, DV), f32),
            shape_of((micro, heads, DK, DV), bf16),
        ],
        compiler_params=pltpu.CompilerParams(vmem_limit_bytes=VMEM_BYTES),
        name="delta_unfinish",
    )(entry, out_local, reach, pre, gain, grad)


def adjoint_call(
    order, pre, halo, conv_w, decay_rows, cols, starts, inverse, transit, entry, maps, bases, ograd, heads
):
    tp, micro, rows, _ = pre.shape
    ctx = maps.shape[0]
    piece = tp * rows
    packs, blocks = piece // PACK, piece // STRETCH
    rate_at = heads * (QKV + DV) // LANES
    grid = pltpu.PrefetchScalarGridSpec(
        num_scalar_prefetch=1,
        grid=(micro, heads),
        in_specs=[
            pl.BlockSpec((tp, 1, rows, QKV), lambda m, a, s: (0, m, 0, a)),
            pl.BlockSpec((tp, 1, rows, LANES), lambda m, a, s: (0, m, 0, rate_at)),
            pl.BlockSpec((1, HALO, QKV), lambda m, a, s: (m, 0, a)),
            pl.BlockSpec((1, 8, QKV), lambda m, a, s: (a, 0, 0)),
            pl.BlockSpec((8, LANES), lambda m, a, s: (0, 0)),
            pl.BlockSpec((1, piece, 8), lambda m, a, s: (m, 0, 0)),
            pl.BlockSpec((1, 1, blocks, DK, AUG), lambda m, a, s: (m, a, 0, 0, 0)),
            pl.BlockSpec((1, 1, packs, PACK, PACK), lambda m, a, s: (m, a, 0, 0, 0)),
            pl.BlockSpec((1, 1, blocks, DK, DK), lambda m, a, s: (m, a, 0, 0, 0)),
            pl.BlockSpec((1, 1, DK, DV), lambda m, a, s: (m, a, 0, 0)),
            pl.BlockSpec((ctx, 1, 1, DK, DK), lambda m, a, s: (0, m, a, 0, DV // DK)),
            pl.BlockSpec((ctx, 1, 1, DK, DV), lambda m, a, s: (0, m, a, 0, 0)),
            pl.BlockSpec((tp, 1, rows, DV), lambda m, a, s: (0, m, 0, a)),
        ],
        out_specs=[
            pl.BlockSpec((tp, 1, rows, QKV), lambda m, a, s: (0, m, 0, a)),
            pl.BlockSpec((1, 1, HALO, QKV), lambda m, a, s: (m, a, 0, 0)),
            pl.BlockSpec((1, 1, 8, QKV), lambda m, a, s: (m, a, 0, 0)),
            pl.BlockSpec((tp, 1, rows, LANES), lambda m, a, s: (0, m, 0, 0)),
            pl.BlockSpec((1, 1, 8, LANES), lambda m, a, s: (m, a, 0, 0)),
        ],
        scratch_shapes=[
            pltpu.VMEM((2 * HALO + piece, QKV), f32),
            pltpu.VMEM((piece, LANES), f32),
            pltpu.VMEM((piece, DV), f32),
            pltpu.VMEM((2 * HALO + piece, QKV), f32),
            pltpu.VMEM((piece, LANES), f32),
        ],
    )
    return pl.pallas_call(
        adjoint_kernel,
        grid_spec=grid,
        out_shape=[
            shape_of((tp, micro, rows, heads * QKV), bf16),
            shape_of((micro, heads, HALO, QKV), f32),
            shape_of((micro, heads, 8, QKV), f32),
            shape_of((tp, micro, rows, LANES), bf16),
            shape_of((micro, heads, 8, LANES), f32),
        ],
        compiler_params=pltpu.CompilerParams(vmem_limit_bytes=VMEM_BYTES),
        name="delta_adjoint",
    )(order, pre, pre, halo, conv_w, decay_rows, cols, starts, inverse, transit, entry, maps, bases, ograd)


def weights_kernel(uses, *refs):
    out_ref = refs[-1]
    start = 0
    for place, use in enumerate(uses):
        still_ref = refs[max(uses) + 1 + place]
        width = still_ref.shape[1]
        out_ref[:, start : start + width] = tn(refs[use][...], still_ref[...]).astype(bf16)
        start += width


def weights_call(moving, uses, still):
    rows = moving[0].shape[0]
    total = sum(part.shape[1] for part in still)
    block = 2 * LANES
    return pl.pallas_call(
        partial(weights_kernel, uses),
        grid=(D // block,),
        in_specs=[pl.BlockSpec((rows, block), lambda i: (0, i)) for _ in moving]
        + [pl.BlockSpec((rows, part.shape[1]), lambda i: (0, 0)) for part in still],
        out_specs=pl.BlockSpec((block, total), lambda i: (i, 0)),
        out_shape=shape_of((D, total), bf16),
        compiler_params=pltpu.CompilerParams(vmem_limit_bytes=VMEM_BYTES),
        cost_estimate=pl.CostEstimate(
            flops=2 * rows * D * total,
            bytes_accessed=2 * (rows * (len(moving) * D + total) + D * total),
            transcendentals=0,
        ),
        name="weight_grads",
    )(*moving, *still)


def rms_norm(values, gain_row):
    return (
        values * lax.rsqrt(jnp.mean(values * values, axis=-1, keepdims=True) + epsilon) * gain_row
    )


def rms_back(values, gain_row, grad):
    scale = lax.rsqrt(jnp.mean(values * values, axis=-1, keepdims=True) + epsilon)
    unit = values * scale
    gain_grad = jnp.sum(grad * unit, axis=0)
    inner = grad * gain_row
    return scale * (inner - unit * jnp.mean(inner * unit, axis=-1, keepdims=True)), gain_grad


def matmul(left, right):
    return jnp.dot(left, right, preferred_element_type=f32)


def matmul_nt(left, right):
    return lax.dot_general(left, right, (((1,), (1,)), ((), ())), preferred_element_type=f32)


def matmul_tn(left, right):
    return lax.dot_general(left, right, (((0,), (0,)), ((), ())), preferred_element_type=f32)


def flat(rows):
    return rows.reshape(-1, rows.shape[-1])


def token_layout(seq_lengths, positions):
    padded = (seq_lengths + STRETCH - 1) // STRETCH * STRETCH
    seq_ends = jnp.cumsum(padded)
    starts = seq_ends - padded
    inside = (positions[:, None] >= starts[None, :]) & (positions[:, None] < seq_ends[None, :])
    start_of = jnp.sum(jnp.where(inside, starts[None, :], 0), axis=1)
    length_of = jnp.sum(jnp.where(inside, seq_lengths[None, :], 0), axis=1)
    offset = positions - start_of
    return (offset, offset < length_of)


def last_place():
    tp = lax.axis_size("tp")
    place_of = jnp.asarray([turned(offset, "tp") for offset in range(tp)], jnp.int32)
    return place_of[lax.axis_index("tp") ^ (tp - 1)]


def layer_forward(hidden_in, hidden_all, w_in, gains, small, layout, layer_at, hooks):
    on_normed, on_maps, on_hidden = hooks
    conv_w, decay_rows, gain_row, widths = small
    order, valid = layout[1], layout[2]
    heads, ff = widths
    tp = lax.axis_size("tp")
    micro, rows, _ = hidden_in.shape
    hidden = flat(hidden_in)
    if hidden_all is None:
        normed_all = gather_rows(rms_norm(hidden, gains[0]).astype(bf16))
    else:
        normed_all = rms_norm(hidden_all.astype(f32), gains[0]).astype(bf16)
    w_ff, w_in, normed_all = on_normed(layer_at, normed_all)
    pre = matmul(flat(normed_all), w_in).reshape(tp, micro, rows, -1)
    tail = lax.dynamic_index_in_dim(pre, last_place(), 0, False)[:, rows - HALO :, : heads * QKV]
    halo = passed_along(tail, "ctx", 1)
    out_local, reach, starts, inverse, transit, piece_map = local_call(
        order, pre, halo, conv_w, decay_rows, layout[0], heads
    )
    maps = ring_gather(after(piece_map, w_ff))
    on_maps(layer_at, maps)
    gated, entry = finish_call(order, maps, out_local, reach, pre, gain_row, heads)
    gated = gated.reshape(tp, micro * rows, heads * DV)
    w_out = w_ff[:, 2 * ff : 2 * ff + heads * DV]

    def mixer_part(low, high):
        return matmul_nt(flat(gated[low:high]), w_out).reshape(high - low, micro * rows, D)

    middle = hidden + valid * scatter_rows(mixer_part, tp)
    normed_two = rms_norm(middle, gains[1]).astype(bf16)
    normed_two_all = flat(gather_rows(normed_two))
    gate_ff = matmul(normed_two_all, w_ff[:, :ff])
    up_ff = matmul(normed_two_all, w_ff[:, ff : 2 * ff])
    hidden_ff = (jax.nn.silu(gate_ff) * up_ff).astype(bf16).reshape(tp, micro * rows, ff)
    on_hidden(layer_at, hidden_ff)
    w_down = w_ff[:, 2 * ff + heads * DV : 3 * ff + heads * DV]

    def ff_part(low, high):
        return matmul_nt(flat(hidden_ff[low:high]), w_down).reshape(high - low, micro * rows, D)

    leaving = middle + valid * scatter_rows(ff_part, tp)
    saved = (
        hidden,
        normed_all,
        pre,
        halo,
        out_local,
        reach,
        starts,
        inverse,
        transit,
        maps,
        entry,
        gated,
        middle,
        normed_two_all,
        gate_ff,
        up_ff,
        hidden_ff,
    )
    return leaving.reshape(hidden_in.shape), saved


def layer_backward(grad_out, saved, weights, small, layout, before, beside):
    (
        hidden,
        normed_all,
        pre,
        halo,
        out_local,
        reach,
        starts,
        inverse,
        transit,
        maps,
        entry,
        gated,
        middle,
        normed_two_all,
        gate_ff,
        up_ff,
        hidden_ff,
    ) = saved
    w_in, w_ff, gains = weights
    conv_w, decay_rows, gain_row, widths = small
    order, valid = layout[1], layout[2]
    heads, ff = widths
    tp = lax.axis_size("tp")
    micro, rows, _ = grad_out.shape
    grad = flat(grad_out)
    ff_grad = flat(gather_rows((valid * grad).astype(bf16)))
    w_down = w_ff[:, 2 * ff + heads * DV : 3 * ff + heads * DV]
    hidden_grad = matmul(ff_grad, w_down)
    open_at = jax.nn.sigmoid(gate_ff)
    gate_grad = (hidden_grad * up_ff * open_at * (1.0 + gate_ff * (1.0 - open_at))).astype(bf16)
    up_grad = (hidden_grad * gate_ff * open_at).astype(bf16)
    blocks_gate = gate_grad.reshape(tp, micro * rows, ff)
    blocks_up = up_grad.reshape(tp, micro * rows, ff)

    def two_part(low, high):
        part = matmul_nt(flat(blocks_gate[low:high]), w_ff[:, :ff]) + matmul_nt(
            flat(blocks_up[low:high]), w_ff[:, ff : 2 * ff]
        )
        return part.reshape(high - low, micro * rows, D)

    middle_part, gain_two = rms_back(middle, gains[1], scatter_rows(two_part, tp))
    middle_grad = grad + middle_part
    mixer_grad = flat(gather_rows((valid * middle_grad).astype(bf16)))
    w_out = w_ff[:, 2 * ff : 2 * ff + heads * DV]
    gated_grad = matmul(mixer_grad, w_out).reshape(tp, micro, rows, heads * DV)
    out_grad, gate_low, gain_grad, base = unfinish_call(
        entry, out_local, reach, pre, gain_row, gated_grad, heads
    )
    bases = ring_gather(after(base, *before))
    if beside is not None:
        bases, beside = lax.optimization_barrier((bases, beside))
    low_ff = weights_call(
        (normed_two_all, mixer_grad, ff_grad),
        (0, 0, 1, 2),
        (gate_grad, up_grad, flat(gated), flat(hidden_ff)),
    )
    low_ff = after(low_ff, bases)
    owned_ff = ring_scatter(low_ff)
    x_grad, halo_grad, conv_grad, rate_low, decay_grad = adjoint_call(
        order, pre, halo, conv_w, decay_rows, layout[0], starts, inverse, transit, entry, maps, bases, out_grad, heads
    )
    log_grad = jnp.sum(decay_grad[:, :, 0, 0], axis=0)
    bias_grad = jnp.stack([jnp.sum(decay_grad[:, at, 4, 2 * at]) for at in range(heads)])
    back_rows = passed_along(halo_grad, "ctx", -1)
    back_rows = jnp.transpose(back_rows, (0, 2, 1, 3)).reshape(1, micro, HALO, heads * QKV)
    at = last_place()
    zero = jnp.zeros((), jnp.int32)
    corner = (at, zero, zero + rows - HALO, zero)
    tail = lax.dynamic_slice(x_grad, corner, (1, micro, HALO, heads * QKV))
    tail = (tail.astype(f32) + back_rows).astype(bf16)
    x_grad = lax.dynamic_update_slice(x_grad, tail, corner)
    parts = [part.reshape(tp, micro * rows, -1) for part in (x_grad, gate_low, rate_low)]

    def one_part(low, high):
        total, start = None, 0
        for part in parts:
            width = part.shape[-1]
            term = matmul_nt(flat(part[low:high]), w_in[:, start : start + width])
            total = term if total is None else total + term
            start += width
        return total.reshape(high - low, micro * rows, D)

    hidden_part, gain_one = rms_back(hidden, gains[0], scatter_rows(one_part, tp))
    leaving = middle_grad + hidden_part
    low_in = weights_call((flat(normed_all),), (0, 0, 0), [flat(part) for part in parts])
    owned_in = ring_scatter(after(low_in, owned_ff))
    conv_grad = jnp.sum(conv_grad, axis=0)[:, :CONV]
    gain_grad = jnp.sum(gain_grad[:, :, 0], axis=(0, 1))
    small_grads = (conv_grad, log_grad, bias_grad, gain_grad, gain_one, gain_two)
    return leaving.reshape(grad_out.shape), owned_in, owned_ff, small_grads, beside


def body(
    inputs,
    cotangent,
    lengths,
    norm_gain,
    w_qkv,
    w_gate,
    w_rates,
    conv_weight,
    decay_log,
    decay_bias,
    out_gain,
    w_out,
    w_gu,
    w_down,
):
    tp = lax.axis_size("tp")
    ctx = lax.axis_size("ctx")
    micro, shard_rows, _ = inputs.shape
    piece_rows = shard_rows * tp
    layers = w_qkv.shape[0]
    own = w_qkv.shape[1]
    heads = w_qkv.shape[2]
    ff = w_gu.shape[3]
    ctx_at = lax.axis_index("ctx")
    tp_at = lax.axis_index("tp")
    piece_pos = ctx_at * piece_rows + jnp.arange(piece_rows, dtype=jnp.int32)
    shard_pos = (ctx_at * tp + tp_at) * shard_rows + jnp.arange(shard_rows, dtype=jnp.int32)
    offset = jnp.stack([token_layout(lengths[m], piece_pos)[0] for m in range(micro)])
    valid = jnp.stack([token_layout(lengths[m], shard_pos)[1] for m in range(micro)])
    valid = valid.astype(f32).reshape(-1, 1)
    ring, places = ring_of(ctx), ring_places()
    order = [ctx_at] + [tp_at ^ turned(place, "tp") for place in range(tp)]
    order = jnp.stack([part.astype(jnp.int32) for part in order] + [jnp.int32(p) for p in places])
    marks = [(offset >= reach).astype(f32) for reach in (1, 2, 3, 1)]
    cols = jnp.stack(marks + [jnp.zeros_like(marks[0])] * 4, axis=-1)
    layout = (cols, order, valid)

    gains = in_order(gather_blocks(norm_gain, "ctx"), "ctx")
    gains = jnp.stack([gains[device] for device in ring])
    gains = jnp.transpose(gains, (1, 2, 0, 3)).reshape(layers, 2, D).astype(f32)
    in_width = heads * (QKV + DV + 2)
    in_spare = -in_width % LANES
    shards = []
    for layer_at in range(layers):
        shard_in = jnp.concatenate(
            [
                w_qkv[layer_at].reshape(own, -1),
                w_gate[layer_at].reshape(own, -1),
                w_rates[layer_at].reshape(own, -1),
                jnp.zeros((own, in_spare), bf16),
            ],
            axis=1,
        )
        shard_ff = jnp.concatenate(
            [
                w_gu[layer_at, 0],
                w_gu[layer_at, 1],
                w_out[layer_at].reshape(-1, own).T,
                w_down[layer_at].T,
            ],
            axis=1,
        )
        shards.append((shard_in, shard_ff))

    def gathered(shard, *before):
        return ring_gather(after(shard, *before), axis=0, tiled=True)

    weights_in = [gathered(shards[0][0])] + [None] * (layers - 1)
    weights_ff = [None] * layers

    def on_normed(layer_at, token):
        if layer_at == 0:
            shard, weights_in[0], token = lax.optimization_barrier(
                (shards[0][1], weights_in[0], token)
            )
            weights_ff[0] = gathered(shard)
        return weights_ff[layer_at], weights_in[layer_at], token

    def on_maps(layer_at, token):
        if layer_at + 1 < layers:
            weights_in[layer_at + 1] = gathered(shards[layer_at + 1][0], token)

    def on_hidden(layer_at, token):
        if layer_at + 1 < layers:
            following = layer_at + 1
            weights_ff[following] = gathered(shards[following][1], weights_in[following], token)

    hooks = (on_normed, on_maps, on_hidden)
    smalls = []
    for layer_at in range(layers):
        conv_w = jnp.transpose(conv_weight[layer_at], (1, 0, 2))
        conv_w = jnp.concatenate([conv_w, jnp.zeros((heads, 8 - CONV, QKV), f32)], axis=1)
        gain_row = jnp.broadcast_to(out_gain[layer_at][None], (8, DV))
        scale, bias = -jnp.exp(decay_log[layer_at]), decay_bias[layer_at]
        pair = jnp.stack([jnp.stack([part, jnp.zeros_like(part)], axis=1) for part in (scale, bias)])
        decay_rows = jnp.pad(pair.reshape(2, -1), ((0, 6), (0, LANES - 2 * heads)))
        smalls.append(
            (conv_w, decay_rows, gain_row, (heads, ff))
        )

    moved = blocks_moved(inputs, ring)
    hidden_all = gather_rows(flat(moved))
    hidden_now = moved.astype(f32)
    saved_all = []
    for layer_at in range(layers):
        hidden_now, saved = layer_forward(
            hidden_now, hidden_all, weights_in[layer_at], gains[layer_at], smalls[layer_at], layout, layer_at, hooks
        )
        hidden_all = None
        saved_all.append(saved)
    weights = list(zip(weights_in, weights_ff, gains))
    grad_now = blocks_moved(cotangent, ring)
    before = ()
    beside = hidden_now
    big = [None] * layers
    small = [None] * layers
    for layer_at in reversed(range(layers)):
        grad_now, owned_in, owned_ff, small_grads, beside = layer_backward(
            grad_now, saved_all[layer_at], weights[layer_at], smalls[layer_at], layout, before, beside
        )
        if beside is not None:
            hidden_now, beside = beside, None
        before = (owned_in,)
        big[layer_at] = (owned_in.astype(f32), owned_ff.astype(f32))
        small[layer_at] = small_grads

    head_parts = [jnp.stack([small[at][member] for at in range(layers)]) for member in range(3)]
    wide_parts = [jnp.stack([small[at][member] for at in range(layers)]) for member in range(3, 6)]
    sizes = [part.size for part in head_parts + wide_parts]
    head_size = sum(sizes[:3])
    packed = jnp.concatenate([part.reshape(-1) for part in head_parts + wide_parts])
    spare = -packed.size % (8 * LANES)
    packed = jnp.concatenate([packed, jnp.zeros((spare,), f32)]).reshape(-1, LANES)
    packed = sum_over(packed, "ctx").reshape(-1)
    wide = packed[head_size : sum(sizes)]
    wide_size = wide.size
    spare = -wide_size % (8 * LANES)
    wide = jnp.concatenate([wide, jnp.zeros((spare,), f32)]).reshape(-1, LANES)
    wide = sum_over(wide, "tp").reshape(-1)
    parts = []
    start = 0
    for part, size in zip(head_parts, sizes[:3]):
        parts.append(packed[start : start + size].reshape(part.shape))
        start += size
    start = 0
    for part, size in zip(wide_parts, sizes[3:]):
        parts.append(wide[start : start + size].reshape(part.shape))
        start += size
    conv_grad, log_grad, bias_grad, ogain_grad, gain_one, gain_two = parts
    conv_grad = jnp.transpose(conv_grad, (0, 2, 1, 3))
    norm_grad = jnp.stack([gain_one, gain_two], axis=1)
    own_place = jnp.asarray(places, jnp.int32)[ctx_at]
    norm_grad = lax.dynamic_slice_in_dim(norm_grad, own_place * own, own, 2)

    in_all = jnp.stack([big[at][0] for at in range(layers)])
    ff_all = jnp.stack([big[at][1] for at in range(layers)])
    qkv_end, gate_end = heads * QKV, heads * (QKV + DV)
    grad_qkv = in_all[..., :qkv_end].reshape(w_qkv.shape)
    grad_gate_w = in_all[..., qkv_end:gate_end].reshape(w_gate.shape)
    grad_rates = in_all[..., gate_end:in_width].reshape(w_rates.shape)
    grad_gu = jnp.stack([ff_all[..., :ff], ff_all[..., ff : 2 * ff]], axis=1)
    out_end = 2 * ff + heads * DV
    grad_out_w = jnp.swapaxes(ff_all[..., 2 * ff : out_end], 1, 2).reshape(w_out.shape)
    grad_down = jnp.swapaxes(ff_all[..., out_end:], 1, 2)
    return (
        blocks_moved(hidden_now, places),
        blocks_moved(grad_now, places),
        norm_grad,
        grad_qkv,
        grad_gate_w,
        grad_rates,
        conv_grad,
        log_grad,
        bias_grad,
        ogain_grad,
        grad_out_w,
        grad_gu,
        grad_down,
    )


def solution(mesh):
    placed = (
        P(None, ("ctx", "tp"), None),
        P(None, ("ctx", "tp"), None),
        P(),
        P(None, None, "ctx"),
        P(None, "ctx", "tp", None),
        P(None, "ctx", "tp", None),
        P(None, "ctx", "tp", None),
        P(None, None, "tp", None),
        P(None, "tp"),
        P(None, "tp"),
        P(),
        P(None, "tp", None, "ctx"),
        P(None, None, "ctx", "tp"),
        P(None, "tp", "ctx"),
    )
    return jax.shard_map(
        body,
        mesh=mesh,
        in_specs=placed,
        out_specs=(
            P(None, ("ctx", "tp"), None),
            P(None, ("ctx", "tp"), None),
            P(None, None, "ctx"),
            P(None, "ctx", "tp", None),
            P(None, "ctx", "tp", None),
            P(None, "ctx", "tp", None),
            P(None, None, "tp", None),
            P(None, "tp"),
            P(None, "tp"),
            P(),
            P(None, "tp", None, "ctx"),
            P(None, None, "ctx", "tp"),
            P(None, "tp", "ctx"),
        ),
        check_vma=False,
    )
```

```python
from functools import partial

import jax
import jax.numpy as jnp
from jax import lax
from jax.experimental import pallas as pl
from jax.experimental.pallas import tpu as pltpu
from jax.sharding import PartitionSpec as P

D = 1024
DK = 128
DV = 256
QKV = 512
AUG = DV + DK
CONV = 4
STRETCH = 64
PACK = 256
PER_PACK = PACK // STRETCH
LANES = 128
HALO = 8

epsilon = 1e-05
unit_eps = 1e-06
f32 = jnp.float32
bf16 = jnp.bfloat16
VMEM_BYTES = 56 * 1024 * 1024


def swap(value, axis, bit):
    count = lax.axis_size(axis)
    return lax.ppermute(value, axis, [(i, i ^ bit) for i in range(count)])


def bits_of(axis):
    count = lax.axis_size(axis)
    bits = []
    bit = count // 2
    while bit >= 1:
        bits.append(bit)
        bit //= 2
    return bits


def turned(place, axis):
    offset = 0
    for step, bit in enumerate(bits_of(axis)):
        if place >> step & 1:
            offset |= bit
    return offset


def gather_blocks(value, axis):
    blocks = value[None]
    for bit in bits_of(axis):
        blocks = jnp.concatenate([blocks, swap(blocks, axis, bit)], axis=0)
    return blocks


def in_order(blocks, axis):
    count = lax.axis_size(axis)
    me = lax.axis_index(axis)
    place_of = [turned(offset, axis) for offset in range(count)]
    place_of = jnp.asarray(place_of, jnp.int32)
    return jnp.stack(
        [
            lax.dynamic_index_in_dim(blocks, place_of[me ^ device], 0, False)
            for device in range(count)
        ]
    )


def to_relative(blocks, axis):
    me = lax.axis_index(axis)
    return jnp.stack(
        [
            lax.dynamic_index_in_dim(blocks, me ^ turned(place, axis), 0, False)
            for place in range(blocks.shape[0])
        ]
    )


def gather_rows(rows):
    return gather_blocks(rows, "tp")


def scatter_rows(product_of, count):
    half = count // 2
    kept = None
    for bit in reversed(bits_of("tp")):
        if kept is None:
            sent = product_of(half, count).astype(bf16)
            received = swap(sent, "tp", bit)
            kept = product_of(0, half) + received.astype(f32)
        else:
            received = swap(kept[half:].astype(bf16), "tp", bit)
            kept = kept[:half] + received.astype(f32)
        half //= 2
    return kept[0]


def sum_over(value, axis):
    for bit in bits_of(axis):
        value = value + swap(value, axis, bit)
    return value


def ring_of(count):
    if count % 4 != 0 or count < 8:
        return list(range(count))
    wide = count // 4
    ring = [row * wide for row in range(4)]
    for row in reversed(range(4)):
        columns = range(1, wide) if row % 2 == 1 else reversed(range(1, wide))
        ring += [row * wide + column for column in columns]
    return ring


def ring_gather(value, **options):
    ring = ring_of(lax.axis_size("ctx"))
    return lax.all_gather(value, "ctx", axis_index_groups=[ring], **options)


def ring_scatter(value):
    ring = ring_of(lax.axis_size("ctx"))
    return lax.psum_scatter(
        value, "ctx", scatter_dimension=0, tiled=True, axis_index_groups=[ring]
    )


def ring_places():
    ring = ring_of(lax.axis_size("ctx"))
    return [ring.index(device) for device in range(len(ring))]


def blocks_moved(value, source_of):
    parts = jnp.split(value, len(source_of), axis=-1)
    return jnp.concatenate([parts[source] for source in source_of], axis=-1)


def after(value, *others):
    return lax.optimization_barrier((value,) + others)[0]


def passed_along(value, axis, steps):
    count = lax.axis_size(axis)
    initial, last = (max(0, -steps), min(count, count - steps))
    return lax.ppermute(value, axis, [(source, source + steps) for source in range(initial, last)])


def dot(left, right, contract):
    return lax.dot_general(
        left.astype(bf16),
        right.astype(bf16),
        (contract, ((), ())),
        preferred_element_type=f32,
    )


def nn(left, right):
    return dot(left, right, ((1,), (0,)))


def nt(left, right):
    return dot(left, right, ((1,), (1,)))


def tn(left, right):
    return dot(left, right, ((0,), (0,)))


def split_right(product, left, right):
    high, low = halves(right)
    return product(left, high) + product(left, low)


def split_left(product, left, right):
    high, low = halves(left)
    return product(high, right) + product(low, right)


def halves(value):
    high = value.astype(bf16)
    return high, (value - high.astype(f32)).astype(bf16)


def nn_fine(left, right):
    left_hi, left_lo = left
    right_hi, right_lo = right
    return nn(left_hi, right_hi) + (nn(left_hi, right_lo) + nn(left_lo, right_hi))


def sigmoid(value):
    return 1.0 / (1.0 + jnp.exp(-value))


def index_grids():
    row_at = lax.broadcasted_iota(jnp.int32, (PACK, PACK), 0)
    col_at = lax.broadcasted_iota(jnp.int32, (PACK, PACK), 1)
    return row_at, col_at


def unit_lower_inverse(lower, row_at, col_at):
    eye = (row_at == col_at).astype(f32)
    small = jnp.where(row_at // 8 == col_at // 8, lower, 0.0)
    small_h = halves(small)
    power2 = nn_fine(small_h, small_h)
    power2_h = halves(power2)
    inverse = eye - small
    inverse = inverse + nn_fine(halves(inverse), power2_h)
    power4 = nn_fine(power2_h, power2_h)
    inverse = inverse + nn_fine(halves(inverse), halves(power4))
    size = 8
    while size < STRETCH:
        corner = jnp.where(
            (row_at // (2 * size) == col_at // (2 * size)) & (row_at // size != col_at // size),
            lower,
            0.0,
        )
        inverse_h = halves(inverse)
        inverse = inverse - nn_fine(inverse_h, halves(nn_fine(halves(corner), inverse_h)))
        size *= 2
    return inverse


def load_rates(order_ref, rate_ref, rs):
    tp, _, rows, _ = rate_ref.shape
    for place in range(tp):
        at = pl.multiple_of(order_ref[1 + place] * rows, 8)
        rs[pl.ds(at, rows), :] = rate_ref[place, 0]


def rate_parts(raw, decay_ref):
    shifted = raw + decay_ref[1:2, :]
    soft = jnp.maximum(shifted, 0.0) + jnp.log1p(jnp.exp(-jnp.abs(shifted)))
    return shifted, decay_ref[0:1, :] * soft, sigmoid(raw)


def exact_sums(pattern, values):
    high, low = halves(values)
    return nn(pattern, high) + nn(pattern, low)


def decay_terms(decays, row_at, col_at):
    same = row_at // STRETCH == col_at // STRETCH
    upto = (same & (row_at >= col_at)).astype(f32).astype(bf16)
    whole = same.astype(f32).astype(bf16)
    running = exact_sums(upto, decays)
    total = exact_sums(whole, decays)
    high, low = halves(decays[:, :8])
    running_rows = dot(high, upto, ((0,), (1,))) + dot(low, upto, ((0,), (1,)))
    return running, running_rows, total


def load_pieces(order_ref, x_ref, halo_ref, xs, head):
    tp, _, rows, _ = x_ref.shape
    lanes = pl.ds(head * QKV, QKV)
    xs[0:HALO, :] = halo_ref[0, :, lanes]
    for place in range(tp):
        at = pl.multiple_of(order_ref[1 + place] * rows + HALO, 8)
        xs[pl.ds(at, rows), :] = x_ref[place, 0, :, lanes]


def conv_of(xs, weights, cols, first, count):
    total = None
    for reach in range(CONV):
        rows = xs[HALO + first - reach : HALO + first - reach + count, :]
        if reach > 0:
            rows = rows * cols[first : first + count, reach - 1 : reach]
        term = rows * weights[CONV - 1 - reach : CONV - reach, :]
        total = term if total is None else total + term
    return total


def front(conv_out):
    gate = sigmoid(conv_out)
    active = conv_out * gate
    raw_q, raw_k, values = active[:, :DK], active[:, DK : 2 * DK], active[:, 2 * DK :]
    scale_q = lax.rsqrt(jnp.sum(raw_q * raw_q, axis=1, keepdims=True) + unit_eps)
    scale_k = lax.rsqrt(jnp.sum(raw_k * raw_k, axis=1, keepdims=True) + unit_eps)
    return gate, raw_q * scale_q, raw_k * scale_k, values, scale_q, scale_k


def pack_terms(queries, keys, running, running_row, row_at, col_at):
    inside = (row_at // STRETCH == col_at // STRETCH) & (row_at >= col_at)
    spread = running - running_row
    weight = jnp.where(inside, jnp.exp(jnp.where(inside, spread, 0.0)), 0.0)
    keys_low = keys.astype(bf16)
    key_dots = nt(keys_low, keys_low)
    scores = nt(queries, keys_low) * weight
    pair = jnp.where(row_at > col_at, key_dots * weight, 0.0)
    return weight, pair, scores


def local_kernel(
    order_ref,
    x_ref,
    rate_ref,
    halo_ref,
    conv_ref,
    decay_ref,
    cols_ref,
    out_ref,
    reach_ref,
    starts_ref,
    inverse_ref,
    transit_ref,
    map_ref,
    xs,
    rs,
    o_scr,
    r_scr,
):
    tp, _, rows, _ = x_ref.shape
    heads = conv_ref.shape[0]
    piece = tp * rows
    packs = piece // PACK
    blocks = piece // STRETCH
    row_at, col_at = index_grids()
    units = [(head, pack) for head in range(heads) for pack in range(packs)]
    held = {}
    shared = {}
    load_rates(order_ref, rate_ref, rs)
    for head in range(heads):
        load_pieces(order_ref, x_ref, halo_ref, xs.at[head], head)
    for pack in range(packs):
        _, decays, betas = rate_parts(rs[pack * PACK : (pack + 1) * PACK, :], decay_ref)
        running, running_rows, total = decay_terms(decays, row_at, col_at)
        shared[pack] = (
            running,
            running_rows,
            betas,
            jnp.exp(running),
            jnp.exp(total - running),
            jnp.exp(total),
        )
    for head, pack in units:
        first = pack * PACK
        conv_out = conv_of(xs.at[head], conv_ref.at[head], cols_ref.at[0], first, PACK)
        _, queries, keys, values, _, _ = front(conv_out)
        lane = 2 * head
        running, running_rows, betas, grown, tail, _ = shared[pack]
        beta = betas[:, lane + 1 : lane + 2]
        grown = grown[:, lane : lane + 1]
        weight, pair, scores = pack_terms(
            queries,
            keys,
            running[:, lane : lane + 1],
            running_rows[lane : lane + 1, :],
            row_at,
            col_at,
        )
        cols = (beta, grown, tail[:, lane : lane + 1], beta * grown)
        held[head, pack] = (queries, keys, values, cols, pair * beta, scores)
    inverses = {
        unit: unit_lower_inverse(held[unit][4], row_at, col_at).astype(bf16) for unit in units
    }
    solved = {}
    moves = {}
    for unit in units:
        head, pack = unit
        queries, keys, values, cols, _, scores = held[unit]
        inverse_ref[0, head, pack] = inverses[unit]
        solved_w = nn(inverses[unit], keys * cols[3])
        solved_u = nn(inverses[unit], values * cols[0])
        tails = (keys * cols[2]).astype(bf16)
        solved_w = solved_w.astype(bf16)
        solved_u_low = solved_u.astype(bf16)
        for sub in range(PER_PACK):
            part = slice(sub * STRETCH, (sub + 1) * STRETCH)
            block = pack * PER_PACK + sub
            transit = tn(tails[part], solved_w[part]).astype(bf16)
            transit_ref[0, head, block] = transit
            moves[head, block] = (transit, tn(tails[part], solved_u_low[part]))
        solved[unit] = (solved_w, solved_u)
    eye = (row_at[:DK, :DK] == col_at[:DK, :DK]).astype(f32)
    biases = [jnp.zeros((DK, DV), f32) for _ in range(heads)]
    maps = [eye for _ in range(heads)]
    for block in range(blocks):
        for head in range(heads):
            at = block % PER_PACK * STRETCH
            retain = shared[block // PER_PACK][5][at : at + 1, 2 * head : 2 * head + 1]
            keep = cols_ref[0, block * STRETCH : block * STRETCH + 1, 3:4]
            bias = biases[head] * keep
            whole = maps[head] * keep
            low = jnp.concatenate([bias, whole], axis=1).astype(bf16)
            starts_ref[0, head, block] = low
            transit, fresh = moves[head, block]
            moved = nn(transit, low)
            biases[head] = bias * retain - moved[:, :DV] + fresh
            maps[head] = whole * retain - moved[:, DV:]
    for head in range(heads):
        map_ref[0, head, :, :DV] = biases[head].astype(bf16)
        map_ref[0, head, :, DV:] = maps[head].astype(bf16)
    for unit in units:
        head, pack = unit
        queries, keys, values, cols, _, scores = held[unit]
        solved_w, solved_u = solved[unit]
        reading = (queries * cols[1]).astype(bf16)
        carried, recalled = [], []
        for sub in range(PER_PACK):
            part = slice(sub * STRETCH, (sub + 1) * STRETCH)
            start = starts_ref[0, head, pack * PER_PACK + sub]
            both = nn(jnp.concatenate([reading[part], solved_w[part]], axis=0), start)
            carried.append(both[:STRETCH])
            recalled.append(both[STRETCH:])
        carried = jnp.concatenate(carried, axis=0)
        recalled = jnp.concatenate(recalled, axis=0)
        low_scores = scores.astype(bf16)
        first = pack * PACK
        o_scr[head, first : first + PACK, :] = carried[:, :DV] + nn(
            low_scores, solved_u - recalled[:, :DV]
        )
        r_scr[head, first : first + PACK, :] = carried[:, DV:] - nn(low_scores, recalled[:, DV:])
    for place in range(tp):
        at = pl.multiple_of(order_ref[1 + place] * rows, 8)
        for head in range(heads):
            out_ref[place, 0, :, head * DV : (head + 1) * DV] = o_scr[head, pl.ds(at, rows), :]
            reach_ref[place, 0, :, head * DK : (head + 1) * DK] = r_scr[
                head, pl.ds(at, rows), :
            ].astype(bf16)


def finish_kernel(order_ref, maps_ref, out_ref, reach_ref, gate_ref, gain_ref, gated_ref, entry_ref):
    tp = out_ref.shape[0]

    def one(step, entry):
        whole = maps_ref[order_ref[1 + tp + step], 0, 0]
        return whole[:, :DV].astype(f32) + nn(whole[:, DV:], entry)

    entry = lax.fori_loop(0, order_ref[0], one, jnp.zeros((DK, DV), f32))
    entry_ref[0, 0] = entry
    entry_low = entry.astype(bf16)
    for place in range(tp):
        outputs = out_ref[place, 0] + nn(reach_ref[place, 0], entry_low)
        scale = lax.rsqrt(jnp.mean(outputs * outputs, axis=1, keepdims=True) + epsilon)
        gate = gate_ref[place, 0]
        gated = outputs * scale * gain_ref[0:1, :] * (gate * sigmoid(gate))
        gated_ref[place, 0] = gated.astype(bf16)


def unfinish_kernel(
    entry_ref, out_ref, reach_ref, gate_ref, gain_ref, grad_ref, ograd_ref, zgrad_ref, ggrad_ref, base_ref
):
    tp = out_ref.shape[0]
    entry_low = entry_ref[0, 0].astype(bf16)
    gain = gain_ref[0:1, :]
    base = jnp.zeros((DK, DV), f32)
    gain_grad = jnp.zeros((1, DV), f32)
    for place in range(tp):
        reach = reach_ref[place, 0]
        outputs = out_ref[place, 0] + nn(reach, entry_low)
        scale = lax.rsqrt(jnp.mean(outputs * outputs, axis=1, keepdims=True) + epsilon)
        unit = outputs * scale
        gate = gate_ref[place, 0]
        open_at = sigmoid(gate)
        grad = grad_ref[place, 0]
        normed_grad = grad * (gate * open_at)
        gate_grad = grad * (unit * gain) * (open_at * (1.0 + gate * (1.0 - open_at)))
        zgrad_ref[place, 0] = gate_grad.astype(bf16)
        gain_grad = gain_grad + jnp.sum(normed_grad * unit, axis=0, keepdims=True)
        inner = normed_grad * gain
        out_grad = scale * (inner - unit * jnp.mean(inner * unit, axis=1, keepdims=True))
        ograd_ref[place, 0] = out_grad
        base = base + split_right(tn, reach, out_grad)
    ggrad_ref[0, 0] = jnp.broadcast_to(gain_grad, (8, DV))
    base_ref[0, 0] = base.astype(bf16)


def adjoint_kernel(
    order_ref,
    x_ref,
    rate_ref,
    halo_ref,
    conv_ref,
    decay_ref,
    cols_ref,
    starts_ref,
    inverse_ref,
    transit_ref,
    entry_ref,
    maps_ref,
    bases_ref,
    ograd_ref,
    xgrad_ref,
    hgrad_ref,
    cgrad_ref,
    rgrad_ref,
    dgrad_ref,
    xs,
    rs,
    gs,
    ds,
    rgs,
):
    tp, _, rows, _ = x_ref.shape
    piece = tp * rows
    packs = piece // PACK
    blocks = piece // STRETCH
    ctx = maps_ref.shape[0]
    row_at, col_at = index_grids()
    head_at = pl.program_id(1)
    load_pieces(order_ref, x_ref, halo_ref, xs, 0)
    load_rates(order_ref, rate_ref, rs)
    lanes = lax.broadcasted_iota(jnp.int32, (PACK, LANES), 1)
    decay_lane = (lanes == 2 * head_at).astype(f32)
    beta_lane = (lanes == 2 * head_at + 1).astype(f32)

    @pl.when(head_at == 0)
    def _():
        rgs[...] = jnp.zeros_like(rgs)

    for place in range(tp):
        at = pl.multiple_of(order_ref[1 + place] * rows, 16)
        gs[pl.ds(at, rows), :] = ograd_ref[place, 0]

    def one(step, grad):
        source = order_ref[1 + tp + ctx - 1 - step]
        return bases_ref[source, 0, 0].astype(f32) + tn(maps_ref[source, 0, 0], grad)

    after = lax.fori_loop(0, ctx - 1 - order_ref[0], one, jnp.zeros((DK, DV), f32))
    entry_low = entry_ref[0, 0].astype(bf16)
    held = {}
    starts = {}
    turns = {}
    retains = {}
    decay_sum = jnp.zeros((1, 1), f32)
    rate_sum = jnp.zeros((1, LANES), f32)
    for pack in range(packs):
        first = pack * PACK
        conv_out = conv_of(xs, conv_ref.at[0], cols_ref.at[0], first, PACK)
        _, queries, keys, values, _, _ = front(conv_out)
        shifted, decays, betas = rate_parts(rs[first : first + PACK, :], decay_ref)
        decay = jnp.sum(decays * decay_lane, axis=1, keepdims=True)
        beta = jnp.sum(betas * beta_lane, axis=1, keepdims=True)
        running, running_rows, total = decay_terms(
            jnp.broadcast_to(decay, (PACK, LANES)), row_at, col_at
        )
        retains[pack] = jnp.exp(total)
        grown = jnp.exp(running)[:, 0:1]
        cols = (beta, grown, jnp.exp(total - running)[:, 0:1], beta * grown)
        weight, pair, scores = pack_terms(
            queries, keys, running[:, 0:1], running_rows[0:1, :], row_at, col_at
        )
        inverse = inverse_ref[0, 0, pack]
        solved_w = nn(inverse, keys * cols[3]).astype(bf16)
        solved_u = nn(inverse, values * cols[0])
        out_grad = gs[first : first + PACK, :]
        through = split_right(tn, scores, out_grad)
        through_low = through.astype(bf16)
        reading = (queries * cols[1]).astype(bf16)
        fresh = []
        for sub in range(PER_PACK):
            part = slice(sub * STRETCH, (sub + 1) * STRETCH)
            block = pack * PER_PACK + sub
            start = starts_ref[0, 0, block]
            start = start[:, :DV].astype(f32) + nn(start[:, DV:], entry_low)
            starts[block] = start
            fresh.append(solved_u[part] - nn(solved_w[part], start))
            turns[block] = split_right(tn, reading[part], out_grad[part]) - tn(solved_w[part], through_low[part])
        held[pack] = (
            queries,
            keys,
            values,
            cols,
            weight,
            pair,
            scores,
            inverse,
            solved_w,
            solved_u,
            out_grad,
            through,
            jnp.concatenate(fresh, axis=0),
            shifted,
            decay,
            betas,
        )
    grads = {}
    grad = after
    for block in reversed(range(blocks)):
        grads[block] = grad
        at = block % PER_PACK * STRETCH
        grad = grad * retains[block // PER_PACK][at : at + 1, 0:1]
        grad = grad - tn(transit_ref[0, 0, block], grads[block]) + turns[block]
        grad = grad * cols_ref[0, block * STRETCH : block * STRETCH + 1, 3:4]
    ds[0:HALO, :] = jnp.zeros((HALO, QKV), f32)
    ds[HALO + piece : 2 * HALO + piece, :] = jnp.zeros((HALO, QKV), f32)
    for pack in range(packs):
        first = pack * PACK
        (
            queries,
            keys,
            values,
            cols,
            weight,
            pair,
            scores,
            inverse,
            solved_w,
            solved_u,
            out_grad,
            through,
            fresh,
            shifted,
            decay,
            betas,
        ) = held[pack]
        beta, grown, tail, beta_grown = cols
        tails = keys * tail
        tails_low = tails.astype(bf16)
        fresh_low = fresh.astype(bf16)
        fresh_grad, read_grad, solved_w_grad, tails_grad, last_grad = [], [], [], [], []
        for sub in range(PER_PACK):
            part = slice(sub * STRETCH, (sub + 1) * STRETCH)
            block = pack * PER_PACK + sub
            grad_now = grads[block]
            grad_low = grad_now.astype(bf16)
            now = through[part] + nn(tails_low[part], grad_low)
            fresh_grad.append(now)
            both = split_left(nt, jnp.concatenate([out_grad[part], now], axis=0), starts[block])
            read_grad.append(both[:STRETCH])
            solved_w_grad.append(-both[STRETCH:])
            tails_grad.append(nt(fresh_low[part], grad_low))
            retain = retains[pack][sub * STRETCH : sub * STRETCH + 1, 0:1]
            meet = starts[block] * grad_now
            last_grad.append(
                retain * jnp.sum(meet[:, :DK] + meet[:, DK:], axis=0, keepdims=True)
            )
        fresh_grad = jnp.concatenate(fresh_grad, axis=0)
        read_grad = jnp.concatenate(read_grad, axis=0)
        solved_w_grad = jnp.concatenate(solved_w_grad, axis=0)
        tails_grad = jnp.concatenate(tails_grad, axis=0)
        score_grad = split_left(nt, out_grad, fresh_low)
        dots_grad = (score_grad * weight).astype(bf16)
        right_grad = tn(inverse, jnp.concatenate([fresh_grad, solved_w_grad], axis=1))
        right_u, right_w = right_grad[:, :DV], right_grad[:, DV:]
        lower_grad = -(nt(right_u, solved_u) + nt(right_w, solved_w))
        lower_grad = jnp.where(row_at > col_at, lower_grad, 0.0)
        pair_grad = lower_grad * pair
        key_dots_grad = (lower_grad * weight * beta).astype(bf16)
        spread_grad = pair_grad * beta + score_grad * scores
        keys_low = keys.astype(bf16)
        queries_low = queries.astype(bf16)
        keys_right = jnp.sum(keys * right_w, axis=1, keepdims=True)
        tails_meet = tails * tails_grad
        keys_grad = (
            beta_grown * right_w
            + nn(key_dots_grad, keys_low)
            + tn(key_dots_grad, keys_low)
            + tn(dots_grad, queries_low)
            + tail * tails_grad
        )
        queries_grad = grown * read_grad + nn(dots_grad, keys_low)
        values_grad = beta * right_u
        beta_grad = (
            jnp.sum(values * right_u, axis=1, keepdims=True)
            + grown * keys_right
            + jnp.sum(pair_grad, axis=1, keepdims=True)
        )
        cum_grad = (
            jnp.sum(spread_grad, axis=1, keepdims=True)
            + beta_grown * keys_right
            + grown * jnp.sum(queries * read_grad, axis=1, keepdims=True)
            - jnp.sum(tails_meet, axis=1, keepdims=True)
        )
        cum_row_grad = -jnp.sum(spread_grad, axis=0, keepdims=True)
        later = (row_at // STRETCH == col_at // STRETCH) & (row_at <= col_at)
        from_rows = jnp.sum(jnp.where(later, cum_row_grad, 0.0), axis=1, keepdims=True)
        later_low = later.astype(f32).astype(bf16)
        from_cols = exact_sums(later_low, jnp.broadcast_to(cum_grad, (PACK, LANES)))[:, 0:1]
        ends = []
        for sub in range(PER_PACK):
            part = slice(sub * STRETCH, (sub + 1) * STRETCH)
            end = last_grad[sub] + jnp.sum(tails_meet[part], axis=0, keepdims=True)
            ends.append(
                jnp.broadcast_to(jnp.sum(end, axis=1, keepdims=True), (STRETCH, 1))
            )
        decay_grad = from_rows + from_cols + jnp.concatenate(ends, axis=0)
        decay_sum = decay_sum + jnp.sum(decay_grad * decay, axis=0, keepdims=True)
        rate_grad = decay_grad * (decay_ref[0:1, :] * decay_lane) * sigmoid(shifted)
        rate_grad = rate_grad + beta_grad * (betas * (1.0 - betas)) * beta_lane
        rate_sum = rate_sum + jnp.sum(rate_grad, axis=0, keepdims=True)
        rgs[first : first + PACK, :] += rate_grad
        conv_out = conv_of(xs, conv_ref.at[0], cols_ref.at[0], first, PACK)
        gate, _, _, _, scale_q, scale_k = front(conv_out)
        raw_q_grad = scale_q * (
            queries_grad - queries * jnp.sum(queries * queries_grad, axis=1, keepdims=True)
        )
        raw_k_grad = scale_k * (
            keys_grad - keys * jnp.sum(keys * keys_grad, axis=1, keepdims=True)
        )
        active_grad = jnp.concatenate([raw_q_grad, raw_k_grad, values_grad], axis=1)
        ds[HALO + first : HALO + first + PACK, :] = active_grad * (
            gate * (1.0 + conv_out * (1.0 - gate))
        )
    taps = []
    for reach in range(CONV):
        grad_rows = ds[HALO : HALO + piece, :]
        if reach > 0:
            grad_rows = grad_rows * cols_ref[0, :, reach - 1 : reach]
        taps.append(
            jnp.sum(grad_rows * xs[HALO - reach : HALO - reach + piece, :], axis=0, keepdims=True)
        )
    cgrad_ref[0, 0] = jnp.concatenate(taps[::-1] + [jnp.zeros((8 - CONV, QKV), f32)], axis=0)
    total = ds[0 : HALO + piece, :] * conv_ref[0, CONV - 1 : CONV, :]
    for reach in range(1, CONV):
        masked = ds[HALO : HALO + piece, :] * cols_ref[0, :, reach - 1 : reach]
        xs[HALO : HALO + piece, :] = masked
        xs[0:HALO, :] = jnp.zeros((HALO, QKV), f32)
        xs[HALO + piece : 2 * HALO + piece, :] = jnp.zeros((HALO, QKV), f32)
        total = total + xs[reach : reach + HALO + piece, :] * conv_ref[
            0, CONV - 1 - reach : CONV - reach, :
        ]
    hgrad_ref[0, 0] = total[:HALO, :]
    ds[0:piece, :] = total[HALO:, :]
    for place in range(tp):
        at = pl.multiple_of(order_ref[1 + place] * rows, 8)
        xgrad_ref[place, 0] = ds[pl.ds(at, rows), :].astype(bf16)
        rgrad_ref[place, 0] = rgs[pl.ds(at, rows), :].astype(bf16)
    dgrad_ref[0, 0] = jnp.concatenate(
        [jnp.broadcast_to(decay_sum, (4, LANES)), jnp.broadcast_to(rate_sum, (4, LANES))], axis=0
    )


def shape_of(shape, dtype):
    return jax.ShapeDtypeStruct(shape, dtype)


def local_call(order, pre, halo, conv_w, decay_rows, cols, heads):
    tp, micro, rows, _ = pre.shape
    piece = tp * rows
    packs, blocks = piece // PACK, piece // STRETCH
    rate_at = heads * (QKV + DV) // LANES
    grid = pltpu.PrefetchScalarGridSpec(
        num_scalar_prefetch=1,
        grid=(micro,),
        in_specs=[
            pl.BlockSpec((tp, 1, rows, heads * QKV), lambda m, s: (0, m, 0, 0)),
            pl.BlockSpec((tp, 1, rows, LANES), lambda m, s: (0, m, 0, rate_at)),
            pl.BlockSpec((1, HALO, heads * QKV), lambda m, s: (m, 0, 0)),
            pl.BlockSpec((heads, 8, QKV), lambda m, s: (0, 0, 0)),
            pl.BlockSpec((8, LANES), lambda m, s: (0, 0)),
            pl.BlockSpec((1, piece, 8), lambda m, s: (m, 0, 0)),
        ],
        out_specs=[
            pl.BlockSpec((tp, 1, rows, heads * DV), lambda m, s: (0, m, 0, 0)),
            pl.BlockSpec((tp, 1, rows, heads * DK), lambda m, s: (0, m, 0, 0)),
            pl.BlockSpec((1, heads, blocks, DK, AUG), lambda m, s: (m, 0, 0, 0, 0)),
            pl.BlockSpec((1, heads, packs, PACK, PACK), lambda m, s: (m, 0, 0, 0, 0)),
            pl.BlockSpec((1, heads, blocks, DK, DK), lambda m, s: (m, 0, 0, 0, 0)),
            pl.BlockSpec((1, heads, DK, AUG), lambda m, s: (m, 0, 0, 0)),
        ],
        scratch_shapes=[
            pltpu.VMEM((heads, HALO + piece, QKV), f32),
            pltpu.VMEM((piece, LANES), f32),
            pltpu.VMEM((heads, piece, DV), f32),
            pltpu.VMEM((heads, piece, DK), f32),
        ],
    )
    return pl.pallas_call(
        local_kernel,
        grid_spec=grid,
        out_shape=[
            shape_of((tp, micro, rows, heads * DV), f32),
            shape_of((tp, micro, rows, heads * DK), bf16),
            shape_of((micro, heads, blocks, DK, AUG), bf16),
            shape_of((micro, heads, packs, PACK, PACK), bf16),
            shape_of((micro, heads, blocks, DK, DK), bf16),
            shape_of((micro, heads, DK, AUG), bf16),
        ],
        compiler_params=pltpu.CompilerParams(vmem_limit_bytes=VMEM_BYTES),
        name="delta_local",
    )(order, pre, pre, halo, conv_w, decay_rows, cols)


def finish_call(order, maps, out_local, reach, pre, gain, heads):
    ctx = maps.shape[0]
    tp, micro, rows, _ = out_local.shape
    gate_at = heads * QKV // DV
    grid = pltpu.PrefetchScalarGridSpec(
        num_scalar_prefetch=1,
        grid=(micro, heads),
        in_specs=[
            pl.BlockSpec((ctx, 1, 1, DK, AUG), lambda m, a, s: (0, m, a, 0, 0)),
            pl.BlockSpec((tp, 1, rows, DV), lambda m, a, s: (0, m, 0, a)),
            pl.BlockSpec((tp, 1, rows, DK), lambda m, a, s: (0, m, 0, a)),
            pl.BlockSpec((tp, 1, rows, DV), lambda m, a, s: (0, m, 0, gate_at + a)),
            pl.BlockSpec((8, DV), lambda m, a, s: (0, 0)),
        ],
        out_specs=[
            pl.BlockSpec((tp, 1, rows, DV), lambda m, a, s: (0, m, 0, a)),
            pl.BlockSpec((1, 1, DK, DV), lambda m, a, s: (m, a, 0, 0)),
        ],
    )
    return pl.pallas_call(
        finish_kernel,
        grid_spec=grid,
        out_shape=[
            shape_of((tp, micro, rows, heads * DV), bf16),
            shape_of((micro, heads, DK, DV), f32),
        ],
        compiler_params=pltpu.CompilerParams(vmem_limit_bytes=VMEM_BYTES),
        name="delta_finish",
    )(order, maps, out_local, reach, pre, gain)


def unfinish_call(entry, out_local, reach, pre, gain, grad, heads):
    tp, micro, rows, _ = out_local.shape
    gate_at = heads * QKV // DV
    return pl.pallas_call(
        unfinish_kernel,
        grid=(micro, heads),
        in_specs=[
            pl.BlockSpec((1, 1, DK, DV), lambda m, a: (m, a, 0, 0)),
            pl.BlockSpec((tp, 1, rows, DV), lambda m, a: (0, m, 0, a)),
            pl.BlockSpec((tp, 1, rows, DK), lambda m, a: (0, m, 0, a)),
            pl.BlockSpec((tp, 1, rows, DV), lambda m, a: (0, m, 0, gate_at + a)),
            pl.BlockSpec((8, DV), lambda m, a: (0, 0)),
            pl.BlockSpec((tp, 1, rows, DV), lambda m, a: (0, m, 0, a)),
        ],
        out_specs=[
            pl.BlockSpec((tp, 1, rows, DV), lambda m, a: (0, m, 0, a)),
            pl.BlockSpec((tp, 1, rows, DV), lambda m, a: (0, m, 0, a)),
            pl.BlockSpec((1, 1, 8, DV), lambda m, a: (m, a, 0, 0)),
            pl.BlockSpec((1, 1, DK, DV), lambda m, a: (m, a, 0, 0)),
        ],
        out_shape=[
            shape_of((tp, micro, rows, heads * DV), f32),
            shape_of((tp, micro, rows, heads * DV), bf16),
            shape_of((micro, heads, 8, DV), f32),
            shape_of((micro, heads, DK, DV), bf16),
        ],
        compiler_params=pltpu.CompilerParams(vmem_limit_bytes=VMEM_BYTES),
        name="delta_unfinish",
    )(entry, out_local, reach, pre, gain, grad)


def adjoint_call(
    order, pre, halo, conv_w, decay_rows, cols, starts, inverse, transit, entry, maps, bases, ograd, heads
):
    tp, micro, rows, _ = pre.shape
    ctx = maps.shape[0]
    piece = tp * rows
    packs, blocks = piece // PACK, piece // STRETCH
    rate_at = heads * (QKV + DV) // LANES
    grid = pltpu.PrefetchScalarGridSpec(
        num_scalar_prefetch=1,
        grid=(micro, heads),
        in_specs=[
            pl.BlockSpec((tp, 1, rows, QKV), lambda m, a, s: (0, m, 0, a)),
            pl.BlockSpec((tp, 1, rows, LANES), lambda m, a, s: (0, m, 0, rate_at)),
            pl.BlockSpec((1, HALO, QKV), lambda m, a, s: (m, 0, a)),
            pl.BlockSpec((1, 8, QKV), lambda m, a, s: (a, 0, 0)),
            pl.BlockSpec((8, LANES), lambda m, a, s: (0, 0)),
            pl.BlockSpec((1, piece, 8), lambda m, a, s: (m, 0, 0)),
            pl.BlockSpec((1, 1, blocks, DK, AUG), lambda m, a, s: (m, a, 0, 0, 0)),
            pl.BlockSpec((1, 1, packs, PACK, PACK), lambda m, a, s: (m, a, 0, 0, 0)),
            pl.BlockSpec((1, 1, blocks, DK, DK), lambda m, a, s: (m, a, 0, 0, 0)),
            pl.BlockSpec((1, 1, DK, DV), lambda m, a, s: (m, a, 0, 0)),
            pl.BlockSpec((ctx, 1, 1, DK, DK), lambda m, a, s: (0, m, a, 0, DV // DK)),
            pl.BlockSpec((ctx, 1, 1, DK, DV), lambda m, a, s: (0, m, a, 0, 0)),
            pl.BlockSpec((tp, 1, rows, DV), lambda m, a, s: (0, m, 0, a)),
        ],
        out_specs=[
            pl.BlockSpec((tp, 1, rows, QKV), lambda m, a, s: (0, m, 0, a)),
            pl.BlockSpec((1, 1, HALO, QKV), lambda m, a, s: (m, a, 0, 0)),
            pl.BlockSpec((1, 1, 8, QKV), lambda m, a, s: (m, a, 0, 0)),
            pl.BlockSpec((tp, 1, rows, LANES), lambda m, a, s: (0, m, 0, 0)),
            pl.BlockSpec((1, 1, 8, LANES), lambda m, a, s: (m, a, 0, 0)),
        ],
        scratch_shapes=[
            pltpu.VMEM((2 * HALO + piece, QKV), f32),
            pltpu.VMEM((piece, LANES), f32),
            pltpu.VMEM((piece, DV), f32),
            pltpu.VMEM((2 * HALO + piece, QKV), f32),
            pltpu.VMEM((piece, LANES), f32),
        ],
    )
    return pl.pallas_call(
        adjoint_kernel,
        grid_spec=grid,
        out_shape=[
            shape_of((tp, micro, rows, heads * QKV), bf16),
            shape_of((micro, heads, HALO, QKV), f32),
            shape_of((micro, heads, 8, QKV), f32),
            shape_of((tp, micro, rows, LANES), bf16),
            shape_of((micro, heads, 8, LANES), f32),
        ],
        compiler_params=pltpu.CompilerParams(vmem_limit_bytes=VMEM_BYTES),
        name="delta_adjoint",
    )(order, pre, pre, halo, conv_w, decay_rows, cols, starts, inverse, transit, entry, maps, bases, ograd)


def weights_kernel(uses, *refs):
    out_ref = refs[-1]
    start = 0
    for place, use in enumerate(uses):
        still_ref = refs[max(uses) + 1 + place]
        width = still_ref.shape[1]
        out_ref[:, start : start + width] = tn(refs[use][...], still_ref[...]).astype(bf16)
        start += width


def weights_call(moving, uses, still):
    rows = moving[0].shape[0]
    total = sum(part.shape[1] for part in still)
    block = 2 * LANES
    return pl.pallas_call(
        partial(weights_kernel, uses),
        grid=(D // block,),
        in_specs=[pl.BlockSpec((rows, block), lambda i: (0, i)) for _ in moving]
        + [pl.BlockSpec((rows, part.shape[1]), lambda i: (0, 0)) for part in still],
        out_specs=pl.BlockSpec((block, total), lambda i: (i, 0)),
        out_shape=shape_of((D, total), bf16),
        compiler_params=pltpu.CompilerParams(vmem_limit_bytes=VMEM_BYTES),
        cost_estimate=pl.CostEstimate(
            flops=rows * D, bytes_accessed=rows * D, transcendentals=0
        ),
        name="weight_grads",
    )(*moving, *still)


def rms_norm(values, gain_row):
    return (
        values * lax.rsqrt(jnp.mean(values * values, axis=-1, keepdims=True) + epsilon) * gain_row
    )


def rms_back(values, gain_row, grad):
    scale = lax.rsqrt(jnp.mean(values * values, axis=-1, keepdims=True) + epsilon)
    unit = values * scale
    gain_grad = jnp.sum(grad * unit, axis=0)
    inner = grad * gain_row
    return scale * (inner - unit * jnp.mean(inner * unit, axis=-1, keepdims=True)), gain_grad


def matmul(left, right):
    return jnp.dot(left, right, preferred_element_type=f32)


def matmul_nt(left, right):
    return lax.dot_general(left, right, (((1,), (1,)), ((), ())), preferred_element_type=f32)


def matmul_tn(left, right):
    return lax.dot_general(left, right, (((0,), (0,)), ((), ())), preferred_element_type=f32)


def flat(rows):
    return rows.reshape(-1, rows.shape[-1])


def token_layout(seq_lengths, positions):
    padded = (seq_lengths + STRETCH - 1) // STRETCH * STRETCH
    seq_ends = jnp.cumsum(padded)
    starts = seq_ends - padded
    inside = (positions[:, None] >= starts[None, :]) & (positions[:, None] < seq_ends[None, :])
    start_of = jnp.sum(jnp.where(inside, starts[None, :], 0), axis=1)
    length_of = jnp.sum(jnp.where(inside, seq_lengths[None, :], 0), axis=1)
    offset = positions - start_of
    return (offset, offset < length_of)


def last_place():
    tp = lax.axis_size("tp")
    place_of = jnp.asarray([turned(offset, "tp") for offset in range(tp)], jnp.int32)
    return place_of[lax.axis_index("tp") ^ (tp - 1)]


def layer_forward(hidden_in, hidden_all, beside, w_in, gains, small, layout, layer_at, hooks):
    on_normed, on_maps, on_hidden = hooks
    conv_w, decay_rows, gain_row, widths = small
    order, valid = layout[1], layout[2]
    heads, ff = widths
    tp = lax.axis_size("tp")
    micro, rows, _ = hidden_in.shape
    hidden = flat(hidden_in)
    if hidden_all is None:
        normed_all = gather_rows(rms_norm(hidden, gains[0]).astype(bf16))
    else:
        normed_all = rms_norm(hidden_all.astype(f32), gains[0]).astype(bf16)
    w_ff, w_in, normed_all = on_normed(layer_at, normed_all)
    pre = matmul(flat(normed_all), w_in).reshape(tp, micro, rows, -1)
    tail = lax.dynamic_index_in_dim(pre, last_place(), 0, False)[:, rows - HALO :, : heads * QKV]
    halo = passed_along(tail, "ctx", 1)
    out_local, reach, starts, inverse, transit, piece_map = local_call(
        order, pre, halo, conv_w, decay_rows, layout[0], heads
    )
    maps = ring_gather(after(piece_map, w_ff))
    if beside is not None:
        maps, beside = lax.optimization_barrier((maps, beside))
    on_maps(layer_at, maps)
    gated, entry = finish_call(order, maps, out_local, reach, pre, gain_row, heads)
    gated = gated.reshape(tp, micro * rows, heads * DV)
    w_out = w_ff[:, 2 * ff : 2 * ff + heads * DV]

    def mixer_part(low, high):
        return matmul_nt(flat(gated[low:high]), w_out).reshape(high - low, micro * rows, D)

    middle = hidden + valid * scatter_rows(mixer_part, tp)
    normed_two = rms_norm(middle, gains[1]).astype(bf16)
    normed_two_all = flat(gather_rows(normed_two))
    gate_ff = matmul(normed_two_all, w_ff[:, :ff])
    up_ff = matmul(normed_two_all, w_ff[:, ff : 2 * ff])
    hidden_ff = (jax.nn.silu(gate_ff) * up_ff).astype(bf16).reshape(tp, micro * rows, ff)
    on_hidden(layer_at, hidden_ff)
    w_down = w_ff[:, 2 * ff + heads * DV : 3 * ff + heads * DV]

    def ff_part(low, high):
        return matmul_nt(flat(hidden_ff[low:high]), w_down).reshape(high - low, micro * rows, D)

    leaving = middle + valid * scatter_rows(ff_part, tp)
    saved = (
        hidden,
        normed_all,
        pre,
        halo,
        out_local,
        reach,
        starts,
        inverse,
        transit,
        maps,
        entry,
        gated,
        middle,
        normed_two_all,
        gate_ff,
        up_ff,
        hidden_ff,
    )
    return leaving.reshape(hidden_in.shape), saved, beside


def layer_backward(grad_out, saved, weights, small, layout, before, beside, ff_grad):
    (
        hidden,
        normed_all,
        pre,
        halo,
        out_local,
        reach,
        starts,
        inverse,
        transit,
        maps,
        entry,
        gated,
        middle,
        normed_two_all,
        gate_ff,
        up_ff,
        hidden_ff,
    ) = saved
    w_in, w_ff, gains = weights
    conv_w, decay_rows, gain_row, widths = small
    order, valid = layout[1], layout[2]
    heads, ff = widths
    tp = lax.axis_size("tp")
    micro, rows, _ = grad_out.shape
    grad = flat(grad_out)
    if ff_grad is None:
        ff_grad = gather_rows((valid * grad).astype(bf16))
    ff_grad = flat(ff_grad)
    w_down = w_ff[:, 2 * ff + heads * DV : 3 * ff + heads * DV]
    hidden_grad = matmul(ff_grad, w_down)
    open_at = jax.nn.sigmoid(gate_ff)
    gate_grad = (hidden_grad * up_ff * open_at * (1.0 + gate_ff * (1.0 - open_at))).astype(bf16)
    up_grad = (hidden_grad * gate_ff * open_at).astype(bf16)
    blocks_gate = gate_grad.reshape(tp, micro * rows, ff)
    blocks_up = up_grad.reshape(tp, micro * rows, ff)

    def two_part(low, high):
        part = matmul_nt(flat(blocks_gate[low:high]), w_ff[:, :ff]) + matmul_nt(
            flat(blocks_up[low:high]), w_ff[:, ff : 2 * ff]
        )
        return part.reshape(high - low, micro * rows, D)

    middle_part, gain_two = rms_back(middle, gains[1], scatter_rows(two_part, tp))
    middle_grad = grad + middle_part
    mixer_grad = flat(gather_rows((valid * middle_grad).astype(bf16)))
    w_out = w_ff[:, 2 * ff : 2 * ff + heads * DV]
    gated_grad = matmul(mixer_grad, w_out).reshape(tp, micro, rows, heads * DV)
    out_grad, gate_low, gain_grad, base = unfinish_call(
        entry, out_local, reach, pre, gain_row, gated_grad, heads
    )
    bases = ring_gather(after(base, *before))
    qkv_end, gate_end = heads * QKV, heads * (QKV + DV)
    gate_part = matmul_nt(flat(gate_low), w_in[:, qkv_end:gate_end])
    bases, beside, gate_part = lax.optimization_barrier((bases, beside, gate_part))
    gate_part = gate_part.reshape(tp, micro * rows, D)
    low_ff = weights_call(
        (normed_two_all, mixer_grad, ff_grad),
        (0, 0, 1, 2),
        (gate_grad, up_grad, flat(gated), flat(hidden_ff)),
    )
    low_ff = after(low_ff, bases)
    owned_ff = ring_scatter(low_ff)
    x_grad, halo_grad, conv_grad, rate_low, decay_grad = adjoint_call(
        order, pre, halo, conv_w, decay_rows, layout[0], starts, inverse, transit, entry, maps, bases, out_grad, heads
    )
    log_grad = jnp.sum(decay_grad[:, :, 0, 0], axis=0)
    bias_grad = jnp.stack([jnp.sum(decay_grad[:, at, 4, 2 * at]) for at in range(heads)])
    back_rows = passed_along(halo_grad, "ctx", -1)
    back_rows = jnp.transpose(back_rows, (0, 2, 1, 3)).reshape(1, micro, HALO, heads * QKV)
    at = last_place()
    zero = jnp.zeros((), jnp.int32)
    corner = (at, zero, zero + rows - HALO, zero)
    tail = lax.dynamic_slice(x_grad, corner, (1, micro, HALO, heads * QKV))
    tail = (tail.astype(f32) + back_rows).astype(bf16)
    x_grad = lax.dynamic_update_slice(x_grad, tail, corner)
    parts = [part.reshape(tp, micro * rows, -1) for part in (x_grad, gate_low, rate_low)]

    def one_part(low, high):
        part = matmul_nt(flat(parts[0][low:high]), w_in[:, :qkv_end])
        part = part + matmul_nt(flat(parts[2][low:high]), w_in[:, gate_end:])
        return part.reshape(high - low, micro * rows, D) + gate_part[low:high]

    hidden_part, gain_one = rms_back(hidden, gains[0], scatter_rows(one_part, tp))
    leaving = middle_grad + hidden_part
    low_in = weights_call((flat(normed_all),), (0, 0, 0), [flat(part) for part in parts])
    owned_in = ring_scatter(after(low_in, owned_ff))
    conv_grad = jnp.sum(conv_grad, axis=0)[:, :CONV]
    gain_grad = jnp.sum(gain_grad[:, :, 0], axis=(0, 1))
    small_grads = (conv_grad, log_grad, bias_grad, gain_grad, gain_one, gain_two)
    return leaving.reshape(grad_out.shape), owned_in, owned_ff, small_grads, beside


def body(
    inputs,
    cotangent,
    lengths,
    norm_gain,
    w_qkv,
    w_gate,
    w_rates,
    conv_weight,
    decay_log,
    decay_bias,
    out_gain,
    w_out,
    w_gu,
    w_down,
):
    tp = lax.axis_size("tp")
    ctx = lax.axis_size("ctx")
    micro, shard_rows, _ = inputs.shape
    piece_rows = shard_rows * tp
    layers = w_qkv.shape[0]
    own = w_qkv.shape[1]
    heads = w_qkv.shape[2]
    ff = w_gu.shape[3]
    ctx_at = lax.axis_index("ctx")
    tp_at = lax.axis_index("tp")
    piece_pos = ctx_at * piece_rows + jnp.arange(piece_rows, dtype=jnp.int32)
    shard_pos = (ctx_at * tp + tp_at) * shard_rows + jnp.arange(shard_rows, dtype=jnp.int32)
    offset = jnp.stack([token_layout(lengths[m], piece_pos)[0] for m in range(micro)])
    valid = jnp.stack([token_layout(lengths[m], shard_pos)[1] for m in range(micro)])
    valid = valid.astype(f32).reshape(-1, 1)
    ring, places = ring_of(ctx), ring_places()
    order = [ctx_at] + [tp_at ^ turned(place, "tp") for place in range(tp)]
    order = jnp.stack([part.astype(jnp.int32) for part in order] + [jnp.int32(p) for p in places])
    marks = [(offset >= reach).astype(f32) for reach in (1, 2, 3, 1)]
    cols = jnp.stack(marks + [jnp.zeros_like(marks[0])] * 4, axis=-1)
    layout = (cols, order, valid)

    gains = in_order(gather_blocks(norm_gain, "ctx"), "ctx")
    gains = jnp.stack([gains[device] for device in ring])
    gains = jnp.transpose(gains, (1, 2, 0, 3)).reshape(layers, 2, D).astype(f32)
    in_width = heads * (QKV + DV + 2)
    in_spare = -in_width % LANES
    shards = []
    for layer_at in range(layers):
        shard_in = jnp.concatenate(
            [
                w_qkv[layer_at].reshape(own, -1),
                w_gate[layer_at].reshape(own, -1),
                w_rates[layer_at].reshape(own, -1),
                jnp.zeros((own, in_spare), bf16),
            ],
            axis=1,
        )
        shard_ff = jnp.concatenate(
            [
                w_gu[layer_at, 0],
                w_gu[layer_at, 1],
                w_out[layer_at].reshape(-1, own).T,
                w_down[layer_at].T,
            ],
            axis=1,
        )
        shards.append((shard_in, shard_ff))

    def gathered(shard, *before):
        return ring_gather(after(shard, *before), axis=0, tiled=True)

    weights_in = [gathered(shards[0][0])] + [None] * (layers - 1)
    weights_ff = [None] * layers

    def on_normed(layer_at, token):
        if layer_at == 0:
            shard, weights_in[0], token = lax.optimization_barrier(
                (shards[0][1], weights_in[0], token)
            )
            weights_ff[0] = gathered(shard)
        return weights_ff[layer_at], weights_in[layer_at], token

    def on_maps(layer_at, token):
        if layer_at + 1 < layers:
            weights_in[layer_at + 1] = gathered(shards[layer_at + 1][0], token)

    def on_hidden(layer_at, token):
        if layer_at + 1 < layers:
            following = layer_at + 1
            weights_ff[following] = gathered(shards[following][1], weights_in[following], token)

    hooks = (on_normed, on_maps, on_hidden)
    smalls = []
    for layer_at in range(layers):
        conv_w = jnp.transpose(conv_weight[layer_at], (1, 0, 2))
        conv_w = jnp.concatenate([conv_w, jnp.zeros((heads, 8 - CONV, QKV), f32)], axis=1)
        gain_row = jnp.broadcast_to(out_gain[layer_at][None], (8, DV))
        scale, bias = -jnp.exp(decay_log[layer_at]), decay_bias[layer_at]
        pair = jnp.stack([jnp.stack([part, jnp.zeros_like(part)], axis=1) for part in (scale, bias)])
        decay_rows = jnp.pad(pair.reshape(2, -1), ((0, 6), (0, LANES - 2 * heads)))
        smalls.append(
            (conv_w, decay_rows, gain_row, (heads, ff))
        )

    moved = blocks_moved(inputs, ring)
    hidden_all = gather_rows(flat(moved))
    hidden_now = moved.astype(f32)
    grad_now = blocks_moved(cotangent, ring)
    ff_grad = gather_rows((valid * flat(grad_now)).astype(bf16))
    saved_all = []
    for layer_at in range(layers):
        hidden_now, saved, kept = layer_forward(
            hidden_now, hidden_all, ff_grad if layer_at == 0 else None, weights_in[layer_at], gains[layer_at], smalls[layer_at], layout, layer_at, hooks
        )
        hidden_all = None
        ff_grad = ff_grad if kept is None else kept
        saved_all.append(saved)
    weights = list(zip(weights_in, weights_ff, gains))
    before = ()
    beside = hidden_now
    big = [None] * layers
    small = [None] * layers
    for layer_at in reversed(range(layers)):
        grad_now, owned_in, owned_ff, small_grads, beside = layer_backward(
            grad_now, saved_all[layer_at], weights[layer_at], smalls[layer_at], layout, before, beside, ff_grad
        )
        ff_grad = None
        if layer_at == layers - 1:
            hidden_now = beside
        else:
            big[layer_at + 1], small[layer_at + 1] = beside
        before = (owned_in,)
        beside = ((owned_in.astype(f32), owned_ff.astype(f32)), small_grads)
    big[0], small[0] = beside

    head_parts = [jnp.stack([small[at][member] for at in range(layers)]) for member in range(3)]
    wide_parts = [jnp.stack([small[at][member] for at in range(layers)]) for member in range(3, 6)]
    sizes = [part.size for part in head_parts + wide_parts]
    head_size = sum(sizes[:3])
    packed = jnp.concatenate([part.reshape(-1) for part in head_parts + wide_parts])
    spare = -packed.size % (8 * LANES)
    packed = jnp.concatenate([packed, jnp.zeros((spare,), f32)]).reshape(-1, LANES)
    packed = sum_over(packed, "ctx").reshape(-1)
    wide = packed[head_size : sum(sizes)]
    wide_size = wide.size
    spare = -wide_size % (8 * LANES)
    wide = jnp.concatenate([wide, jnp.zeros((spare,), f32)]).reshape(-1, LANES)
    wide = sum_over(wide, "tp").reshape(-1)
    parts = []
    start = 0
    for part, size in zip(head_parts, sizes[:3]):
        parts.append(packed[start : start + size].reshape(part.shape))
        start += size
    start = 0
    for part, size in zip(wide_parts, sizes[3:]):
        parts.append(wide[start : start + size].reshape(part.shape))
        start += size
    conv_grad, log_grad, bias_grad, ogain_grad, gain_one, gain_two = parts
    conv_grad = jnp.transpose(conv_grad, (0, 2, 1, 3))
    norm_grad = jnp.stack([gain_one, gain_two], axis=1)
    own_place = jnp.asarray(places, jnp.int32)[ctx_at]
    norm_grad = lax.dynamic_slice_in_dim(norm_grad, own_place * own, own, 2)

    in_all = jnp.stack([big[at][0] for at in range(layers)])
    ff_all = jnp.stack([big[at][1] for at in range(layers)])
    qkv_end, gate_end = heads * QKV, heads * (QKV + DV)
    grad_qkv = in_all[..., :qkv_end].reshape(w_qkv.shape)
    grad_gate_w = in_all[..., qkv_end:gate_end].reshape(w_gate.shape)
    grad_rates = in_all[..., gate_end:in_width].reshape(w_rates.shape)
    grad_gu = jnp.stack([ff_all[..., :ff], ff_all[..., ff : 2 * ff]], axis=1)
    out_end = 2 * ff + heads * DV
    grad_out_w = jnp.swapaxes(ff_all[..., 2 * ff : out_end], 1, 2).reshape(w_out.shape)
    grad_down = jnp.swapaxes(ff_all[..., out_end:], 1, 2)
    return (
        blocks_moved(hidden_now, places),
        blocks_moved(grad_now, places),
        norm_grad,
        grad_qkv,
        grad_gate_w,
        grad_rates,
        conv_grad,
        log_grad,
        bias_grad,
        ogain_grad,
        grad_out_w,
        grad_gu,
        grad_down,
    )


def solution(mesh):
    placed = (
        P(None, ("ctx", "tp"), None),
        P(None, ("ctx", "tp"), None),
        P(),
        P(None, None, "ctx"),
        P(None, "ctx", "tp", None),
        P(None, "ctx", "tp", None),
        P(None, "ctx", "tp", None),
        P(None, None, "tp", None),
        P(None, "tp"),
        P(None, "tp"),
        P(),
        P(None, "tp", None, "ctx"),
        P(None, None, "ctx", "tp"),
        P(None, "tp", "ctx"),
    )
    return jax.shard_map(
        body,
        mesh=mesh,
        in_specs=placed,
        out_specs=(
            P(None, ("ctx", "tp"), None),
            P(None, ("ctx", "tp"), None),
            P(None, None, "ctx"),
            P(None, "ctx", "tp", None),
            P(None, "ctx", "tp", None),
            P(None, "ctx", "tp", None),
            P(None, None, "tp", None),
            P(None, "tp"),
            P(None, "tp"),
            P(),
            P(None, "tp", None, "ctx"),
            P(None, None, "ctx", "tp"),
            P(None, "tp", "ctx"),
        ),
        check_vma=False,
    )
```
